256 devices in a mesh: row: 16 (over x, y_hi, core), col: 16 (over z, y_lo).
Axes of the slice: x: 4, y: 4 (y_hi: 2, y_lo: 2; y = y_hi * 2 + y_lo), z: 8, core: 2. Of those that a mesh axis runs over, the one named last changes fastest.
Arguments:
- sequence: bfloat16 [128, 256, 768], P('row', 'col'), may hold values from -6 to 6
- conv_weights: float32 [3, 2304], replicated, may hold values from -3.5 to 3.5
- cotangent: bfloat16 [128, 256, 768], P('row', 'col'), may hold values from -6 to 6
- filter_re: bfloat16 [128, 768, 256], P('col', 'row'), may hold values from -6 to 6
- filter_im: bfloat16 [128, 768, 256], P('col', 'row'), may hold values from -6 to 6
Outputs:
- mixed: bfloat16 [128, 256, 768], P('row', 'col')
- input_grad: bfloat16 [128, 256, 768], P('row', 'col')
- filter_grad_re: float32 [128, 768, 256], P('col', 'row')
- filter_grad_im: float32 [128, 768, 256], P('col', 'row')
- conv_weight_grad: float32 [3, 2304], replicated
The draws below stay inside these ranges and needn't reach their ends.
All inputs are finite; a program needn't handle non-finite values.
Results may differ from the reference program's by a relative error of at most 0.0091.
Values may be sent and summed in bfloat16 or wider, within the bound.
A program may use at most 64 MiB of HBM per device.

```python
import math
import jax
import jax.numpy as jnp
from jax import lax

D = 768
N1 = 128
N2 = 256
SEQ = 32768


def block_scale(key, dims, pieces, low, largest):
    def one(position, shards_of):
        heights = jax.random.uniform(jax.random.fold_in(jax.random.fold_in(key, 6), position), (shards_of,), jnp.float32, low / len(pieces), largest / len(pieces))
        return jnp.repeat(jnp.exp(heights), dims[position] // shards_of).reshape((-1,) + (1,) * (len(dims) - position - 1))

    level = one(*pieces[0])
    for cut in pieces[1:]:
        level = level * one(*cut)
    return level


def scatter_about(key, dims, spread, limit, split=(), kind=jnp.bfloat16):
    array = jax.random.normal(key, dims, jnp.float32) * spread
    if len(split) > 0:
        array = block_scale(key, dims, split, -0.22, 0.18) * array
    return jnp.clip(array, min=-limit, max=limit).astype(kind)


def setup_inputs(seed: int = 0) -> dict:
    key_of = jax.random.split(jax.random.key(seed), 6)
    return {
        "sequence": scatter_about(key_of[0], (N1, N2, D), 1.0, 6.0, ((0, 16), (1, 16))),
        "conv_weights": scatter_about(key_of[1], (3, 3 * D), 3 ** -0.5, 3.5, (), jnp.float32),
        "cotangent": scatter_about(key_of[2], (N1, N2, D), 1.0, 6.0, ((0, 16), (1, 16))),
        "filter_re": scatter_about(key_of[3], (N1, D, N2), 1.0, 6.0, ((0, 16), (1, 16))),
        "filter_im": scatter_about(key_of[4], (N1, D, N2), 1.0, 6.0, ((0, 16), (1, 16))),
    }


def dft_tables(length):
    index_row = jnp.arange(length, dtype=jnp.int32)
    product = index_row[:, None] * index_row[None, :] % length
    angles = product.astype(jnp.float32) * (2.0 * math.pi / length)
    return (jnp.cos(angles).astype(jnp.bfloat16), jnp.sin(angles).astype(jnp.bfloat16))

def rounded(values):
    return lax.optimization_barrier(values.astype(jnp.bfloat16)).astype(jnp.float32)

def as_float(values):
    return values.astype(jnp.float32)

def forward_transform(field, tables):
    cos_first, sin_first, cos_second, sin_second, tw_cos, tw_sin = tables
    field_f = as_float(field)
    first_re = jnp.einsum('nmd,nk->kmd', field_f, cos_first)
    first_im = -jnp.einsum('nmd,nk->kmd', field_f, sin_first)
    cos_b = tw_cos[:, :, None]
    sin_b = tw_sin[:, :, None]
    part_re = rounded(first_re * cos_b + first_im * sin_b)
    part_im = rounded(first_im * cos_b - first_re * sin_b)
    out_re = jnp.einsum('kmd,mj->kdj', part_re, cos_second) + jnp.einsum('kmd,mj->kdj', part_im, sin_second)
    out_im = jnp.einsum('kmd,mj->kdj', part_im, cos_second) - jnp.einsum('kmd,mj->kdj', part_re, sin_second)
    return (out_re, out_im)

def inverse_transform(spec_re, spec_im, tables):
    cos_first, sin_first, cos_second, sin_second, tw_cos, tw_sin = tables
    spec_re = as_float(spec_re)
    spec_im = as_float(spec_im)
    inner_re = jnp.einsum('kdj,jn->kdn', spec_re, cos_second) - jnp.einsum('kdj,jn->kdn', spec_im, sin_second)
    inner_im = jnp.einsum('kdj,jn->kdn', spec_im, cos_second) + jnp.einsum('kdj,jn->kdn', spec_re, sin_second)
    cos_b = tw_cos[:, None, :]
    sin_b = tw_sin[:, None, :]
    turned_re = rounded(inner_re * cos_b - inner_im * sin_b)
    turned_im = rounded(inner_im * cos_b + inner_re * sin_b)
    summed = jnp.einsum('kdn,kj->jnd', turned_re, cos_first) - jnp.einsum('kdn,kj->jnd', turned_im, sin_first)
    return (summed / SEQ).astype(jnp.bfloat16)

def delayed_by(values, offset):
    if offset == 0:
        return values
    pad_rows = jnp.zeros((offset, values.shape[1]), values.dtype)
    return jnp.concatenate([pad_rows, values[:SEQ - offset]], 0)

def advanced_by(values, offset):
    if offset == 0:
        return values
    pad_rows = jnp.zeros((offset, values.shape[1]), values.dtype)
    return jnp.concatenate([values[offset:], pad_rows], 0)

def block_pass(inputs, tables):
    seq_block, weight_block, grad_block, filt_re, filt_im = inputs
    chan_count = seq_block.shape[2]
    flat_input = seq_block.reshape(SEQ, chan_count).astype(jnp.float32)
    previous = [delayed_by(flat_input, offset) for offset in range(3)]
    streams = []
    for stream in range(3):
        total_sum = weight_block[0, stream] * previous[0]
        total_sum = total_sum + weight_block[1, stream] * previous[1]
        total_sum = total_sum + weight_block[2, stream] * previous[2]
        streams.append(total_sum)
    stream_a, stream_b, stream_c = streams
    gated = (stream_a * stream_b).astype(jnp.bfloat16).reshape(N1, N2, chan_count)
    spec_re, spec_im = forward_transform(gated, tables)
    filt_re = as_float(filt_re)
    filt_im = as_float(filt_im)
    prod_re = (spec_re * filt_re - spec_im * filt_im).astype(jnp.bfloat16)
    prod_im = (spec_re * filt_im + spec_im * filt_re).astype(jnp.bfloat16)
    filtered = inverse_transform(prod_re, prod_im, tables).reshape(SEQ, chan_count)
    filtered_f = filtered.astype(jnp.float32)
    mixed = (stream_c * filtered_f).astype(jnp.bfloat16)
    grad_f = grad_block.reshape(SEQ, chan_count).astype(jnp.float32)
    grad_gate = (grad_f * stream_c).astype(jnp.bfloat16).reshape(N1, N2, chan_count)
    gspec_re, gspec_im = forward_transform(grad_gate, tables)
    fgrad_re = (spec_re * gspec_re + spec_im * gspec_im) / SEQ
    fgrad_im = (spec_re * gspec_im - spec_im * gspec_re) / SEQ
    back_re = (gspec_re * filt_re + gspec_im * filt_im).astype(jnp.bfloat16)
    back_im = (gspec_im * filt_re - gspec_re * filt_im).astype(jnp.bfloat16)
    grad_filtered = inverse_transform(back_re, back_im, tables).reshape(SEQ, chan_count).astype(jnp.float32)
    stream_grads = [rounded(grad_filtered * stream_b), rounded(grad_filtered * stream_a), rounded(grad_f * filtered_f)]
    input_acc = jnp.zeros((SEQ, chan_count), jnp.float32)
    for offset in range(3):
        for stream in range(3):
            input_acc = input_acc + weight_block[offset, stream] * advanced_by(stream_grads[stream], offset)
    input_grad = input_acc.astype(jnp.bfloat16).reshape(N1, N2, chan_count)
    weight_rows = []
    for offset in range(3):
        weight_rows.append(jnp.stack([lax.optimization_barrier(jnp.sum(previous[offset] * stream_grads[stream], 0)) for stream in range(3)]))
    weight_grad = jnp.stack(weight_rows) / math.sqrt(SEQ)
    return (mixed.reshape(N1, N2, chan_count), input_grad, fgrad_re, fgrad_im, weight_grad)

def reference(sequence, conv_weights, cotangent, filter_re, filter_im):
    block_width = math.gcd(D, 128)
    block_count = D // block_width
    cos_first, sin_first = dft_tables(N1)
    cos_second, sin_second = dft_tables(N2)
    first_index = jnp.arange(N1, dtype=jnp.int32)
    second_index = jnp.arange(N2, dtype=jnp.int32)
    product = first_index[:, None] * second_index[None, :] % SEQ
    angles = product.astype(jnp.float32) * (2.0 * math.pi / SEQ)
    tables = (as_float(cos_first), as_float(sin_first), as_float(cos_second), as_float(sin_second), jnp.cos(angles), jnp.sin(angles))
    seq_blocks = sequence.reshape(N1, N2, block_count, block_width).transpose(2, 0, 1, 3)
    grad_blocks = cotangent.reshape(N1, N2, block_count, block_width).transpose(2, 0, 1, 3)
    weight_blocks = conv_weights.reshape(3, 3, block_count, block_width).transpose(2, 0, 1, 3)
    fre_blocks = filter_re.reshape(N1, block_count, block_width, N2).transpose(1, 0, 2, 3)
    fim_blocks = filter_im.reshape(N1, block_count, block_width, N2).transpose(1, 0, 2, 3)

    def one_block(inputs):
        return block_pass(inputs, tables)
    mixed, input_grad, fgrad_re, fgrad_im, weight_grad = lax.map(one_block, (seq_blocks, weight_blocks, grad_blocks, fre_blocks, fim_blocks))
    mixed = mixed.transpose(1, 2, 0, 3).reshape(N1, N2, D)
    input_grad = input_grad.transpose(1, 2, 0, 3).reshape(N1, N2, D)
    fgrad_re = fgrad_re.transpose(1, 0, 2, 3).reshape(N1, D, N2)
    fgrad_im = fgrad_im.transpose(1, 0, 2, 3).reshape(N1, D, N2)
    weight_grad = weight_grad.transpose(1, 2, 0, 3).reshape(3, 3 * D)
    return (mixed, input_grad, fgrad_re, fgrad_im, weight_grad)
```

```python
import functools
import math

import jax
import jax.numpy as jnp
import ml_dtypes
import numpy as np
from jax import lax
from jax.experimental import pallas as pl
from jax.experimental.pallas import tpu as pltpu
from jax.sharding import PartitionSpec as P

MESH = pl.DeviceIdType.MESH
F32 = jnp.float32
BF16 = jnp.bfloat16

NP = 16
DL = 48
GR = 16
N1 = 128
N2 = 256
SEQ = N1 * N2

XR, CR, FM, HX, SS, GG, YY, ZZ, GM, HG, D1, MR, IR, D2 = range(14)


def slot_freq(col, slot):
    return 8 * col + slot + (1 if col >= 8 else 0)


def tables():
    lane_n1 = np.array([8 * (l % 16) + l // 16 for l in range(128)])
    first = np.zeros((128, 128))
    last = np.zeros((128, 128))
    for col in range(16):
        for slot in range(4):
            k1 = slot_freq(col, slot)
            turn = 2 * np.pi * (lane_n1 * k1 % 128) / 128
            re_row, im_row = slot * 16 + col, (slot + 4) * 16 + col
            if k1 == 0:
                first[:, re_row] = 1.0
                first[:, im_row] = np.cos(np.pi * lane_n1)
                last[re_row] = 1.0
                last[im_row] = np.cos(np.pi * lane_n1)
            else:
                first[:, re_row] = np.cos(turn)
                first[:, im_row] = -np.sin(turn)
                last[re_row] = np.cos(turn)
                last[im_row] = -np.sin(turn)
    last = last / SEQ
    idx = np.arange(N2)
    angle = 2 * np.pi * (idx[:, None] * idx[None, :] % N2) / N2
    second = np.concatenate([np.cos(angle), np.sin(angle)], 1)
    fwd = np.zeros((16, 2, 16, 128), np.float32)
    inv = np.zeros((16, 2, 8, N2), np.float32)
    low = np.arange(16)
    for col in range(16):
        for target in range(16):
            for slot in range(4):
                k1 = slot_freq(target, slot)
                turn = 2 * np.pi * (k1 * (16 * col + low) % SEQ) / SEQ
                re_l, im_l = slot * 16 + low, (slot + 4) * 16 + low
                fwd[col, 0, target, re_l] = np.cos(turn)
                fwd[col, 0, target, im_l] = np.cos(turn)
                fwd[col, 1, target, re_l] = np.sin(turn)
                fwd[col, 1, target, im_l] = -np.sin(turn)
        for slot in range(5):
            k1 = slot_freq(col, slot) if slot < 4 else 64
            turn = 2 * np.pi * (k1 * idx % SEQ) / SEQ
            inv[col, 0, slot] = np.cos(turn)
            inv[col, 1, slot] = np.sin(turn)
    return (
        first.astype(ml_dtypes.bfloat16),
        last.astype(ml_dtypes.bfloat16),
        second.astype(ml_dtypes.bfloat16),
        fwd,
        inv,
    )


def swap_bits(planes, pairs):
    lane = lax.broadcasted_iota(jnp.int32, planes[0].shape, 1)
    planes = list(planes)
    for plane_bit, lane_bit in pairs:
        shift = 1 << lane_bit
        upper = (lane & shift) != 0
        for i in range(len(planes)):
            if i & (1 << plane_bit):
                continue
            j = i | (1 << plane_bit)
            low, high = planes[i], planes[j]
            planes[i] = jnp.where(upper, pltpu.roll(high, shift, 1), low)
            planes[j] = jnp.where(upper, high, pltpu.roll(low, 128 - shift, 1))
    return planes


LOW4 = ((0, 0), (1, 1), (2, 2), (3, 3))
HIGH3 = ((0, 4), (1, 5), (2, 6))


def kernel(
    x_ref, w_ref, cot_ref, fr_ref, fi_ref, first_ref, last_ref, second_ref, fwd_ref, inv_ref,
    mixed_ref, ig_ref, fgr_ref, fgi_ref, dw_ref,
    xt, xrecv, ct, crecv, w9, wt, wb, fo, fm, rev, fh, tf, ti,
    xp, hx_send, hx_recv, cp, ap, bp, sp, yp, fld,
    s_send, s_recv, g_send, g_recv, y_send, y_recv, z_send, z_recv,
    pp, uu, sr, si, qq, gs_send, gm_recv, gp, hg_send, hg_recv,
    d1_send, d1_recv, d2_send, d2_recv, m_send, m_recv, i_send, i_recv,
    send_sem, recv_sem, local_sem,
):
    row = lax.axis_index("row")
    col = lax.axis_index("col")
    low_half = col < 8

    def remote(src, dst, which, target):
        return pltpu.make_async_remote_copy(
            src_ref=src,
            dst_ref=dst,
            send_sem=send_sem.at[which],
            recv_sem=recv_sem.at[which],
            device_id=target,
            device_id_type=MESH,
        )

    def exchange(axis, me, which, src_at, dst):
        def body(step, carry):
            peer = lax.rem(me + step, NP)
            remote(src_at(peer), dst, which, {axis: peer}).start()
            return carry

        lax.fori_loop(1, NP, body, 0)

    def wait_bytes(ref, sem):
        pltpu.make_async_copy(ref, ref, sem).wait()

    def tile_of(ref, peer):
        return ref.at[pl.ds(pl.multiple_of(peer * DL, DL), DL)]

    def over_groups(body):
        def step(g, carry):
            body(pl.ds(pl.multiple_of(g * GR, GR), GR))
            return carry

        lax.fori_loop(0, DL // GR, step, 0)

    loads = [
        pltpu.make_async_copy(fr_ref, fo.at[0], local_sem.at[0]),
        pltpu.make_async_copy(fi_ref, fo.at[1], local_sem.at[1]),
        pltpu.make_async_copy(fwd_ref.at[col], tf, local_sem.at[2]),
        pltpu.make_async_copy(inv_ref.at[col], ti, local_sem.at[3]),
    ]
    for load in loads:
        load.start()

    barrier = pltpu.get_barrier_semaphore()

    def greet(step, carry):
        pl.semaphore_signal(
            barrier, inc=1, device_id={"row": lax.rem(row + step, NP)}, device_id_type=MESH
        )
        pl.semaphore_signal(
            barrier, inc=1, device_id={"col": lax.rem(col + step, NP)}, device_id_type=MESH
        )
        return carry

    lax.fori_loop(1, NP, greet, 0)

    def turn_home(src_ref, dst):
        for i in range(6):
            block = src_ref[:, :, 128 * i : 128 * (i + 1)].reshape(128, 128).astype(F32)
            dst[128 * i : 128 * (i + 1), :] = block.T.astype(BF16)

    turn_home(x_ref, xt)
    pl.semaphore_wait(barrier, 2 * (NP - 1))

    exchange("row", row, XR, lambda p: tile_of(xt, p), tile_of(xrecv, row))
    own_rows = pl.ds(pl.multiple_of(row * DL, DL), DL)
    xrecv[own_rows, :] = xt[own_rows, :]
    turn_home(cot_ref, ct)
    exchange("row", row, CR, lambda p: tile_of(ct, p), tile_of(crecv, row))
    crecv[own_rows, :] = ct[own_rows, :]

    partner = 15 - col
    extra_row = jnp.where(low_half, 4, 0)
    extra_to = jnp.where(low_half, partner, lax.rem(16 - col, 8))
    for part, ref in enumerate((fr_ref, fi_ref)):
        remote(ref.at[pl.ds(5, 3)], fm.at[part, pl.ds(1, 3)], FM, {"col": partner}).start()
        remote(ref.at[extra_row], fm.at[part, 0], FM, {"col": extra_to}).start()

    w9[...] = jnp.zeros_like(w9)
    for tap in range(3):
        for stream in range(3):
            q = 3 * tap + stream
            w9[q : q + 1, :] = w_ref[tap : tap + 1, 768 * stream : 768 * (stream + 1)]
    for i in range(6):
        wt[128 * i : 128 * (i + 1), :] = w9[:, 128 * i : 128 * (i + 1)].T
    columns = wt[own_rows, :]
    for q in range(9):
        wb[q] = jnp.broadcast_to(columns[:, q : q + 1], (DL, 128))
    for load in loads:
        load.wait()

    lane = lax.broadcasted_iota(jnp.int32, (DL, 128), 1)

    def planes_in(recv, dst, base):
        def body(rows):
            planes = [recv[i, rows, :].astype(F32) for i in range(NP)]
            planes = swap_bits(planes, LOW4)
            for i in range(NP):
                dst[base + i, rows, :] = planes[i]

        over_groups(body)

    def tiles_out(src, dst, table):
        def body(rows):
            flat = src[:, rows, :].reshape(NP * GR, 128)
            out = jnp.dot(flat, first_ref[...], preferred_element_type=F32).reshape(NP, GR, 128)
            tiles = swap_bits([out[i] for i in range(NP)], LOW4)
            for i in range(NP):
                turned = tiles[i] * tf[0, i : i + 1, :] + pltpu.roll(tiles[i], 64, 1) * tf[1, i : i + 1, :]
                dst[i, rows, :] = turned.astype(BF16)

        over_groups(body)

    wait_bytes(xrecv.at[pl.ds(0, 15 * DL)], recv_sem.at[XR])
    x3 = xrecv.reshape(NP, DL, 128)
    planes_in(x3, xp, 2)
    hx_send[0] = xp[16].astype(BF16)
    hx_send[1] = xp[17].astype(BF16)
    remote(hx_send, hx_recv, HX, {"col": lax.rem(col + 1, NP)}).start()

    wait_bytes(hx_recv, recv_sem.at[HX])
    for i in range(2):
        halo = hx_recv[i].astype(F32)
        back = jnp.where(lane >= 16, pltpu.roll(halo, 16, 1), pltpu.roll(halo, 17, 1))
        back = jnp.where(lane == 0, 0.0, back)
        xp[i] = jnp.where(col == 0, back, halo)

    def streams(rows):
        taps = [wb[q, rows, :] for q in range(9)]
        behind2, behind1 = xp[0, rows, :], xp[1, rows, :]
        for i in range(NP):
            now = xp[i + 2, rows, :]
            z = [taps[j] * now + taps[3 + j] * behind1 + taps[6 + j] * behind2 for j in range(3)]
            ap[i, rows, :] = z[0]
            bp[i, rows, :] = z[1]
            sp[i, rows, :] = z[2]
            fld[i, rows, :] = (z[0] * z[1]).astype(BF16)
            behind2, behind1 = behind1, now

    over_groups(streams)
    tiles_out(fld, s_send, tf)
    exchange("col", col, SS, lambda p: s_send.at[p], s_recv.at[col])
    s_recv[col] = s_send[col]

    wait_bytes(crecv.at[pl.ds(0, 15 * DL)], recv_sem.at[CR])
    planes_in(crecv.reshape(NP, DL, 128), cp, 0)

    def gate_grad(rows):
        for i in range(NP):
            fld[i, rows, :] = (cp[i, rows, :] * sp[i, rows, :]).astype(BF16)

    over_groups(gate_grad)
    tiles_out(fld, g_send, tf)
    exchange("col", col, GG, lambda p: g_send.at[p], g_recv.at[col])
    g_recv[col] = g_send[col]

    wait_bytes(fm, recv_sem.at[FM])
    at_row = lax.broadcasted_iota(jnp.int32, (N2, N2), 0)
    at_col = lax.broadcasted_iota(jnp.int32, (N2, N2), 1)
    reverse = jnp.where(at_row + at_col == N2 - 1, 1.0, 0.0).astype(BF16)
    rev[...] = jnp.dot(
        fm[...].reshape(8 * DL, N2), reverse, preferred_element_type=F32
    ).reshape(2, 4, DL, N2)

    def mirror_at(slot):
        return jnp.where(low_half, (4 - slot) % 4, 3 - slot)

    own_at = jnp.where(low_half, 0, 1)
    for slot in range(4):
        rev_re = rev[0, mirror_at(slot)]
        rev_im = -rev[1, mirror_at(slot)]
        if slot == 0:
            fh[0, 4] = rev_re
            fh[1, 4] = rev_im
            rev_re = jnp.where(col == 0, 0.0, rev_re)
            rev_im = jnp.where(col == 0, 0.0, rev_im)
        fh[0, slot] = fo[0, own_at + slot].astype(F32) + rev_re
        fh[1, slot] = fo[1, own_at + slot].astype(F32) + rev_im

    parts = [(0, 4), (1, 5), (2, 6), (3, 7), (8, 9)]

    def spectrum(recv):
        def body(rows):
            planes = swap_bits([recv[i, rows, :].astype(F32) for i in range(NP)], HIGH3)
            for i in range(NP):
                half = i // 8
                pp[i % 8, rows, 128 * half : 128 * (half + 1)] = planes[i].astype(BF16)

        over_groups(body)
        middle = pp[4].astype(F32)
        pp[8] = (middle * ti[0, 4:5, :]).astype(BF16)
        pp[9] = (-middle * ti[1, 4:5, :]).astype(BF16)
        pp[4] = jnp.where(col == 0, 0.0, middle).astype(BF16)
        uu[...] = jnp.dot(
            pp[...].reshape(10 * DL, N2), second_ref[...], preferred_element_type=F32
        ).reshape(10, DL, 2 * N2)

    def value(slot):
        re, im = parts[slot]
        return (
            uu[re, :, :N2] + uu[im, :, N2:],
            uu[im, :, :N2] - uu[re, :, N2:],
        )

    def restore(dst):
        uu[...] = jnp.dot(
            pp[...].reshape(10 * DL, N2), second_ref[...], preferred_element_type=F32
        ).reshape(10, DL, 2 * N2)
        for slot in range(4):
            re, im = parts[slot]
            z_re = uu[re, :, :N2] - uu[im, :, N2:]
            z_im = uu[im, :, :N2] + uu[re, :, N2:]
            cos, sin = ti[0, slot : slot + 1, :], ti[1, slot : slot + 1, :]
            qq[slot] = z_re * cos - z_im * sin
            q_im = z_im * cos + z_re * sin
            if slot == 0:
                re4, im4 = parts[4]
                z_re4 = uu[re4, :, :N2] - uu[im4, :, N2:]
                z_im4 = uu[im4, :, :N2] + uu[re4, :, N2:]
                q_im = jnp.where(col == 0, z_re4 * ti[0, 4:5, :] - z_im4 * ti[1, 4:5, :], q_im)
            qq[4 + slot] = q_im

        def body(rows):
            planes = [
                qq[i % 8, rows, 128 * (i // 8) : 128 * (i // 8 + 1)] for i in range(NP)
            ]
            planes = swap_bits(planes, HIGH3)
            for i in range(NP):
                dst[i, rows, :] = planes[i].astype(BF16)

        over_groups(body)

    wait_bytes(s_recv.at[pl.ds(0, 15)], recv_sem.at[SS])
    spectrum(s_recv)
    for slot in range(5):
        re, im = parts[slot]
        s_re, s_im = value(slot)
        sr[slot] = s_re
        si[slot] = s_im
        f_re, f_im = fh[0, slot], fh[1, slot]
        pp[re] = (s_re * f_re - s_im * f_im).astype(BF16)
        pp[im] = (s_re * f_im + s_im * f_re).astype(BF16)
    restore(y_send)
    exchange("col", col, YY, lambda p: y_send.at[p], y_recv.at[col])
    y_recv[col] = y_send[col]

    wait_bytes(g_recv.at[pl.ds(0, 15)], recv_sem.at[GG])
    spectrum(g_recv)
    for slot in range(5):
        re, im = parts[slot]
        g_re, g_im = value(slot)
        f_re, f_im = fh[0, slot], fh[1, slot]
        pp[re] = (g_re * f_re + g_im * f_im).astype(BF16)
        pp[im] = (g_im * f_re - g_re * f_im).astype(BF16)
        s_re, s_im = sr[slot], si[slot]
        grad_re = (s_re * g_re + s_im * g_im) * (1.0 / SEQ)
        grad_im = (s_re * g_im - s_im * g_re) * (1.0 / SEQ)
        if slot < 4:
            fgr_ref[own_at + slot] = grad_re
            fgi_ref[own_at + slot] = grad_im
            gs_send[0, mirror_at(slot)] = grad_re.astype(BF16)
            gs_send[1, mirror_at(slot)] = grad_im.astype(BF16)
        else:
            gs_send[0, 0] = jnp.where(col == 0, grad_re, gs_send[0, 0].astype(F32)).astype(BF16)
            gs_send[1, 0] = jnp.where(col == 0, grad_im, gs_send[1, 0].astype(F32)).astype(BF16)
    restore(z_send)
    exchange("col", col, ZZ, lambda p: z_send.at[p], z_recv.at[col])
    z_recv[col] = z_send[col]
    back_to = jnp.where(low_half, jnp.where(col == 0, 8, 16 - col), partner)
    back_to = lax.rem(back_to, NP)
    for part in range(2):
        remote(gs_send.at[part, pl.ds(1, 3)], gm_recv.at[part, pl.ds(1, 3)], GM, {"col": partner}).start()
        remote(gs_send.at[part, 0], gm_recv.at[part, 0], GM, {"col": back_to}).start()

    def field_back(recv, dst):
        def body(rows):
            planes = swap_bits([recv[i, rows, :].astype(F32) for i in range(NP)], LOW4)
            flat = jnp.stack([p.astype(BF16) for p in planes]).reshape(NP * GR, 128)
            out = jnp.dot(flat, last_ref[...], preferred_element_type=F32)
            dst[:, rows, :] = out.astype(BF16).astype(F32).reshape(NP, GR, 128)

        over_groups(body)

    def send_home(make, dst):
        def body(rows):
            tiles = swap_bits([make(i, rows) for i in range(NP)], LOW4)
            for i in range(NP):
                dst[i, rows, :] = tiles[i].astype(BF16)

        over_groups(body)

    wait_bytes(y_recv.at[pl.ds(0, 15)], recv_sem.at[YY])
    field_back(y_recv, yp)
    send_home(lambda i, rows: sp[i, rows, :] * yp[i, rows, :], m_send)
    exchange("row", row, MR, lambda p: m_send.at[p], tile_of(m_recv, row))
    m_recv[own_rows, :] = m_send[row]

    wait_bytes(z_recv.at[pl.ds(0, 15)], recv_sem.at[ZZ])
    field_back(z_recv, gp)

    def rounded(value):
        return value.astype(BF16).astype(F32)

    def stream_grads(rows):
        taps = [wb[q, rows, :] for q in range(9)]
        sums = [jnp.zeros((GR, 128), F32)] * 9
        before1 = before2 = None
        for i in range(NP):
            gs = gp[i, rows, :]
            grads = (
                rounded(gs * bp[i, rows, :]),
                rounded(gs * ap[i, rows, :]),
                rounded(cp[i, rows, :] * yp[i, rows, :]),
            )
            at_tap = [
                taps[3 * t] * grads[0] + taps[3 * t + 1] * grads[1] + taps[3 * t + 2] * grads[2]
                for t in range(3)
            ]
            past = [xp[i + 2 - t, rows, :] for t in range(3)]
            sums = [sums[q] + past[q // 3] * grads[q % 3] for q in range(9)]
            if i == 0:
                hg_send[0, rows, :] = at_tap[2].astype(BF16)
                first_one = at_tap[1]
            if i == 1:
                hg_send[1, rows, :] = (first_one + at_tap[2]).astype(BF16)
            if before2 is not None:
                gp[i - 2, rows, :] = before2 + at_tap[2]
            before2 = None if before1 is None else before1 + at_tap[1]
            before1 = at_tap[0]
        gp[14, rows, :] = before2
        gp[15, rows, :] = before1
        at = lax.broadcasted_iota(jnp.int32, (GR, 128), 1)
        total = jnp.zeros((GR, 128), F32)
        for q in range(9):
            total = jnp.where(at == q, jnp.sum(sums[q], axis=1, keepdims=True), total)
        wt[rows, :] = total[:, :16]

    over_groups(stream_grads)
    remote(hg_send, hg_recv, HG, {"col": lax.rem(col + NP - 1, NP)}).start()
    d1_send[...] = jnp.zeros_like(d1_send)
    d1_send[:, :DL] = wt[:DL, :].T * (1.0 / math.sqrt(SEQ))
    exchange("col", col, D1, lambda p: d1_send, d1_recv.at[col])
    d1_recv[col] = d1_send[...]

    wait_bytes(hg_recv, recv_sem.at[HG])
    for i in range(2):
        halo = hg_recv[i].astype(F32)
        ahead = jnp.where(lane < 112, pltpu.roll(halo, 112, 1), pltpu.roll(halo, 111, 1))
        ahead = jnp.where(lane == 127, 0.0, ahead)
        gp[14 + i] = gp[14 + i] + jnp.where(col == NP - 1, ahead, halo)
    send_home(lambda i, rows: gp[i, rows, :], i_send)
    exchange("row", row, IR, lambda p: i_send.at[p], tile_of(i_recv, row))
    i_recv[own_rows, :] = i_send[row]

    wait_bytes(gm_recv, recv_sem.at[GM])
    rev[...] = jnp.dot(
        gm_recv[...].reshape(8 * DL, N2), reverse, preferred_element_type=F32
    ).reshape(2, 4, DL, N2)
    fgr_ref[extra_row] = rev[0, 0]
    fgi_ref[extra_row] = -rev[1, 0]
    for i in range(1, 4):
        fgr_ref[4 + i] = rev[0, i]
        fgi_ref[4 + i] = -rev[1, i]

    wait_bytes(d1_recv.at[pl.ds(0, 15)], recv_sem.at[D1])
    total = d1_recv[0]
    for i in range(1, NP):
        total = total + d1_recv[i]
    d2_send[...] = total
    exchange("row", row, D2, lambda p: d2_send, d2_recv.at[row])
    d2_recv[row] = total

    def home(src, dst_ref):
        for i in range(6):
            block = src[128 * i : 128 * (i + 1), :].astype(F32).T
            dst_ref[:, :, 128 * i : 128 * (i + 1)] = block.astype(BF16).reshape(8, 16, 128)

    wait_bytes(m_recv.at[pl.ds(0, 15 * DL)], recv_sem.at[MR])
    home(m_recv, mixed_ref)
    wait_bytes(d2_recv.at[pl.ds(0, 15)], recv_sem.at[D2])
    spot = lax.broadcasted_iota(jnp.int32, (16, 128), 1)
    blocks = [jnp.zeros((16, 128), F32)] * 6
    for i in range(NP):
        block, off = divmod(DL * i, 128)
        piece = pltpu.roll(d2_recv[i], off, 1) if off else d2_recv[i]
        if off + DL > 128:
            blocks[block] = blocks[block] + jnp.where(spot >= off, piece, 0.0)
            blocks[block + 1] = blocks[block + 1] + jnp.where(spot < off, piece, 0.0)
        else:
            blocks[block] = blocks[block] + piece
    for tap in range(3):
        for stream in range(3):
            q = 3 * tap + stream
            for i in range(6):
                at = 768 * stream + 128 * i
                dw_ref[tap : tap + 1, at : at + 128] = blocks[i][q : q + 1, :]
    wait_bytes(i_recv.at[pl.ds(0, 15 * DL)], recv_sem.at[IR])
    home(i_recv, ig_ref)

    wait_bytes(xt.at[pl.ds(0, 15 * DL)], send_sem.at[XR])
    wait_bytes(ct.at[pl.ds(0, 15 * DL)], send_sem.at[CR])
    wait_bytes(fm, send_sem.at[FM])
    wait_bytes(hx_send, send_sem.at[HX])
    for ref, which in (
        (s_send, SS), (g_send, GG), (y_send, YY), (z_send, ZZ), (m_send, MR), (i_send, IR),
        (d1_recv, D1), (d2_recv, D2),
    ):
        wait_bytes(ref.at[pl.ds(0, 15)], send_sem.at[which])
    wait_bytes(gs_send, send_sem.at[GM])
    wait_bytes(hg_send, send_sem.at[HG])


def per_device(sequence, conv_weights, cotangent, filter_re, filter_im):
    first, last, second, fwd, inv = (jnp.asarray(t) for t in tables())
    vmem = pl.BlockSpec(memory_space=pltpu.VMEM)
    hbm = pl.BlockSpec(memory_space=pl.ANY)
    tiles = pltpu.VMEM((NP, DL, 128), BF16)
    planes = pltpu.VMEM((NP, DL, 128), F32)
    flat = pltpu.VMEM((NP * DL, 128), BF16)
    spec = pltpu.VMEM((2, 4, DL, N2), BF16)
    pair = pltpu.VMEM((2, DL, 128), BF16)
    small = pltpu.VMEM((NP, 16, 128), F32)
    one = pltpu.VMEM((16, 128), F32)
    return pl.pallas_call(
        kernel,
        out_shape=(
            jax.ShapeDtypeStruct(sequence.shape, BF16),
            jax.ShapeDtypeStruct(sequence.shape, BF16),
            jax.ShapeDtypeStruct(filter_re.shape, F32),
            jax.ShapeDtypeStruct(filter_re.shape, F32),
            jax.ShapeDtypeStruct(conv_weights.shape, F32),
        ),
        in_specs=[vmem, vmem, vmem, hbm, hbm, vmem, vmem, vmem, hbm, hbm],
        out_specs=[vmem] * 5,
        scratch_shapes=[
            flat, flat, flat, flat,
            pltpu.VMEM((16, 768), F32),
            pltpu.VMEM((768, 16), F32),
            pltpu.VMEM((9, DL, 128), F32),
            pltpu.VMEM((2, 8, DL, N2), BF16),
            spec,
            pltpu.VMEM((2, 4, DL, N2), F32),
            pltpu.VMEM((2, 5, DL, N2), F32),
            pltpu.VMEM((2, 16, 128), F32),
            pltpu.VMEM((2, 8, N2), F32),
            pltpu.VMEM((NP + 2, DL, 128), F32),
            pair, pair,
            planes, planes, planes, planes, planes,
            tiles,
            tiles, tiles, tiles, tiles, tiles, tiles, tiles, tiles,
            pltpu.VMEM((10, DL, N2), BF16),
            pltpu.VMEM((10, DL, 2 * N2), F32),
            pltpu.VMEM((5, DL, N2), F32),
            pltpu.VMEM((5, DL, N2), F32),
            pltpu.VMEM((8, DL, N2), F32),
            spec, spec,
            planes,
            pair, pair,
            one, small, one, small,
            tiles, flat, tiles, flat,
            pltpu.SemaphoreType.DMA((14,)),
            pltpu.SemaphoreType.DMA((14,)),
            pltpu.SemaphoreType.DMA((4,)),
        ],
        compiler_params=pltpu.CompilerParams(
            collective_id=0, has_side_effects=True, vmem_limit_bytes=40 * 1024 * 1024
        ),
    )(
        sequence, conv_weights, cotangent, filter_re, filter_im,
        first, last, second, fwd, inv,
    )


def solution(mesh):
    return jax.shard_map(
        per_device,
        mesh=mesh,
        in_specs=(
            P("row", "col", None),
            P(),
            P("row", "col", None),
            P("col", "row", None),
            P("col", "row", None),
        ),
        out_specs=(
            P("row", "col", None),
            P("row", "col", None),
            P("col", "row", None),
            P("col", "row", None),
            P(),
        ),
        check_vma=False,
    )
```

```python
import functools
import math

import jax
import jax.numpy as jnp
import ml_dtypes
import numpy as np
from jax import lax
from jax.experimental import pallas as pl
from jax.experimental.pallas import tpu as pltpu
from jax.sharding import PartitionSpec as P

MESH = pl.DeviceIdType.MESH
F32 = jnp.float32
BF16 = jnp.bfloat16

NP = 16
DL = 48
GR = 16
N1 = 128
N2 = 256
SEQ = N1 * N2

XR, CR, FM, HX, SS, GG, YY, ZZ, GM, HG, D1, MR, IR, D2 = range(14)


def slot_freq(col, slot):
    return 8 * col + slot + (1 if col >= 8 else 0)


def tables():
    lane_n1 = np.array([8 * (l % 16) + l // 16 for l in range(128)])
    first = np.zeros((128, 128))
    last = np.zeros((128, 128))
    for col in range(16):
        for slot in range(4):
            k1 = slot_freq(col, slot)
            turn = 2 * np.pi * (lane_n1 * k1 % 128) / 128
            re_row, im_row = slot * 16 + col, (slot + 4) * 16 + col
            if k1 == 0:
                first[:, re_row] = 1.0
                first[:, im_row] = np.cos(np.pi * lane_n1)
                last[re_row] = 1.0
                last[im_row] = np.cos(np.pi * lane_n1)
            else:
                first[:, re_row] = np.cos(turn)
                first[:, im_row] = -np.sin(turn)
                last[re_row] = np.cos(turn)
                last[im_row] = -np.sin(turn)
    last = last / SEQ
    idx = np.arange(N2)
    angle = 2 * np.pi * (idx[:, None] * idx[None, :] % N2) / N2
    second = np.concatenate([np.cos(angle), np.sin(angle)], 1)
    fwd = np.zeros((16, 2, 16, 128), np.float32)
    inv = np.zeros((16, 2, 8, N2), np.float32)
    low = np.arange(16)
    for col in range(16):
        for target in range(16):
            for slot in range(4):
                k1 = slot_freq(target, slot)
                turn = 2 * np.pi * (k1 * (16 * col + low) % SEQ) / SEQ
                re_l, im_l = slot * 16 + low, (slot + 4) * 16 + low
                fwd[col, 0, target, re_l] = np.cos(turn)
                fwd[col, 0, target, im_l] = np.cos(turn)
                fwd[col, 1, target, re_l] = np.sin(turn)
                fwd[col, 1, target, im_l] = -np.sin(turn)
        for slot in range(5):
            k1 = slot_freq(col, slot) if slot < 4 else 64
            turn = 2 * np.pi * (k1 * idx % SEQ) / SEQ
            inv[col, 0, slot] = np.cos(turn)
            inv[col, 1, slot] = np.sin(turn)
    return (
        first.astype(ml_dtypes.bfloat16),
        last.astype(ml_dtypes.bfloat16),
        second.astype(ml_dtypes.bfloat16),
        fwd,
        inv,
    )


def swap_bits(planes, pairs):
    lane = lax.broadcasted_iota(jnp.int32, planes[0].shape, 1)
    planes = list(planes)
    for plane_bit, lane_bit in pairs:
        shift = 1 << lane_bit
        upper = (lane & shift) != 0
        for i in range(len(planes)):
            if i & (1 << plane_bit):
                continue
            j = i | (1 << plane_bit)
            low, high = planes[i], planes[j]
            planes[i] = jnp.where(upper, pltpu.roll(high, shift, 1), low)
            planes[j] = jnp.where(upper, high, pltpu.roll(low, 128 - shift, 1))
    return planes


LOW4 = ((0, 0), (1, 1), (2, 2), (3, 3))
HIGH3 = ((0, 4), (1, 5), (2, 6))


def kernel(
    x_hbm, w_hbm, cot_hbm, fr_ref, fi_ref, first_hbm, last_hbm, second_hbm, fwd_ref, inv_ref,
    mixed_ref, ig_ref, fgr_ref, fgi_ref, dw_ref,
    x_ref, w_ref, cot_ref, first_ref, last_ref, second_ref,
    xt, xrecv, ct, crecv, w9, wt, wb, fo, fm, rev, fh, tf, ti,
    xp, hx_send, hx_recv, cp, ap, bp, sp, yp, fld,
    s_send, s_recv, g_send, g_recv, y_send, y_recv, z_send, z_recv,
    pp, uu, sr, si, qq, gs_send, gm_recv, gp, hg_send, hg_recv,
    d1_send, d1_recv, d2_send, d2_recv, m_send, m_recv, i_send, i_recv,
    send_sem, recv_sem, local_sem,
):
    row = lax.axis_index("row")
    col = lax.axis_index("col")
    low_half = col < 8

    def remote(src, dst, which, target):
        return pltpu.make_async_remote_copy(
            src_ref=src,
            dst_ref=dst,
            send_sem=send_sem.at[which],
            recv_sem=recv_sem.at[which],
            device_id=target,
            device_id_type=MESH,
        )

    def exchange(axis, me, which, src_at, dst):
        def body(step, carry):
            peer = lax.rem(me + step, NP)
            remote(src_at(peer), dst, which, {axis: peer}).start()
            return carry

        lax.fori_loop(1, NP, body, 0)

    def wait_bytes(ref, sem):
        pltpu.make_async_copy(ref, ref, sem).wait()

    leaving, arriving = {}, {}

    def under_way(which, sent, received):
        leaving[which], arriving[which] = sent, received

    def arrived(which):
        wait_bytes(arriving.pop(which), recv_sem.at[which])

    def drain():
        for which in list(arriving):
            arrived(which)
        for which, ref in leaving.items():
            wait_bytes(ref, send_sem.at[which])

    def tile_of(ref, peer):
        return ref.at[pl.ds(pl.multiple_of(peer * DL, DL), DL)]

    def over_groups(body):
        def step(g, carry):
            body(pl.ds(pl.multiple_of(g * GR, GR), GR))
            return carry

        lax.fori_loop(0, DL // GR, step, 0)

    x_load = pltpu.make_async_copy(x_hbm, x_ref, local_sem.at[4])
    cot_load = pltpu.make_async_copy(cot_hbm, cot_ref, local_sem.at[5])
    w_load = pltpu.make_async_copy(w_hbm, w_ref, local_sem.at[6])
    x_load.start()
    cot_load.start()
    w_load.start()
    loads = [
        pltpu.make_async_copy(first_hbm, first_ref, local_sem.at[7]),
        pltpu.make_async_copy(second_hbm, second_ref, local_sem.at[8]),
        pltpu.make_async_copy(last_hbm, last_ref, local_sem.at[9]),
        pltpu.make_async_copy(fr_ref, fo.at[0], local_sem.at[0]),
        pltpu.make_async_copy(fi_ref, fo.at[1], local_sem.at[1]),
        pltpu.make_async_copy(fwd_ref.at[col], tf, local_sem.at[2]),
        pltpu.make_async_copy(inv_ref.at[col], ti, local_sem.at[3]),
    ]
    for load in loads:
        load.start()

    barrier = pltpu.get_barrier_semaphore()

    def greet(step, carry):
        pl.semaphore_signal(
            barrier, inc=1, device_id={"row": lax.rem(row + step, NP)}, device_id_type=MESH
        )
        pl.semaphore_signal(
            barrier, inc=1, device_id={"col": lax.rem(col + step, NP)}, device_id_type=MESH
        )
        return carry

    lax.fori_loop(1, NP, greet, 0)

    def turn_home(src_ref, dst):
        for i in range(6):
            block = src_ref[:, :, 128 * i : 128 * (i + 1)].reshape(128, 128).astype(F32)
            dst[128 * i : 128 * (i + 1), :] = block.T.astype(BF16)

    x_load.wait()
    turn_home(x_ref, xt)
    pl.semaphore_wait(barrier, 2 * (NP - 1))

    partner = 15 - col
    extra_row = jnp.where(low_half, 4, 0)
    extra_to = jnp.where(low_half, partner, lax.rem(16 - col, 8))
    for part, ref in enumerate((fr_ref, fi_ref)):
        remote(ref.at[pl.ds(5, 3)], fm.at[part, pl.ds(1, 3)], FM, {"col": partner}).start()
        remote(ref.at[extra_row], fm.at[part, 0], FM, {"col": extra_to}).start()
    under_way(FM, fm, fm)

    exchange("row", row, XR, lambda p: tile_of(xt, p), tile_of(xrecv, row))
    under_way(XR, xt.at[pl.ds(0, 15 * DL)], xrecv.at[pl.ds(0, 15 * DL)])
    own_rows = pl.ds(pl.multiple_of(row * DL, DL), DL)
    xrecv[own_rows, :] = xt[own_rows, :]
    cot_load.wait()
    turn_home(cot_ref, ct)
    exchange("row", row, CR, lambda p: tile_of(ct, p), tile_of(crecv, row))
    under_way(CR, ct.at[pl.ds(0, 15 * DL)], crecv.at[pl.ds(0, 15 * DL)])
    crecv[own_rows, :] = ct[own_rows, :]

    w_load.wait()
    w9[...] = jnp.zeros_like(w9)
    for tap in range(3):
        for stream in range(3):
            q = 3 * tap + stream
            w9[q : q + 1, :] = w_ref[tap : tap + 1, 768 * stream : 768 * (stream + 1)]
    for i in range(6):
        wt[128 * i : 128 * (i + 1), :] = w9[:, 128 * i : 128 * (i + 1)].T
    columns = wt[own_rows, :]
    for q in range(9):
        wb[q] = jnp.broadcast_to(columns[:, q : q + 1], (DL, 128))
    for load in loads:
        load.wait()

    lane = lax.broadcasted_iota(jnp.int32, (DL, 128), 1)

    def planes_in(recv, dst, base):
        def body(rows):
            planes = [recv[i, rows, :].astype(F32) for i in range(NP)]
            planes = swap_bits(planes, LOW4)
            for i in range(NP):
                dst[base + i, rows, :] = planes[i]

        over_groups(body)

    def tiles_out(src, dst, table):
        def body(rows):
            flat = src[:, rows, :].reshape(NP * GR, 128)
            out = jnp.dot(flat, first_ref[...], preferred_element_type=F32).reshape(NP, GR, 128)
            tiles = swap_bits([out[i] for i in range(NP)], LOW4)
            for i in range(NP):
                turned = tiles[i] * tf[0, i : i + 1, :] + pltpu.roll(tiles[i], 64, 1) * tf[1, i : i + 1, :]
                dst[i, rows, :] = turned.astype(BF16)

        over_groups(body)

    arrived(XR)
    x3 = xrecv.reshape(NP, DL, 128)
    planes_in(x3, xp, 2)
    hx_send[0] = xp[16].astype(BF16)
    hx_send[1] = xp[17].astype(BF16)
    remote(hx_send, hx_recv, HX, {"col": lax.rem(col + 1, NP)}).start()
    under_way(HX, hx_send, hx_recv)

    arrived(CR)
    planes_in(crecv.reshape(NP, DL, 128), cp, 0)
    arrived(HX)
    for i in range(2):
        halo = hx_recv[i].astype(F32)
        back = jnp.where(lane >= 16, pltpu.roll(halo, 16, 1), pltpu.roll(halo, 17, 1))
        back = jnp.where(lane == 0, 0.0, back)
        xp[i] = jnp.where(col == 0, back, halo)

    def streams(rows):
        taps = [wb[q, rows, :] for q in range(9)]
        behind2, behind1 = xp[0, rows, :], xp[1, rows, :]
        for i in range(NP):
            now = xp[i + 2, rows, :]
            z = [taps[j] * now + taps[3 + j] * behind1 + taps[6 + j] * behind2 for j in range(3)]
            ap[i, rows, :] = z[0]
            bp[i, rows, :] = z[1]
            sp[i, rows, :] = z[2]
            fld[i, rows, :] = (z[0] * z[1]).astype(BF16)
            behind2, behind1 = behind1, now

    over_groups(streams)
    tiles_out(fld, s_send, tf)
    exchange("col", col, SS, lambda p: s_send.at[p], s_recv.at[col])
    under_way(SS, s_send.at[pl.ds(0, 15)], s_recv.at[pl.ds(0, 15)])
    s_recv[col] = s_send[col]

    def gate_grad(rows):
        for i in range(NP):
            fld[i, rows, :] = (cp[i, rows, :] * sp[i, rows, :]).astype(BF16)

    over_groups(gate_grad)
    tiles_out(fld, g_send, tf)
    exchange("col", col, GG, lambda p: g_send.at[p], g_recv.at[col])
    under_way(GG, g_send.at[pl.ds(0, 15)], g_recv.at[pl.ds(0, 15)])
    g_recv[col] = g_send[col]

    arrived(FM)
    at_row = lax.broadcasted_iota(jnp.int32, (N2, N2), 0)
    at_col = lax.broadcasted_iota(jnp.int32, (N2, N2), 1)
    reverse = jnp.where(at_row + at_col == N2 - 1, 1.0, 0.0).astype(BF16)
    rev[...] = jnp.dot(
        fm[...].reshape(8 * DL, N2), reverse, preferred_element_type=F32
    ).reshape(2, 4, DL, N2)

    def mirror_at(slot):
        return jnp.where(low_half, (4 - slot) % 4, 3 - slot)

    own_at = jnp.where(low_half, 0, 1)
    for slot in range(4):
        rev_re = rev[0, mirror_at(slot)]
        rev_im = -rev[1, mirror_at(slot)]
        if slot == 0:
            fh[0, 4] = rev_re
            fh[1, 4] = rev_im
            rev_re = jnp.where(col == 0, 0.0, rev_re)
            rev_im = jnp.where(col == 0, 0.0, rev_im)
        fh[0, slot] = fo[0, own_at + slot].astype(F32) + rev_re
        fh[1, slot] = fo[1, own_at + slot].astype(F32) + rev_im

    parts = [(0, 4), (1, 5), (2, 6), (3, 7), (8, 9)]

    def spectrum(recv):
        def body(rows):
            planes = swap_bits([recv[i, rows, :].astype(F32) for i in range(NP)], HIGH3)
            for i in range(NP):
                half = i // 8
                pp[i % 8, rows, 128 * half : 128 * (half + 1)] = planes[i].astype(BF16)

        over_groups(body)
        middle = pp[4].astype(F32)
        pp[8] = (middle * ti[0, 4:5, :]).astype(BF16)
        pp[9] = (-middle * ti[1, 4:5, :]).astype(BF16)
        pp[4] = jnp.where(col == 0, 0.0, middle).astype(BF16)
        uu[...] = jnp.dot(
            pp[...].reshape(10 * DL, N2), second_ref[...], preferred_element_type=F32
        ).reshape(10, DL, 2 * N2)

    def value(slot):
        re, im = parts[slot]
        return (
            uu[re, :, :N2] + uu[im, :, N2:],
            uu[im, :, :N2] - uu[re, :, N2:],
        )

    def restore(dst):
        uu[...] = jnp.dot(
            pp[...].reshape(10 * DL, N2), second_ref[...], preferred_element_type=F32
        ).reshape(10, DL, 2 * N2)
        for slot in range(4):
            re, im = parts[slot]
            z_re = uu[re, :, :N2] - uu[im, :, N2:]
            z_im = uu[im, :, :N2] + uu[re, :, N2:]
            cos, sin = ti[0, slot : slot + 1, :], ti[1, slot : slot + 1, :]
            qq[slot] = z_re * cos - z_im * sin
            q_im = z_im * cos + z_re * sin
            if slot == 0:
                re4, im4 = parts[4]
                z_re4 = uu[re4, :, :N2] - uu[im4, :, N2:]
                z_im4 = uu[im4, :, :N2] + uu[re4, :, N2:]
                q_im = jnp.where(col == 0, z_re4 * ti[0, 4:5, :] - z_im4 * ti[1, 4:5, :], q_im)
            qq[4 + slot] = q_im

        def body(rows):
            planes = [
                qq[i % 8, rows, 128 * (i // 8) : 128 * (i // 8 + 1)] for i in range(NP)
            ]
            planes = swap_bits(planes, HIGH3)
            for i in range(NP):
                dst[i, rows, :] = planes[i].astype(BF16)

        over_groups(body)

    arrived(SS)
    spectrum(s_recv)
    for slot in range(5):
        re, im = parts[slot]
        s_re, s_im = value(slot)
        sr[slot] = s_re
        si[slot] = s_im
        f_re, f_im = fh[0, slot], fh[1, slot]
        pp[re] = (s_re * f_re - s_im * f_im).astype(BF16)
        pp[im] = (s_re * f_im + s_im * f_re).astype(BF16)
    restore(y_send)
    exchange("col", col, YY, lambda p: y_send.at[p], y_recv.at[col])
    under_way(YY, y_send.at[pl.ds(0, 15)], y_recv.at[pl.ds(0, 15)])
    y_recv[col] = y_send[col]

    arrived(GG)
    spectrum(g_recv)
    for slot in range(5):
        re, im = parts[slot]
        g_re, g_im = value(slot)
        f_re, f_im = fh[0, slot], fh[1, slot]
        pp[re] = (g_re * f_re + g_im * f_im).astype(BF16)
        pp[im] = (g_im * f_re - g_re * f_im).astype(BF16)
        s_re, s_im = sr[slot], si[slot]
        grad_re = (s_re * g_re + s_im * g_im) * (1.0 / SEQ)
        grad_im = (s_re * g_im - s_im * g_re) * (1.0 / SEQ)
        if slot < 4:
            fgr_ref[own_at + slot] = grad_re
            fgi_ref[own_at + slot] = grad_im
            gs_send[0, mirror_at(slot)] = grad_re.astype(BF16)
            gs_send[1, mirror_at(slot)] = grad_im.astype(BF16)
        else:
            gs_send[0, 0] = jnp.where(col == 0, grad_re, gs_send[0, 0].astype(F32)).astype(BF16)
            gs_send[1, 0] = jnp.where(col == 0, grad_im, gs_send[1, 0].astype(F32)).astype(BF16)
    restore(z_send)
    exchange("col", col, ZZ, lambda p: z_send.at[p], z_recv.at[col])
    under_way(ZZ, z_send.at[pl.ds(0, 15)], z_recv.at[pl.ds(0, 15)])
    z_recv[col] = z_send[col]
    def send_mirrored():
        back_to = jnp.where(low_half, jnp.where(col == 0, 8, 16 - col), partner)
        back_to = lax.rem(back_to, NP)
        for part in range(2):
            remote(gs_send.at[part, pl.ds(1, 3)], gm_recv.at[part, pl.ds(1, 3)], GM, {"col": partner}).start()
            remote(gs_send.at[part, 0], gm_recv.at[part, 0], GM, {"col": back_to}).start()
        under_way(GM, gs_send, gm_recv)

    def field_back(recv, dst):
        def body(rows):
            planes = swap_bits([recv[i, rows, :].astype(F32) for i in range(NP)], LOW4)
            flat = jnp.stack([p.astype(BF16) for p in planes]).reshape(NP * GR, 128)
            out = jnp.dot(flat, last_ref[...], preferred_element_type=F32)
            dst[:, rows, :] = out.astype(BF16).astype(F32).reshape(NP, GR, 128)

        over_groups(body)

    def send_home(make, dst):
        def body(rows):
            tiles = swap_bits([make(i, rows) for i in range(NP)], LOW4)
            for i in range(NP):
                dst[i, rows, :] = tiles[i].astype(BF16)

        over_groups(body)

    arrived(YY)
    field_back(y_recv, yp)
    send_home(lambda i, rows: sp[i, rows, :] * yp[i, rows, :], m_send)
    exchange("row", row, MR, lambda p: m_send.at[p], tile_of(m_recv, row))
    under_way(MR, m_send.at[pl.ds(0, 15)], m_recv.at[pl.ds(0, 15 * DL)])
    m_recv[own_rows, :] = m_send[row]

    send_mirrored()
    arrived(ZZ)
    field_back(z_recv, gp)

    def rounded(value):
        return value.astype(BF16).astype(F32)

    def stream_grads(rows):
        taps = [wb[q, rows, :] for q in range(9)]
        sums = [jnp.zeros((GR, 128), F32)] * 9
        before1 = before2 = None
        for i in range(NP):
            gs = gp[i, rows, :]
            grads = (
                rounded(gs * bp[i, rows, :]),
                rounded(gs * ap[i, rows, :]),
                rounded(cp[i, rows, :] * yp[i, rows, :]),
            )
            at_tap = [
                taps[3 * t] * grads[0] + taps[3 * t + 1] * grads[1] + taps[3 * t + 2] * grads[2]
                for t in range(3)
            ]
            past = [xp[i + 2 - t, rows, :] for t in range(3)]
            sums = [sums[q] + past[q // 3] * grads[q % 3] for q in range(9)]
            if i == 0:
                hg_send[0, rows, :] = at_tap[2].astype(BF16)
                first_one = at_tap[1]
            if i == 1:
                hg_send[1, rows, :] = (first_one + at_tap[2]).astype(BF16)
            if before2 is not None:
                gp[i - 2, rows, :] = before2 + at_tap[2]
            before2 = None if before1 is None else before1 + at_tap[1]
            before1 = at_tap[0]
        gp[14, rows, :] = before2
        gp[15, rows, :] = before1
        at = lax.broadcasted_iota(jnp.int32, (GR, 128), 1)
        total = jnp.zeros((GR, 128), F32)
        for q in range(9):
            total = jnp.where(at == q, jnp.sum(sums[q], axis=1, keepdims=True), total)
        wt[rows, :] = total[:, :16]

    over_groups(stream_grads)
    remote(hg_send, hg_recv, HG, {"col": lax.rem(col + NP - 1, NP)}).start()
    under_way(HG, hg_send, hg_recv)
    d1_send[...] = jnp.zeros_like(d1_send)
    d1_send[:, :DL] = wt[:DL, :].T * (1.0 / math.sqrt(SEQ))
    exchange("col", col, D1, lambda p: d1_send, d1_recv.at[col])
    under_way(D1, d1_recv.at[pl.ds(0, 15)], d1_recv.at[pl.ds(0, 15)])
    d1_recv[col] = d1_send[...]

    arrived(D1)
    total = d1_recv[0]
    for i in range(1, NP):
        total = total + d1_recv[i]
    d2_send[...] = total
    exchange("row", row, D2, lambda p: d2_send, d2_recv.at[row])
    under_way(D2, d2_recv.at[pl.ds(0, 15)], d2_recv.at[pl.ds(0, 15)])
    d2_recv[row] = total

    arrived(HG)
    for i in range(2):
        halo = hg_recv[i].astype(F32)
        ahead = jnp.where(lane < 112, pltpu.roll(halo, 112, 1), pltpu.roll(halo, 111, 1))
        ahead = jnp.where(lane == 127, 0.0, ahead)
        gp[14 + i] = gp[14 + i] + jnp.where(col == NP - 1, ahead, halo)
    send_home(lambda i, rows: gp[i, rows, :], i_send)
    exchange("row", row, IR, lambda p: i_send.at[p], tile_of(i_recv, row))
    under_way(IR, i_send.at[pl.ds(0, 15)], i_recv.at[pl.ds(0, 15 * DL)])
    i_recv[own_rows, :] = i_send[row]

    def home(src, dst_ref):
        for i in range(6):
            block = src[128 * i : 128 * (i + 1), :].astype(F32).T
            dst_ref[:, :, 128 * i : 128 * (i + 1)] = block.astype(BF16).reshape(8, 16, 128)

    arrived(MR)
    home(m_recv, mixed_ref)

    arrived(GM)
    rev[...] = jnp.dot(
        gm_recv[...].reshape(8 * DL, N2), reverse, preferred_element_type=F32
    ).reshape(2, 4, DL, N2)
    fgr_ref[extra_row] = rev[0, 0]
    fgi_ref[extra_row] = -rev[1, 0]
    for i in range(1, 4):
        fgr_ref[4 + i] = rev[0, i]
        fgi_ref[4 + i] = -rev[1, i]

    arrived(D2)
    spot = lax.broadcasted_iota(jnp.int32, (16, 128), 1)
    blocks = [jnp.zeros((16, 128), F32)] * 6
    for i in range(NP):
        block, off = divmod(DL * i, 128)
        piece = pltpu.roll(d2_recv[i], off, 1) if off else d2_recv[i]
        if off + DL > 128:
            blocks[block] = blocks[block] + jnp.where(spot >= off, piece, 0.0)
            blocks[block + 1] = blocks[block + 1] + jnp.where(spot < off, piece, 0.0)
        else:
            blocks[block] = blocks[block] + piece
    for tap in range(3):
        for stream in range(3):
            q = 3 * tap + stream
            for i in range(6):
                at = 768 * stream + 128 * i
                dw_ref[tap : tap + 1, at : at + 128] = blocks[i][q : q + 1, :]
    arrived(IR)
    home(i_recv, ig_ref)

    drain()


def finish(*refs):
    count = len(refs) // 2
    sems = refs[-1]
    copies = [
        pltpu.make_async_copy(refs[i], refs[count + i], sems.at[i]) for i in range(count)
    ]
    for copy in copies:
        copy.start()
    for copy in copies:
        copy.wait()


def per_device(sequence, conv_weights, cotangent, filter_re, filter_im):
    first, last, second, fwd, inv = (jnp.asarray(t) for t in tables())
    vmem = pl.BlockSpec(memory_space=pltpu.VMEM)
    hbm = pl.BlockSpec(memory_space=pl.ANY)
    tiles = pltpu.VMEM((NP, DL, 128), BF16)
    planes = pltpu.VMEM((NP, DL, 128), F32)
    flat = pltpu.VMEM((NP * DL, 128), BF16)
    spec = pltpu.VMEM((2, 4, DL, N2), BF16)
    pair = pltpu.VMEM((2, DL, 128), BF16)
    small = pltpu.VMEM((NP, 16, 128), F32)
    one = pltpu.VMEM((16, 128), F32)
    shapes = (
        jax.ShapeDtypeStruct(sequence.shape, BF16),
        jax.ShapeDtypeStruct(sequence.shape, BF16),
        jax.ShapeDtypeStruct(filter_re.shape, F32),
        jax.ShapeDtypeStruct(filter_re.shape, F32),
        jax.ShapeDtypeStruct(conv_weights.shape, F32),
    )
    outs = pl.pallas_call(
        kernel,
        out_shape=shapes,
        in_specs=[hbm] * 10,
        out_specs=[vmem] * 5,
        scratch_shapes=[
            pltpu.VMEM(sequence.shape, BF16),
            pltpu.VMEM(conv_weights.shape, F32),
            pltpu.VMEM(sequence.shape, BF16),
            pltpu.VMEM((128, 128), BF16),
            pltpu.VMEM((128, 128), BF16),
            pltpu.VMEM((N2, 2 * N2), BF16),
            flat, flat, flat, flat,
            pltpu.VMEM((16, 768), F32),
            pltpu.VMEM((768, 16), F32),
            pltpu.VMEM((9, DL, 128), F32),
            pltpu.VMEM((2, 8, DL, N2), BF16),
            spec,
            pltpu.VMEM((2, 4, DL, N2), F32),
            pltpu.VMEM((2, 5, DL, N2), F32),
            pltpu.VMEM((2, 16, 128), F32),
            pltpu.VMEM((2, 8, N2), F32),
            pltpu.VMEM((NP + 2, DL, 128), F32),
            pair, pair,
            planes, planes, planes, planes, planes,
            tiles,
            tiles, tiles, tiles, tiles, tiles, tiles, tiles, tiles,
            pltpu.VMEM((10, DL, N2), BF16),
            pltpu.VMEM((10, DL, 2 * N2), F32),
            pltpu.VMEM((5, DL, N2), F32),
            pltpu.VMEM((5, DL, N2), F32),
            pltpu.VMEM((8, DL, N2), F32),
            spec, spec,
            planes,
            pair, pair,
            one, small, one, small,
            tiles, flat, tiles, flat,
            pltpu.SemaphoreType.DMA((14,)),
            pltpu.SemaphoreType.DMA((14,)),
            pltpu.SemaphoreType.DMA((10,)),
        ],
        compiler_params=pltpu.CompilerParams(
            collective_id=0, has_side_effects=True, vmem_limit_bytes=56 * 1024 * 1024
        ),
    )(
        sequence, conv_weights, cotangent, filter_re, filter_im,
        first, last, second, fwd, inv,
    )
    return pl.pallas_call(
        finish,
        out_shape=shapes,
        in_specs=[vmem] * 5,
        out_specs=[hbm] * 5,
        scratch_shapes=[pltpu.SemaphoreType.DMA((5,))],
    )(*outs)


def solution(mesh):
    return jax.shard_map(
        per_device,
        mesh=mesh,
        in_specs=(
            P("row", "col", None),
            P(),
            P("row", "col", None),
            P("col", "row", None),
            P("col", "row", None),
        ),
        out_specs=(
            P("row", "col", None),
            P("row", "col", None),
            P("col", "row", None),
            P("col", "row", None),
            P(),
        ),
        check_vma=False,
    )
```

```python
import functools
import math

import jax
import jax.numpy as jnp
import ml_dtypes
import numpy as np
from jax import lax
from jax.experimental import pallas as pl
from jax.experimental.pallas import tpu as pltpu
from jax.sharding import PartitionSpec as P

MESH = pl.DeviceIdType.MESH
F32 = jnp.float32
BF16 = jnp.bfloat16

NP = 16
DL = 48
GR = 16
N1 = 128
N2 = 256
SEQ = N1 * N2

XR, CR, FM, HX, SS, GG, YY, ZZ, GM, HG, D1, MR, IR, D2 = range(14)


def slot_freq(col, slot):
    return 8 * col + slot + (1 if col >= 8 else 0)


def tables():
    lane_n1 = np.array([8 * (l % 16) + l // 16 for l in range(128)])
    first = np.zeros((128, 128))
    last = np.zeros((128, 128))
    for col in range(16):
        for slot in range(4):
            k1 = slot_freq(col, slot)
            turn = 2 * np.pi * (lane_n1 * k1 % 128) / 128
            re_row, im_row = slot * 16 + col, (slot + 4) * 16 + col
            if k1 == 0:
                first[:, re_row] = 1.0
                first[:, im_row] = np.cos(np.pi * lane_n1)
                last[re_row] = 1.0
                last[im_row] = np.cos(np.pi * lane_n1)
            else:
                first[:, re_row] = np.cos(turn)
                first[:, im_row] = -np.sin(turn)
                last[re_row] = np.cos(turn)
                last[im_row] = -np.sin(turn)
    last = last / SEQ
    idx = np.arange(N2)
    angle = 2 * np.pi * (idx[:, None] * idx[None, :] % N2) / N2
    second = np.concatenate([np.cos(angle), np.sin(angle)], 1)
    fwd = np.zeros((16, 2, 16, 128), np.float32)
    inv = np.zeros((16, 2, 8, N2), np.float32)
    low = np.arange(16)
    for col in range(16):
        for target in range(16):
            for slot in range(4):
                k1 = slot_freq(target, slot)
                turn = 2 * np.pi * (k1 * (16 * col + low) % SEQ) / SEQ
                re_l, im_l = slot * 16 + low, (slot + 4) * 16 + low
                fwd[col, 0, target, re_l] = np.cos(turn)
                fwd[col, 0, target, im_l] = np.cos(turn)
                fwd[col, 1, target, re_l] = np.sin(turn)
                fwd[col, 1, target, im_l] = -np.sin(turn)
        for slot in range(5):
            k1 = slot_freq(col, slot) if slot < 4 else 64
            turn = 2 * np.pi * (k1 * idx % SEQ) / SEQ
            inv[col, 0, slot] = np.cos(turn)
            inv[col, 1, slot] = np.sin(turn)
    return (
        first.astype(ml_dtypes.bfloat16),
        last.astype(ml_dtypes.bfloat16),
        second.astype(ml_dtypes.bfloat16),
        fwd,
        inv,
    )


def swap_bits(planes, pairs):
    lane = lax.broadcasted_iota(jnp.int32, planes[0].shape, 1)
    planes = list(planes)
    for plane_bit, lane_bit in pairs:
        shift = 1 << lane_bit
        upper = (lane & shift) != 0
        for i in range(len(planes)):
            if i & (1 << plane_bit):
                continue
            j = i | (1 << plane_bit)
            low, high = planes[i], planes[j]
            planes[i] = jnp.where(upper, pltpu.roll(high, shift, 1), low)
            planes[j] = jnp.where(upper, high, pltpu.roll(low, 128 - shift, 1))
    return planes


LOW4 = ((0, 0), (1, 1), (2, 2), (3, 3))
HIGH3 = ((0, 4), (1, 5), (2, 6))


def kernel(
    x_hbm, w_hbm, cot_hbm, fr_ref, fi_ref, first_hbm, last_hbm, second_hbm, fwd_ref, inv_ref,
    mixed_hbm, ig_hbm, fgr_hbm, fgi_hbm, dw_hbm,
    mixed_ref, ig_ref, fgr_ref, fgi_ref, dw_ref,
    x_ref, w_ref, cot_ref, first_ref, last_ref, second_ref,
    xt, xrecv, ct, crecv, w9, wt, wb, fo, fm, rev, fh, tf, ti,
    xp, hx_send, hx_recv, cp, ap, bp, sp, yp, fld,
    s_send, s_recv, g_send, g_recv, y_send, y_recv, z_send, z_recv,
    pp, uu, sr, si, qq, gs_send, gm_recv, gp, hg_send, hg_recv,
    d1_send, d1_recv, d2_send, d2_recv, m_send, m_recv, i_send, i_recv,
    send_sem, recv_sem, local_sem,
):
    row = lax.axis_index("row")
    col = lax.axis_index("col")
    low_half = col < 8

    def remote(src, dst, which, target):
        return pltpu.make_async_remote_copy(
            src_ref=src,
            dst_ref=dst,
            send_sem=send_sem.at[which],
            recv_sem=recv_sem.at[which],
            device_id=target,
            device_id_type=MESH,
        )

    def exchange(axis, me, which, src_at, dst):
        def body(step, carry):
            peer = lax.rem(me + step, NP)
            remote(src_at(peer), dst, which, {axis: peer}).start()
            return carry

        lax.fori_loop(1, NP, body, 0)

    def wait_bytes(ref, sem):
        pltpu.make_async_copy(ref, ref, sem).wait()

    leaving, arriving = {}, {}
    stores = []

    def store(src, dst):
        stores.append(pltpu.make_async_copy(src, dst, local_sem.at[10 + len(stores)]))
        stores[-1].start()

    def under_way(which, sent, received):
        leaving[which], arriving[which] = sent, received

    def arrived(which):
        wait_bytes(arriving.pop(which), recv_sem.at[which])

    def drain():
        for which in list(arriving):
            arrived(which)
        for which, ref in leaving.items():
            wait_bytes(ref, send_sem.at[which])

    def tile_of(ref, peer):
        return ref.at[pl.ds(pl.multiple_of(peer * DL, DL), DL)]

    def over_groups(body):
        def step(g, carry):
            body(pl.ds(pl.multiple_of(g * GR, GR), GR))
            return carry

        lax.fori_loop(0, DL // GR, step, 0)

    x_load = pltpu.make_async_copy(x_hbm, x_ref, local_sem.at[4])
    cot_load = pltpu.make_async_copy(cot_hbm, cot_ref, local_sem.at[5])
    w_load = pltpu.make_async_copy(w_hbm, w_ref, local_sem.at[6])
    x_load.start()
    cot_load.start()
    w_load.start()
    loads = [
        pltpu.make_async_copy(first_hbm, first_ref, local_sem.at[7]),
        pltpu.make_async_copy(second_hbm, second_ref, local_sem.at[8]),
        pltpu.make_async_copy(last_hbm, last_ref, local_sem.at[9]),
        pltpu.make_async_copy(fr_ref, fo.at[0], local_sem.at[0]),
        pltpu.make_async_copy(fi_ref, fo.at[1], local_sem.at[1]),
        pltpu.make_async_copy(fwd_ref.at[col], tf, local_sem.at[2]),
        pltpu.make_async_copy(inv_ref.at[col], ti, local_sem.at[3]),
    ]
    for load in loads:
        load.start()

    barrier = pltpu.get_barrier_semaphore()

    def greet(step, carry):
        pl.semaphore_signal(
            barrier, inc=1, device_id={"row": lax.rem(row + step, NP)}, device_id_type=MESH
        )
        pl.semaphore_signal(
            barrier, inc=1, device_id={"col": lax.rem(col + step, NP)}, device_id_type=MESH
        )
        return carry

    lax.fori_loop(1, NP, greet, 0)

    def turn_home(src_ref, dst):
        for i in range(6):
            block = src_ref[:, :, 128 * i : 128 * (i + 1)].reshape(128, 128).astype(F32)
            dst[128 * i : 128 * (i + 1), :] = block.T.astype(BF16)

    x_load.wait()
    turn_home(x_ref, xt)
    pl.semaphore_wait(barrier, 2 * (NP - 1))

    partner = 15 - col
    extra_row = jnp.where(low_half, 4, 0)
    extra_to = jnp.where(low_half, partner, lax.rem(16 - col, 8))
    for part, ref in enumerate((fr_ref, fi_ref)):
        remote(ref.at[pl.ds(5, 3)], fm.at[part, pl.ds(1, 3)], FM, {"col": partner}).start()
        remote(ref.at[extra_row], fm.at[part, 0], FM, {"col": extra_to}).start()
    under_way(FM, fm, fm)

    exchange("row", row, XR, lambda p: tile_of(xt, p), tile_of(xrecv, row))
    under_way(XR, xt.at[pl.ds(0, 15 * DL)], xrecv.at[pl.ds(0, 15 * DL)])
    own_rows = pl.ds(pl.multiple_of(row * DL, DL), DL)
    xrecv[own_rows, :] = xt[own_rows, :]
    cot_load.wait()
    turn_home(cot_ref, ct)
    exchange("row", row, CR, lambda p: tile_of(ct, p), tile_of(crecv, row))
    under_way(CR, ct.at[pl.ds(0, 15 * DL)], crecv.at[pl.ds(0, 15 * DL)])
    crecv[own_rows, :] = ct[own_rows, :]

    w_load.wait()
    w9[...] = jnp.zeros_like(w9)
    for tap in range(3):
        for stream in range(3):
            q = 3 * tap + stream
            w9[q : q + 1, :] = w_ref[tap : tap + 1, 768 * stream : 768 * (stream + 1)]
    for i in range(6):
        wt[128 * i : 128 * (i + 1), :] = w9[:, 128 * i : 128 * (i + 1)].T
    columns = wt[own_rows, :]
    for q in range(9):
        wb[q] = jnp.broadcast_to(columns[:, q : q + 1], (DL, 128))
    for load in loads:
        load.wait()

    lane = lax.broadcasted_iota(jnp.int32, (DL, 128), 1)

    def planes_in(recv, dst, base):
        def body(rows):
            planes = [recv[i, rows, :].astype(F32) for i in range(NP)]
            planes = swap_bits(planes, LOW4)
            for i in range(NP):
                dst[base + i, rows, :] = planes[i]

        over_groups(body)

    def tiles_out(src, dst, table):
        def body(rows):
            flat = src[:, rows, :].reshape(NP * GR, 128)
            out = jnp.dot(flat, first_ref[...], preferred_element_type=F32).reshape(NP, GR, 128)
            tiles = swap_bits([out[i] for i in range(NP)], LOW4)
            for i in range(NP):
                turned = tiles[i] * tf[0, i : i + 1, :] + pltpu.roll(tiles[i], 64, 1) * tf[1, i : i + 1, :]
                dst[i, rows, :] = turned.astype(BF16)

        over_groups(body)

    arrived(XR)
    x3 = xrecv.reshape(NP, DL, 128)
    planes_in(x3, xp, 2)
    hx_send[0] = xp[16].astype(BF16)
    hx_send[1] = xp[17].astype(BF16)
    remote(hx_send, hx_recv, HX, {"col": lax.rem(col + 1, NP)}).start()
    under_way(HX, hx_send, hx_recv)

    def streams(first, last):
        def body(rows):
            taps = [wb[q, rows, :] for q in range(9)]
            behind2, behind1 = xp[first, rows, :], xp[first + 1, rows, :]
            for i in range(first, last):
                now = xp[i + 2, rows, :]
                z = [taps[j] * now + taps[3 + j] * behind1 + taps[6 + j] * behind2 for j in range(3)]
                ap[i, rows, :] = z[0]
                bp[i, rows, :] = z[1]
                sp[i, rows, :] = z[2]
                fld[i, rows, :] = (z[0] * z[1]).astype(BF16)
                behind2, behind1 = behind1, now

        return body

    over_groups(streams(2, NP))
    arrived(CR)
    planes_in(crecv.reshape(NP, DL, 128), cp, 0)
    arrived(HX)
    for i in range(2):
        halo = hx_recv[i].astype(F32)
        back = jnp.where(lane >= 16, pltpu.roll(halo, 16, 1), pltpu.roll(halo, 17, 1))
        back = jnp.where(lane == 0, 0.0, back)
        xp[i] = jnp.where(col == 0, back, halo)

    over_groups(streams(0, 2))
    tiles_out(fld, s_send, tf)
    exchange("col", col, SS, lambda p: s_send.at[p], s_recv.at[col])
    under_way(SS, s_send.at[pl.ds(0, 15)], s_recv.at[pl.ds(0, 15)])
    s_recv[col] = s_send[col]

    def gate_grad(rows):
        for i in range(NP):
            fld[i, rows, :] = (cp[i, rows, :] * sp[i, rows, :]).astype(BF16)

    over_groups(gate_grad)
    tiles_out(fld, g_send, tf)
    exchange("col", col, GG, lambda p: g_send.at[p], g_recv.at[col])
    under_way(GG, g_send.at[pl.ds(0, 15)], g_recv.at[pl.ds(0, 15)])
    g_recv[col] = g_send[col]

    arrived(FM)
    at_row = lax.broadcasted_iota(jnp.int32, (N2, N2), 0)
    at_col = lax.broadcasted_iota(jnp.int32, (N2, N2), 1)
    reverse = jnp.where(at_row + at_col == N2 - 1, 1.0, 0.0).astype(BF16)
    rev[...] = jnp.dot(
        fm[...].reshape(8 * DL, N2), reverse, preferred_element_type=F32
    ).reshape(2, 4, DL, N2)

    def mirror_at(slot):
        return jnp.where(low_half, (4 - slot) % 4, 3 - slot)

    own_at = jnp.where(low_half, 0, 1)
    for slot in range(4):
        rev_re = rev[0, mirror_at(slot)]
        rev_im = -rev[1, mirror_at(slot)]
        if slot == 0:
            fh[0, 4] = rev_re
            fh[1, 4] = rev_im
            rev_re = jnp.where(col == 0, 0.0, rev_re)
            rev_im = jnp.where(col == 0, 0.0, rev_im)
        fh[0, slot] = fo[0, own_at + slot].astype(F32) + rev_re
        fh[1, slot] = fo[1, own_at + slot].astype(F32) + rev_im

    parts = [(0, 4), (1, 5), (2, 6), (3, 7), (8, 9)]

    def spectrum(recv):
        def body(rows):
            planes = swap_bits([recv[i, rows, :].astype(F32) for i in range(NP)], HIGH3)
            for i in range(NP):
                half = i // 8
                pp[i % 8, rows, 128 * half : 128 * (half + 1)] = planes[i].astype(BF16)

        over_groups(body)
        middle = pp[4].astype(F32)
        pp[8] = (middle * ti[0, 4:5, :]).astype(BF16)
        pp[9] = (-middle * ti[1, 4:5, :]).astype(BF16)
        pp[4] = jnp.where(col == 0, 0.0, middle).astype(BF16)
        uu[...] = jnp.dot(
            pp[...].reshape(10 * DL, N2), second_ref[...], preferred_element_type=F32
        ).reshape(10, DL, 2 * N2)

    def value(slot):
        re, im = parts[slot]
        return (
            uu[re, :, :N2] + uu[im, :, N2:],
            uu[im, :, :N2] - uu[re, :, N2:],
        )

    def restore(dst):
        uu[...] = jnp.dot(
            pp[...].reshape(10 * DL, N2), second_ref[...], preferred_element_type=F32
        ).reshape(10, DL, 2 * N2)
        for slot in range(4):
            re, im = parts[slot]
            z_re = uu[re, :, :N2] - uu[im, :, N2:]
            z_im = uu[im, :, :N2] + uu[re, :, N2:]
            cos, sin = ti[0, slot : slot + 1, :], ti[1, slot : slot + 1, :]
            qq[slot] = z_re * cos - z_im * sin
            q_im = z_im * cos + z_re * sin
            if slot == 0:
                re4, im4 = parts[4]
                z_re4 = uu[re4, :, :N2] - uu[im4, :, N2:]
                z_im4 = uu[im4, :, :N2] + uu[re4, :, N2:]
                q_im = jnp.where(col == 0, z_re4 * ti[0, 4:5, :] - z_im4 * ti[1, 4:5, :], q_im)
            qq[4 + slot] = q_im

        def body(rows):
            planes = [
                qq[i % 8, rows, 128 * (i // 8) : 128 * (i // 8 + 1)] for i in range(NP)
            ]
            planes = swap_bits(planes, HIGH3)
            for i in range(NP):
                dst[i, rows, :] = planes[i].astype(BF16)

        over_groups(body)

    arrived(SS)
    spectrum(s_recv)
    for slot in range(5):
        re, im = parts[slot]
        s_re, s_im = value(slot)
        sr[slot] = s_re
        si[slot] = s_im
        f_re, f_im = fh[0, slot], fh[1, slot]
        pp[re] = (s_re * f_re - s_im * f_im).astype(BF16)
        pp[im] = (s_re * f_im + s_im * f_re).astype(BF16)
    restore(y_send)
    exchange("col", col, YY, lambda p: y_send.at[p], y_recv.at[col])
    under_way(YY, y_send.at[pl.ds(0, 15)], y_recv.at[pl.ds(0, 15)])
    y_recv[col] = y_send[col]

    arrived(GG)
    spectrum(g_recv)
    for slot in range(5):
        re, im = parts[slot]
        g_re, g_im = value(slot)
        f_re, f_im = fh[0, slot], fh[1, slot]
        pp[re] = (g_re * f_re + g_im * f_im).astype(BF16)
        pp[im] = (g_im * f_re - g_re * f_im).astype(BF16)
        s_re, s_im = sr[slot], si[slot]
        grad_re = (s_re * g_re + s_im * g_im) * (1.0 / SEQ)
        grad_im = (s_re * g_im - s_im * g_re) * (1.0 / SEQ)
        if slot < 4:
            fgr_ref[own_at + slot] = grad_re
            fgi_ref[own_at + slot] = grad_im
            gs_send[0, mirror_at(slot)] = grad_re.astype(BF16)
            gs_send[1, mirror_at(slot)] = grad_im.astype(BF16)
        else:
            gs_send[0, 0] = jnp.where(col == 0, grad_re, gs_send[0, 0].astype(F32)).astype(BF16)
            gs_send[1, 0] = jnp.where(col == 0, grad_im, gs_send[1, 0].astype(F32)).astype(BF16)
    restore(z_send)
    exchange("col", col, ZZ, lambda p: z_send.at[p], z_recv.at[col])
    under_way(ZZ, z_send.at[pl.ds(0, 15)], z_recv.at[pl.ds(0, 15)])
    z_recv[col] = z_send[col]
    def send_mirrored():
        back_to = jnp.where(low_half, jnp.where(col == 0, 8, 16 - col), partner)
        back_to = lax.rem(back_to, NP)
        for part in range(2):
            remote(gs_send.at[part, pl.ds(1, 3)], gm_recv.at[part, pl.ds(1, 3)], GM, {"col": partner}).start()
            remote(gs_send.at[part, 0], gm_recv.at[part, 0], GM, {"col": back_to}).start()
        under_way(GM, gs_send, gm_recv)

    def field_back(recv, dst):
        def body(rows):
            planes = swap_bits([recv[i, rows, :].astype(F32) for i in range(NP)], LOW4)
            flat = jnp.stack([p.astype(BF16) for p in planes]).reshape(NP * GR, 128)
            out = jnp.dot(flat, last_ref[...], preferred_element_type=F32)
            dst[:, rows, :] = out.astype(BF16).astype(F32).reshape(NP, GR, 128)

        over_groups(body)

    def send_home(make, dst):
        def body(rows):
            tiles = swap_bits([make(i, rows) for i in range(NP)], LOW4)
            for i in range(NP):
                dst[i, rows, :] = tiles[i].astype(BF16)

        over_groups(body)

    arrived(YY)
    field_back(y_recv, yp)
    send_home(lambda i, rows: sp[i, rows, :] * yp[i, rows, :], m_send)
    exchange("row", row, MR, lambda p: m_send.at[p], tile_of(m_recv, row))
    under_way(MR, m_send.at[pl.ds(0, 15)], m_recv.at[pl.ds(0, 15 * DL)])
    m_recv[own_rows, :] = m_send[row]

    send_mirrored()
    arrived(ZZ)
    field_back(z_recv, gp)

    def rounded(value):
        return value.astype(BF16).astype(F32)

    def stream_grads(rows):
        taps = [wb[q, rows, :] for q in range(9)]
        sums = [jnp.zeros((GR, 128), F32)] * 9
        before1 = before2 = None
        for i in range(NP):
            gs = gp[i, rows, :]
            grads = (
                rounded(gs * bp[i, rows, :]),
                rounded(gs * ap[i, rows, :]),
                rounded(cp[i, rows, :] * yp[i, rows, :]),
            )
            at_tap = [
                taps[3 * t] * grads[0] + taps[3 * t + 1] * grads[1] + taps[3 * t + 2] * grads[2]
                for t in range(3)
            ]
            past = [xp[i + 2 - t, rows, :] for t in range(3)]
            sums = [sums[q] + past[q // 3] * grads[q % 3] for q in range(9)]
            if i == 0:
                hg_send[0, rows, :] = at_tap[2].astype(BF16)
                first_one = at_tap[1]
            if i == 1:
                hg_send[1, rows, :] = (first_one + at_tap[2]).astype(BF16)
            if before2 is not None:
                gp[i - 2, rows, :] = before2 + at_tap[2]
            before2 = None if before1 is None else before1 + at_tap[1]
            before1 = at_tap[0]
        gp[14, rows, :] = before2
        gp[15, rows, :] = before1
        at = lax.broadcasted_iota(jnp.int32, (GR, 128), 1)
        total = jnp.zeros((GR, 128), F32)
        for q in range(9):
            total = jnp.where(at == q, jnp.sum(sums[q], axis=1, keepdims=True), total)
        wt[rows, :] = total[:, :16]

    over_groups(stream_grads)
    remote(hg_send, hg_recv, HG, {"col": lax.rem(col + NP - 1, NP)}).start()
    under_way(HG, hg_send, hg_recv)
    d1_send[...] = jnp.zeros_like(d1_send)
    terms = wt[:DL, :].T * (1.0 / math.sqrt(SEQ))
    d1_send[:, :DL] = terms[:8]
    d1_send[0:1, 64 : 64 + DL] = terms[8:9]
    exchange("col", col, D1, lambda p: d1_send, d1_recv.at[col])
    under_way(D1, d1_recv.at[pl.ds(0, 15)], d1_recv.at[pl.ds(0, 15)])
    d1_recv[col] = d1_send[...]

    arrived(HG)
    for i in range(2):
        halo = hg_recv[i].astype(F32)
        ahead = jnp.where(lane < 112, pltpu.roll(halo, 112, 1), pltpu.roll(halo, 111, 1))
        ahead = jnp.where(lane == 127, 0.0, ahead)
        gp[14 + i] = gp[14 + i] + jnp.where(col == NP - 1, ahead, halo)
    send_home(lambda i, rows: gp[i, rows, :], i_send)
    exchange("row", row, IR, lambda p: i_send.at[p], tile_of(i_recv, row))
    under_way(IR, i_send.at[pl.ds(0, 15)], i_recv.at[pl.ds(0, 15 * DL)])
    i_recv[own_rows, :] = i_send[row]

    arrived(D1)
    total = d1_recv[0]
    for i in range(1, NP):
        total = total + d1_recv[i]
    d2_send[...] = total
    exchange("row", row, D2, lambda p: d2_send, d2_recv.at[row])
    under_way(D2, d2_recv.at[pl.ds(0, 15)], d2_recv.at[pl.ds(0, 15)])
    d2_recv[row] = total

    def home(src, dst_ref):
        for i in range(6):
            block = src[128 * i : 128 * (i + 1), :].astype(F32).T
            dst_ref[:, :, 128 * i : 128 * (i + 1)] = block.astype(BF16).reshape(8, 16, 128)

    arrived(MR)
    home(m_recv, mixed_ref)
    store(mixed_ref, mixed_hbm)

    arrived(GM)
    rev[...] = jnp.dot(
        gm_recv[...].reshape(8 * DL, N2), reverse, preferred_element_type=F32
    ).reshape(2, 4, DL, N2)
    fgr_ref[extra_row] = rev[0, 0]
    fgi_ref[extra_row] = -rev[1, 0]
    for i in range(1, 4):
        fgr_ref[4 + i] = rev[0, i]
        fgi_ref[4 + i] = -rev[1, i]

    store(fgr_ref, fgr_hbm)
    store(fgi_ref, fgi_hbm)

    arrived(D2)
    spot = lax.broadcasted_iota(jnp.int32, (16, 128), 1)
    blocks = [jnp.zeros((16, 128), F32)] * 6
    for i in range(NP):
        block, off = divmod(DL * i, 128)
        packed = d2_recv[i]
        piece = jnp.concatenate([packed, pltpu.roll(packed, 64, 1)], 0)
        piece = jnp.where(spot < DL, piece, 0.0)
        piece = pltpu.roll(piece, off, 1) if off else piece
        if off + DL > 128:
            blocks[block] = blocks[block] + jnp.where(spot >= off, piece, 0.0)
            blocks[block + 1] = blocks[block + 1] + jnp.where(spot < off, piece, 0.0)
        else:
            blocks[block] = blocks[block] + piece
    for tap in range(3):
        for stream in range(3):
            q = 3 * tap + stream
            for i in range(6):
                at = 768 * stream + 128 * i
                dw_ref[tap : tap + 1, at : at + 128] = blocks[i][q : q + 1, :]
    store(dw_ref, dw_hbm)
    arrived(IR)
    home(i_recv, ig_ref)
    store(ig_ref, ig_hbm)
    for copy in stores:
        copy.wait()

    drain()


def finish(*refs):
    sources, results, held = refs[:5], refs[5:10], refs[10:15]
    load_sem, store_sem = refs[15:]
    loads = [pltpu.make_async_copy(sources[i], held[i], load_sem.at[i]) for i in range(5)]
    stores = [pltpu.make_async_copy(held[i], results[i], store_sem.at[i]) for i in range(5)]
    for load in loads:
        load.start()
    for load, copy in zip(loads, stores):
        load.wait()
        copy.start()
    for copy in stores:
        copy.wait()


def per_device(sequence, conv_weights, cotangent, filter_re, filter_im):
    first, last, second, fwd, inv = (jnp.asarray(t) for t in tables())
    vmem = pl.BlockSpec(memory_space=pltpu.VMEM)
    hbm = pl.BlockSpec(memory_space=pl.ANY)
    tiles = pltpu.VMEM((NP, DL, 128), BF16)
    planes = pltpu.VMEM((NP, DL, 128), F32)
    flat = pltpu.VMEM((NP * DL, 128), BF16)
    spec = pltpu.VMEM((2, 4, DL, N2), BF16)
    pair = pltpu.VMEM((2, DL, 128), BF16)
    small = pltpu.VMEM((NP, 8, 128), F32)
    one = pltpu.VMEM((8, 128), F32)
    shapes = (
        jax.ShapeDtypeStruct(sequence.shape, BF16),
        jax.ShapeDtypeStruct(sequence.shape, BF16),
        jax.ShapeDtypeStruct(filter_re.shape, F32),
        jax.ShapeDtypeStruct(filter_re.shape, F32),
        jax.ShapeDtypeStruct(conv_weights.shape, F32),
    )
    outs = pl.pallas_call(
        kernel,
        out_shape=shapes,
        in_specs=[hbm] * 10,
        out_specs=[hbm] * 5,
        scratch_shapes=[
            *(pltpu.VMEM(s.shape, s.dtype) for s in shapes),
            pltpu.VMEM(sequence.shape, BF16),
            pltpu.VMEM(conv_weights.shape, F32),
            pltpu.VMEM(sequence.shape, BF16),
            pltpu.VMEM((128, 128), BF16),
            pltpu.VMEM((128, 128), BF16),
            pltpu.VMEM((N2, 2 * N2), BF16),
            flat, flat, flat, flat,
            pltpu.VMEM((16, 768), F32),
            pltpu.VMEM((768, 16), F32),
            pltpu.VMEM((9, DL, 128), F32),
            pltpu.VMEM((2, 8, DL, N2), BF16),
            spec,
            pltpu.VMEM((2, 4, DL, N2), F32),
            pltpu.VMEM((2, 5, DL, N2), F32),
            pltpu.VMEM((2, 16, 128), F32),
            pltpu.VMEM((2, 8, N2), F32),
            pltpu.VMEM((NP + 2, DL, 128), F32),
            pair, pair,
            planes, planes, planes, planes, planes,
            tiles,
            tiles, tiles, tiles, tiles, tiles, tiles, tiles, tiles,
            pltpu.VMEM((10, DL, N2), BF16),
            pltpu.VMEM((10, DL, 2 * N2), F32),
            pltpu.VMEM((5, DL, N2), F32),
            pltpu.VMEM((5, DL, N2), F32),
            pltpu.VMEM((8, DL, N2), F32),
            spec, spec,
            planes,
            pair, pair,
            one, small, one, small,
            tiles, flat, tiles, flat,
            pltpu.SemaphoreType.DMA((14,)),
            pltpu.SemaphoreType.DMA((14,)),
            pltpu.SemaphoreType.DMA((15,)),
        ],
        compiler_params=pltpu.CompilerParams(
            collective_id=0, has_side_effects=True, vmem_limit_bytes=56 * 1024 * 1024
        ),
    )(
        sequence, conv_weights, cotangent, filter_re, filter_im,
        first, last, second, fwd, inv,
    )
    return pl.pallas_call(
        finish,
        out_shape=shapes,
        in_specs=[hbm] * 5,
        out_specs=[hbm] * 5,
        scratch_shapes=[
            *(pltpu.VMEM(s.shape, s.dtype) for s in shapes),
            pltpu.SemaphoreType.DMA((5,)),
            pltpu.SemaphoreType.DMA((5,)),
        ],
    )(*outs)


def solution(mesh):
    return jax.shard_map(
        per_device,
        mesh=mesh,
        in_specs=(
            P("row", "col", None),
            P(),
            P("row", "col", None),
            P("col", "row", None),
            P("col", "row", None),
        ),
        out_specs=(
            P("row", "col", None),
            P("row", "col", None),
            P("col", "row", None),
            P("col", "row", None),
            P(),
        ),
        check_vma=False,
    )
```

```python
import functools
import math

import jax
import jax.numpy as jnp
import ml_dtypes
import numpy as np
from jax import lax
from jax.experimental import pallas as pl
from jax.experimental.pallas import tpu as pltpu
from jax.sharding import PartitionSpec as P

MESH = pl.DeviceIdType.MESH
F32 = jnp.float32
BF16 = jnp.bfloat16

NP = 16
DL = 48
GR = 16
N1 = 128
N2 = 256
SEQ = N1 * N2

XR, CR, FM, HX, SS, GG, YY, ZZ, GM, HG, D1, MR, IR, D2 = range(14)


def slot_freq(col, slot):
    return 8 * col + slot + (1 if col >= 8 else 0)


def tables():
    lane_n1 = np.array([8 * (l % 16) + l // 16 for l in range(128)])
    first = np.zeros((128, 128))
    last = np.zeros((128, 128))
    for col in range(16):
        for slot in range(4):
            k1 = slot_freq(col, slot)
            turn = 2 * np.pi * (lane_n1 * k1 % 128) / 128
            re_row, im_row = slot * 16 + col, (slot + 4) * 16 + col
            if k1 == 0:
                first[:, re_row] = 1.0
                first[:, im_row] = np.cos(np.pi * lane_n1)
                last[re_row] = 1.0
                last[im_row] = np.cos(np.pi * lane_n1)
            else:
                first[:, re_row] = np.cos(turn)
                first[:, im_row] = -np.sin(turn)
                last[re_row] = np.cos(turn)
                last[im_row] = -np.sin(turn)
    last = last / SEQ
    idx = np.arange(N2)
    angle = 2 * np.pi * (idx[:, None] * idx[None, :] % N2) / N2
    second = np.concatenate([np.cos(angle), np.sin(angle)], 1)
    fwd = np.zeros((16, 2, 16, 128), np.float32)
    inv = np.zeros((16, 2, 8, N2), np.float32)
    low = np.arange(16)
    for col in range(16):
        for target in range(16):
            for slot in range(4):
                k1 = slot_freq(target, slot)
                turn = 2 * np.pi * (k1 * (16 * col + low) % SEQ) / SEQ
                re_l, im_l = slot * 16 + low, (slot + 4) * 16 + low
                fwd[col, 0, target, re_l] = np.cos(turn)
                fwd[col, 0, target, im_l] = np.cos(turn)
                fwd[col, 1, target, re_l] = np.sin(turn)
                fwd[col, 1, target, im_l] = -np.sin(turn)
        for slot in range(5):
            k1 = slot_freq(col, slot) if slot < 4 else 64
            turn = 2 * np.pi * (k1 * idx % SEQ) / SEQ
            inv[col, 0, slot] = np.cos(turn)
            inv[col, 1, slot] = np.sin(turn)
    return (
        first.astype(ml_dtypes.bfloat16),
        last.astype(ml_dtypes.bfloat16),
        second.astype(ml_dtypes.bfloat16),
        fwd,
        inv,
    )


def swap_bits(planes, pairs):
    lane = lax.broadcasted_iota(jnp.int32, planes[0].shape, 1)
    planes = list(planes)
    for plane_bit, lane_bit in pairs:
        shift = 1 << lane_bit
        upper = (lane & shift) != 0
        for i in range(len(planes)):
            if i & (1 << plane_bit):
                continue
            j = i | (1 << plane_bit)
            low, high = planes[i], planes[j]
            planes[i] = jnp.where(upper, pltpu.roll(high, shift, 1), low)
            planes[j] = jnp.where(upper, high, pltpu.roll(low, 128 - shift, 1))
    return planes


LOW4 = ((0, 0), (1, 1), (2, 2), (3, 3))
HIGH3 = ((0, 4), (1, 5), (2, 6))


def kernel(
    x_hbm, w_hbm, cot_hbm, fr_ref, fi_ref, first_hbm, last_hbm, second_hbm, fwd_ref, inv_ref,
    mixed_hbm, ig_hbm, fgr_hbm, fgi_hbm, dw_hbm,
    mixed_ref, ig_ref, fgr_ref, fgi_ref, dw_ref,
    x_ref, w_ref, cot_ref, first_ref, last_ref, second_ref,
    xt, xrecv, ct, crecv, w9, wt, wb, fo, fm, rev, fh, tf, ti,
    xp, hx_send, hx_recv, cp, ap, bp, sp, yp, fld,
    s_send, s_recv, g_send, g_recv, y_send, y_recv, z_send, z_recv,
    pp, uu, sr, si, qq, gs_send, gm_recv, gp, hg_send, hg_recv,
    d1_send, d1_recv, d2_send, d2_recv, m_send, m_recv, i_send, i_recv,
    send_sem, recv_sem, local_sem,
):
    row = lax.axis_index("row")
    col = lax.axis_index("col")
    low_half = col < 8

    def remote(src, dst, which, target):
        return pltpu.make_async_remote_copy(
            src_ref=src,
            dst_ref=dst,
            send_sem=send_sem.at[which],
            recv_sem=recv_sem.at[which],
            device_id=target,
            device_id_type=MESH,
        )

    def exchange(axis, me, which, src_at, dst):
        def body(step, carry):
            peer = lax.rem(me + step, NP)
            remote(src_at(peer), dst, which, {axis: peer}).start()
            return carry

        lax.fori_loop(1, NP, body, 0)

    def wait_bytes(ref, sem):
        pltpu.make_async_copy(ref, ref, sem).wait()

    leaving, arriving = {}, {}
    stores = []

    def store(src, dst):
        stores.append(pltpu.make_async_copy(src, dst, local_sem.at[10 + len(stores)]))
        stores[-1].start()

    def under_way(which, sent, received):
        leaving[which], arriving[which] = sent, received

    def arrived(which):
        wait_bytes(arriving.pop(which), recv_sem.at[which])

    def drain():
        for which in list(arriving):
            arrived(which)
        for which, ref in leaving.items():
            wait_bytes(ref, send_sem.at[which])

    def tile_of(ref, peer):
        return ref.at[pl.ds(pl.multiple_of(peer * DL, DL), DL)]

    def over_groups(body):
        def step(g, carry):
            body(pl.ds(pl.multiple_of(g * GR, GR), GR))
            return carry

        lax.fori_loop(0, DL // GR, step, 0, unroll=True)

    x_load = pltpu.make_async_copy(x_hbm, x_ref, local_sem.at[4])
    cot_load = pltpu.make_async_copy(cot_hbm, cot_ref, local_sem.at[5])
    w_load = pltpu.make_async_copy(w_hbm, w_ref, local_sem.at[6])
    x_load.start()
    cot_load.start()
    w_load.start()
    loads = [
        pltpu.make_async_copy(first_hbm, first_ref, local_sem.at[7]),
        pltpu.make_async_copy(second_hbm, second_ref, local_sem.at[8]),
        pltpu.make_async_copy(last_hbm, last_ref, local_sem.at[9]),
        pltpu.make_async_copy(fr_ref, fo.at[0], local_sem.at[0]),
        pltpu.make_async_copy(fi_ref, fo.at[1], local_sem.at[1]),
        pltpu.make_async_copy(fwd_ref.at[col], tf, local_sem.at[2]),
        pltpu.make_async_copy(inv_ref.at[col], ti, local_sem.at[3]),
    ]
    for load in loads:
        load.start()

    barrier = pltpu.get_barrier_semaphore()

    def greet(step, carry):
        pl.semaphore_signal(
            barrier, inc=1, device_id={"row": lax.rem(row + step, NP)}, device_id_type=MESH
        )
        pl.semaphore_signal(
            barrier, inc=1, device_id={"col": lax.rem(col + step, NP)}, device_id_type=MESH
        )
        return carry

    lax.fori_loop(1, NP, greet, 0)

    def turn_home(src_ref, dst):
        for i in range(6):
            block = src_ref[:, :, 128 * i : 128 * (i + 1)].reshape(128, 128).astype(F32)
            dst[128 * i : 128 * (i + 1), :] = block.T.astype(BF16)

    x_load.wait()
    turn_home(x_ref, xt)
    pl.semaphore_wait(barrier, 2 * (NP - 1))

    partner = 15 - col
    extra_row = jnp.where(low_half, 4, 0)
    extra_to = jnp.where(low_half, partner, lax.rem(16 - col, 8))
    for part, ref in enumerate((fr_ref, fi_ref)):
        remote(ref.at[pl.ds(5, 3)], fm.at[part, pl.ds(1, 3)], FM, {"col": partner}).start()
        remote(ref.at[extra_row], fm.at[part, 0], FM, {"col": extra_to}).start()
    under_way(FM, fm, fm)

    exchange("row", row, XR, lambda p: tile_of(xt, p), tile_of(xrecv, row))
    under_way(XR, xt.at[pl.ds(0, 15 * DL)], xrecv.at[pl.ds(0, 15 * DL)])
    own_rows = pl.ds(pl.multiple_of(row * DL, DL), DL)
    xrecv[own_rows, :] = xt[own_rows, :]
    cot_load.wait()
    turn_home(cot_ref, ct)
    exchange("row", row, CR, lambda p: tile_of(ct, p), tile_of(crecv, row))
    under_way(CR, ct.at[pl.ds(0, 15 * DL)], crecv.at[pl.ds(0, 15 * DL)])
    crecv[own_rows, :] = ct[own_rows, :]

    w_load.wait()
    w9[...] = jnp.zeros_like(w9)
    for tap in range(3):
        for stream in range(3):
            q = 3 * tap + stream
            w9[q : q + 1, :] = w_ref[tap : tap + 1, 768 * stream : 768 * (stream + 1)]
    for i in range(6):
        wt[128 * i : 128 * (i + 1), :] = w9[:, 128 * i : 128 * (i + 1)].T
    columns = wt[own_rows, :]
    for q in range(9):
        wb[q] = jnp.broadcast_to(columns[:, q : q + 1], (DL, 128))
    for load in loads:
        load.wait()

    lane = lax.broadcasted_iota(jnp.int32, (DL, 128), 1)

    def planes_in(recv, dst, base):
        def body(rows):
            planes = [recv[i, rows, :].astype(F32) for i in range(NP)]
            planes = swap_bits(planes, LOW4)
            for i in range(NP):
                dst[base + i, rows, :] = planes[i]

        over_groups(body)

    def tiles_out(src, dst, table):
        def body(rows):
            flat = src[:, rows, :].reshape(NP * GR, 128)
            out = jnp.dot(flat, first_ref[...], preferred_element_type=F32).reshape(NP, GR, 128)
            tiles = swap_bits([out[i] for i in range(NP)], LOW4)
            for i in range(NP):
                turned = tiles[i] * tf[0, i : i + 1, :] + pltpu.roll(tiles[i], 64, 1) * tf[1, i : i + 1, :]
                dst[i, rows, :] = turned.astype(BF16)

        over_groups(body)

    arrived(XR)
    x3 = xrecv.reshape(NP, DL, 128)
    planes_in(x3, xp, 2)
    hx_send[0] = xp[16].astype(BF16)
    hx_send[1] = xp[17].astype(BF16)
    remote(hx_send, hx_recv, HX, {"col": lax.rem(col + 1, NP)}).start()
    under_way(HX, hx_send, hx_recv)

    def streams(first, last):
        def body(rows):
            taps = [wb[q, rows, :] for q in range(9)]
            behind2, behind1 = xp[first, rows, :], xp[first + 1, rows, :]
            for i in range(first, last):
                now = xp[i + 2, rows, :]
                z = [taps[j] * now + taps[3 + j] * behind1 + taps[6 + j] * behind2 for j in range(3)]
                ap[i, rows, :] = z[0]
                bp[i, rows, :] = z[1]
                sp[i, rows, :] = z[2]
                fld[i, rows, :] = (z[0] * z[1]).astype(BF16)
                behind2, behind1 = behind1, now

        return body

    over_groups(streams(2, NP))
    arrived(CR)
    planes_in(crecv.reshape(NP, DL, 128), cp, 0)
    arrived(HX)
    for i in range(2):
        halo = hx_recv[i].astype(F32)
        back = jnp.where(lane >= 16, pltpu.roll(halo, 16, 1), pltpu.roll(halo, 17, 1))
        back = jnp.where(lane == 0, 0.0, back)
        xp[i] = jnp.where(col == 0, back, halo)

    over_groups(streams(0, 2))
    tiles_out(fld, s_send, tf)
    exchange("col", col, SS, lambda p: s_send.at[p], s_recv.at[col])
    under_way(SS, s_send.at[pl.ds(0, 15)], s_recv.at[pl.ds(0, 15)])
    s_recv[col] = s_send[col]

    def gate_grad(rows):
        for i in range(NP):
            fld[i, rows, :] = (cp[i, rows, :] * sp[i, rows, :]).astype(BF16)

    over_groups(gate_grad)
    tiles_out(fld, g_send, tf)
    exchange("col", col, GG, lambda p: g_send.at[p], g_recv.at[col])
    under_way(GG, g_send.at[pl.ds(0, 15)], g_recv.at[pl.ds(0, 15)])
    g_recv[col] = g_send[col]

    arrived(FM)
    at_row = lax.broadcasted_iota(jnp.int32, (N2, N2), 0)
    at_col = lax.broadcasted_iota(jnp.int32, (N2, N2), 1)
    reverse = jnp.where(at_row + at_col == N2 - 1, 1.0, 0.0).astype(BF16)
    rev[...] = jnp.dot(
        fm[...].reshape(8 * DL, N2), reverse, preferred_element_type=F32
    ).reshape(2, 4, DL, N2)

    def mirror_at(slot):
        return jnp.where(low_half, (4 - slot) % 4, 3 - slot)

    own_at = jnp.where(low_half, 0, 1)
    for slot in range(4):
        rev_re = rev[0, mirror_at(slot)]
        rev_im = -rev[1, mirror_at(slot)]
        if slot == 0:
            fh[0, 4] = rev_re
            fh[1, 4] = rev_im
            rev_re = jnp.where(col == 0, 0.0, rev_re)
            rev_im = jnp.where(col == 0, 0.0, rev_im)
        fh[0, slot] = fo[0, own_at + slot].astype(F32) + rev_re
        fh[1, slot] = fo[1, own_at + slot].astype(F32) + rev_im

    parts = [(0, 4), (1, 5), (2, 6), (3, 7), (8, 9)]

    def spectrum(recv):
        def body(rows):
            planes = swap_bits([recv[i, rows, :].astype(F32) for i in range(NP)], HIGH3)
            for i in range(NP):
                half = i // 8
                pp[i % 8, rows, 128 * half : 128 * (half + 1)] = planes[i].astype(BF16)

        over_groups(body)
        middle = pp[4].astype(F32)
        pp[8] = (middle * ti[0, 4:5, :]).astype(BF16)
        pp[9] = (-middle * ti[1, 4:5, :]).astype(BF16)
        pp[4] = jnp.where(col == 0, 0.0, middle).astype(BF16)
        uu[...] = jnp.dot(
            pp[...].reshape(10 * DL, N2), second_ref[...], preferred_element_type=F32
        ).reshape(10, DL, 2 * N2)

    def value(slot):
        re, im = parts[slot]
        return (
            uu[re, :, :N2] + uu[im, :, N2:],
            uu[im, :, :N2] - uu[re, :, N2:],
        )

    def restore(dst):
        uu[...] = jnp.dot(
            pp[...].reshape(10 * DL, N2), second_ref[...], preferred_element_type=F32
        ).reshape(10, DL, 2 * N2)
        for slot in range(4):
            re, im = parts[slot]
            z_re = uu[re, :, :N2] - uu[im, :, N2:]
            z_im = uu[im, :, :N2] + uu[re, :, N2:]
            cos, sin = ti[0, slot : slot + 1, :], ti[1, slot : slot + 1, :]
            qq[slot] = z_re * cos - z_im * sin
            q_im = z_im * cos + z_re * sin
            if slot == 0:
                re4, im4 = parts[4]
                z_re4 = uu[re4, :, :N2] - uu[im4, :, N2:]
                z_im4 = uu[im4, :, :N2] + uu[re4, :, N2:]
                q_im = jnp.where(col == 0, z_re4 * ti[0, 4:5, :] - z_im4 * ti[1, 4:5, :], q_im)
            qq[4 + slot] = q_im

        def body(rows):
            planes = [
                qq[i % 8, rows, 128 * (i // 8) : 128 * (i // 8 + 1)] for i in range(NP)
            ]
            planes = swap_bits(planes, HIGH3)
            for i in range(NP):
                dst[i, rows, :] = planes[i].astype(BF16)

        over_groups(body)

    arrived(SS)
    spectrum(s_recv)
    for slot in range(5):
        re, im = parts[slot]
        s_re, s_im = value(slot)
        sr[slot] = s_re
        si[slot] = s_im
        f_re, f_im = fh[0, slot], fh[1, slot]
        pp[re] = (s_re * f_re - s_im * f_im).astype(BF16)
        pp[im] = (s_re * f_im + s_im * f_re).astype(BF16)
    restore(y_send)
    exchange("col", col, YY, lambda p: y_send.at[p], y_recv.at[col])
    under_way(YY, y_send.at[pl.ds(0, 15)], y_recv.at[pl.ds(0, 15)])
    y_recv[col] = y_send[col]

    arrived(GG)
    spectrum(g_recv)
    for slot in range(5):
        re, im = parts[slot]
        g_re, g_im = value(slot)
        f_re, f_im = fh[0, slot], fh[1, slot]
        pp[re] = (g_re * f_re + g_im * f_im).astype(BF16)
        pp[im] = (g_im * f_re - g_re * f_im).astype(BF16)
        s_re, s_im = sr[slot], si[slot]
        grad_re = (s_re * g_re + s_im * g_im) * (1.0 / SEQ)
        grad_im = (s_re * g_im - s_im * g_re) * (1.0 / SEQ)
        if slot < 4:
            fgr_ref[own_at + slot] = grad_re
            fgi_ref[own_at + slot] = grad_im
            gs_send[0, mirror_at(slot)] = grad_re.astype(BF16)
            gs_send[1, mirror_at(slot)] = grad_im.astype(BF16)
        else:
            gs_send[0, 0] = jnp.where(col == 0, grad_re, gs_send[0, 0].astype(F32)).astype(BF16)
            gs_send[1, 0] = jnp.where(col == 0, grad_im, gs_send[1, 0].astype(F32)).astype(BF16)
    restore(z_send)
    exchange("col", col, ZZ, lambda p: z_send.at[p], z_recv.at[col])
    under_way(ZZ, z_send.at[pl.ds(0, 15)], z_recv.at[pl.ds(0, 15)])
    z_recv[col] = z_send[col]
    def send_mirrored():
        back_to = jnp.where(low_half, jnp.where(col == 0, 8, 16 - col), partner)
        back_to = lax.rem(back_to, NP)
        for part in range(2):
            remote(gs_send.at[part, pl.ds(1, 3)], gm_recv.at[part, pl.ds(1, 3)], GM, {"col": partner}).start()
            remote(gs_send.at[part, 0], gm_recv.at[part, 0], GM, {"col": back_to}).start()
        under_way(GM, gs_send, gm_recv)

    def field_back(recv, dst):
        def body(rows):
            planes = swap_bits([recv[i, rows, :].astype(F32) for i in range(NP)], LOW4)
            flat = jnp.stack([p.astype(BF16) for p in planes]).reshape(NP * GR, 128)
            out = jnp.dot(flat, last_ref[...], preferred_element_type=F32)
            dst[:, rows, :] = out.astype(BF16).astype(F32).reshape(NP, GR, 128)

        over_groups(body)

    def send_home(make, dst):
        def body(rows):
            tiles = swap_bits([make(i, rows) for i in range(NP)], LOW4)
            for i in range(NP):
                dst[i, rows, :] = tiles[i].astype(BF16)

        over_groups(body)

    arrived(YY)
    field_back(y_recv, yp)
    send_home(lambda i, rows: sp[i, rows, :] * yp[i, rows, :], m_send)
    exchange("row", row, MR, lambda p: m_send.at[p], tile_of(m_recv, row))
    under_way(MR, m_send.at[pl.ds(0, 15)], m_recv.at[pl.ds(0, 15 * DL)])
    m_recv[own_rows, :] = m_send[row]

    send_mirrored()
    arrived(ZZ)
    field_back(z_recv, gp)

    def rounded(value):
        return value.astype(BF16).astype(F32)

    def stream_grads(rows):
        taps = [wb[q, rows, :] for q in range(9)]
        sums = [jnp.zeros((GR, 128), F32)] * 9
        before1 = before2 = None
        for i in range(NP):
            gs = gp[i, rows, :]
            grads = (
                rounded(gs * bp[i, rows, :]),
                rounded(gs * ap[i, rows, :]),
                rounded(cp[i, rows, :] * yp[i, rows, :]),
            )
            at_tap = [
                taps[3 * t] * grads[0] + taps[3 * t + 1] * grads[1] + taps[3 * t + 2] * grads[2]
                for t in range(3)
            ]
            past = [xp[i + 2 - t, rows, :] for t in range(3)]
            sums = [sums[q] + past[q // 3] * grads[q % 3] for q in range(9)]
            if i == 0:
                hg_send[0, rows, :] = at_tap[2].astype(BF16)
                first_one = at_tap[1]
            if i == 1:
                hg_send[1, rows, :] = (first_one + at_tap[2]).astype(BF16)
            if before2 is not None:
                gp[i - 2, rows, :] = before2 + at_tap[2]
            before2 = None if before1 is None else before1 + at_tap[1]
            before1 = at_tap[0]
        gp[14, rows, :] = before2
        gp[15, rows, :] = before1
        at = lax.broadcasted_iota(jnp.int32, (GR, 128), 1)
        total = jnp.zeros((GR, 128), F32)
        for q in range(9):
            total = jnp.where(at == q, jnp.sum(sums[q], axis=1, keepdims=True), total)
        wt[rows, :] = total[:, :16]

    over_groups(stream_grads)
    remote(hg_send, hg_recv, HG, {"col": lax.rem(col + NP - 1, NP)}).start()
    under_way(HG, hg_send, hg_recv)
    d1_send[...] = jnp.zeros_like(d1_send)
    terms = wt[:DL, :].T * (1.0 / math.sqrt(SEQ))
    d1_send[:, :DL] = terms[:8]
    d1_send[0:1, 64 : 64 + DL] = terms[8:9]
    exchange("col", col, D1, lambda p: d1_send, d1_recv.at[col])
    under_way(D1, d1_recv.at[pl.ds(0, 15)], d1_recv.at[pl.ds(0, 15)])
    d1_recv[col] = d1_send[...]

    arrived(HG)
    for i in range(2):
        halo = hg_recv[i].astype(F32)
        ahead = jnp.where(lane < 112, pltpu.roll(halo, 112, 1), pltpu.roll(halo, 111, 1))
        ahead = jnp.where(lane == 127, 0.0, ahead)
        gp[14 + i] = gp[14 + i] + jnp.where(col == NP - 1, ahead, halo)
    send_home(lambda i, rows: gp[i, rows, :], i_send)
    exchange("row", row, IR, lambda p: i_send.at[p], tile_of(i_recv, row))
    under_way(IR, i_send.at[pl.ds(0, 15)], i_recv.at[pl.ds(0, 15 * DL)])
    i_recv[own_rows, :] = i_send[row]

    arrived(D1)
    total = d1_recv[0]
    for i in range(1, NP):
        total = total + d1_recv[i]
    d2_send[...] = total
    exchange("row", row, D2, lambda p: d2_send, d2_recv.at[row])
    under_way(D2, d2_recv.at[pl.ds(0, 15)], d2_recv.at[pl.ds(0, 15)])
    d2_recv[row] = total

    def home(src, dst_ref):
        for i in range(6):
            block = src[128 * i : 128 * (i + 1), :].astype(F32).T
            dst_ref[:, :, 128 * i : 128 * (i + 1)] = block.astype(BF16).reshape(8, 16, 128)

    arrived(MR)
    home(m_recv, mixed_ref)
    store(mixed_ref, mixed_hbm)

    arrived(GM)
    rev[...] = jnp.dot(
        gm_recv[...].reshape(8 * DL, N2), reverse, preferred_element_type=F32
    ).reshape(2, 4, DL, N2)
    fgr_ref[extra_row] = rev[0, 0]
    fgi_ref[extra_row] = -rev[1, 0]
    for i in range(1, 4):
        fgr_ref[4 + i] = rev[0, i]
        fgi_ref[4 + i] = -rev[1, i]

    store(fgr_ref, fgr_hbm)
    store(fgi_ref, fgi_hbm)

    arrived(D2)
    spot = lax.broadcasted_iota(jnp.int32, (16, 128), 1)
    blocks = [jnp.zeros((16, 128), F32)] * 6
    for i in range(NP):
        block, off = divmod(DL * i, 128)
        packed = d2_recv[i]
        piece = jnp.concatenate([packed, pltpu.roll(packed, 64, 1)], 0)
        piece = jnp.where(spot < DL, piece, 0.0)
        piece = pltpu.roll(piece, off, 1) if off else piece
        if off + DL > 128:
            blocks[block] = blocks[block] + jnp.where(spot >= off, piece, 0.0)
            blocks[block + 1] = blocks[block + 1] + jnp.where(spot < off, piece, 0.0)
        else:
            blocks[block] = blocks[block] + piece
    for tap in range(3):
        for stream in range(3):
            q = 3 * tap + stream
            for i in range(6):
                at = 768 * stream + 128 * i
                dw_ref[tap : tap + 1, at : at + 128] = blocks[i][q : q + 1, :]
    store(dw_ref, dw_hbm)
    arrived(IR)
    home(i_recv, ig_ref)
    store(ig_ref, ig_hbm)
    for copy in stores:
        copy.wait()

    drain()


def finish(*refs):
    sources, results, held = refs[:5], refs[5:10], refs[10:15]
    load_sem, store_sem = refs[15:]
    loads = [pltpu.make_async_copy(sources[i], held[i], load_sem.at[i]) for i in range(5)]
    stores = [pltpu.make_async_copy(held[i], results[i], store_sem.at[i]) for i in range(5)]
    for load in loads:
        load.start()
    for load, copy in zip(loads, stores):
        load.wait()
        copy.start()
    for copy in stores:
        copy.wait()


def per_device(sequence, conv_weights, cotangent, filter_re, filter_im):
    first, last, second, fwd, inv = (jnp.asarray(t) for t in tables())
    vmem = pl.BlockSpec(memory_space=pltpu.VMEM)
    hbm = pl.BlockSpec(memory_space=pl.ANY)
    tiles = pltpu.VMEM((NP, DL, 128), BF16)
    planes = pltpu.VMEM((NP, DL, 128), F32)
    flat = pltpu.VMEM((NP * DL, 128), BF16)
    spec = pltpu.VMEM((2, 4, DL, N2), BF16)
    pair = pltpu.VMEM((2, DL, 128), BF16)
    small = pltpu.VMEM((NP, 8, 128), F32)
    one = pltpu.VMEM((8, 128), F32)
    shapes = (
        jax.ShapeDtypeStruct(sequence.shape, BF16),
        jax.ShapeDtypeStruct(sequence.shape, BF16),
        jax.ShapeDtypeStruct(filter_re.shape, F32),
        jax.ShapeDtypeStruct(filter_re.shape, F32),
        jax.ShapeDtypeStruct(conv_weights.shape, F32),
    )
    outs = pl.pallas_call(
        kernel,
        out_shape=shapes,
        in_specs=[hbm] * 10,
        out_specs=[hbm] * 5,
        scratch_shapes=[
            *(pltpu.VMEM(s.shape, s.dtype) for s in shapes),
            pltpu.VMEM(sequence.shape, BF16),
            pltpu.VMEM(conv_weights.shape, F32),
            pltpu.VMEM(sequence.shape, BF16),
            pltpu.VMEM((128, 128), BF16),
            pltpu.VMEM((128, 128), BF16),
            pltpu.VMEM((N2, 2 * N2), BF16),
            flat, flat, flat, flat,
            pltpu.VMEM((16, 768), F32),
            pltpu.VMEM((768, 16), F32),
            pltpu.VMEM((9, DL, 128), F32),
            pltpu.VMEM((2, 8, DL, N2), BF16),
            spec,
            pltpu.VMEM((2, 4, DL, N2), F32),
            pltpu.VMEM((2, 5, DL, N2), F32),
            pltpu.VMEM((2, 16, 128), F32),
            pltpu.VMEM((2, 8, N2), F32),
            pltpu.VMEM((NP + 2, DL, 128), F32),
            pair, pair,
            planes, planes, planes, planes, planes,
            tiles,
            tiles, tiles, tiles, tiles, tiles, tiles, tiles, tiles,
            pltpu.VMEM((10, DL, N2), BF16),
            pltpu.VMEM((10, DL, 2 * N2), F32),
            pltpu.VMEM((5, DL, N2), F32),
            pltpu.VMEM((5, DL, N2), F32),
            pltpu.VMEM((8, DL, N2), F32),
            spec, spec,
            planes,
            pair, pair,
            one, small, one, small,
            tiles, flat, tiles, flat,
            pltpu.SemaphoreType.DMA((14,)),
            pltpu.SemaphoreType.DMA((14,)),
            pltpu.SemaphoreType.DMA((15,)),
        ],
        compiler_params=pltpu.CompilerParams(
            collective_id=0, has_side_effects=True, vmem_limit_bytes=56 * 1024 * 1024
        ),
    )(
        sequence, conv_weights, cotangent, filter_re, filter_im,
        first, last, second, fwd, inv,
    )
    return pl.pallas_call(
        finish,
        out_shape=shapes,
        in_specs=[hbm] * 5,
        out_specs=[hbm] * 5,
        scratch_shapes=[
            *(pltpu.VMEM(s.shape, s.dtype) for s in shapes),
            pltpu.SemaphoreType.DMA((5,)),
            pltpu.SemaphoreType.DMA((5,)),
        ],
    )(*outs)


def solution(mesh):
    return jax.shard_map(
        per_device,
        mesh=mesh,
        in_specs=(
            P("row", "col", None),
            P(),
            P("row", "col", None),
            P("col", "row", None),
            P("col", "row", None),
        ),
        out_specs=(
            P("row", "col", None),
            P("row", "col", None),
            P("col", "row", None),
            P("col", "row", None),
            P(),
        ),
        check_vma=False,
    )
```

```python
import functools
import math

import jax
import jax.numpy as jnp
import ml_dtypes
import numpy as np
from jax import lax
from jax.experimental import pallas as pl
from jax.experimental.pallas import tpu as pltpu
from jax.sharding import PartitionSpec as P

MESH = pl.DeviceIdType.MESH
F32 = jnp.float32
BF16 = jnp.bfloat16

NP = 16
DL = 48
GR = 16
N1 = 128
N2 = 256
SEQ = N1 * N2

XR, CR, FM, HX, SS, GG, YY, ZZ, GM, HG, D1, MR, IR, D2 = range(14)


def slot_freq(col, slot):
    return 8 * col + slot + (1 if col >= 8 else 0)


def tables():
    lane_n1 = np.array([8 * (l % 16) + l // 16 for l in range(128)])
    first = np.zeros((128, 128))
    last = np.zeros((128, 128))
    for col in range(16):
        for slot in range(4):
            k1 = slot_freq(col, slot)
            turn = 2 * np.pi * (lane_n1 * k1 % 128) / 128
            re_row, im_row = slot * 16 + col, (slot + 4) * 16 + col
            if k1 == 0:
                first[:, re_row] = 1.0
                first[:, im_row] = np.cos(np.pi * lane_n1)
                last[re_row] = 1.0
                last[im_row] = np.cos(np.pi * lane_n1)
            else:
                first[:, re_row] = np.cos(turn)
                first[:, im_row] = -np.sin(turn)
                last[re_row] = np.cos(turn)
                last[im_row] = -np.sin(turn)
    last = last / SEQ
    idx = np.arange(N2)
    angle = 2 * np.pi * (idx[:, None] * idx[None, :] % N2) / N2
    second = np.concatenate([np.cos(angle), np.sin(angle)], 1)
    fwd = np.zeros((16, 2, 16, 128), np.float32)
    inv = np.zeros((16, 2, 8, N2), np.float32)
    low = np.arange(16)
    for col in range(16):
        for target in range(16):
            for slot in range(4):
                k1 = slot_freq(target, slot)
                turn = 2 * np.pi * (k1 * (16 * col + low) % SEQ) / SEQ
                re_l, im_l = slot * 16 + low, (slot + 4) * 16 + low
                fwd[col, 0, target, re_l] = np.cos(turn)
                fwd[col, 0, target, im_l] = np.cos(turn)
                fwd[col, 1, target, re_l] = np.sin(turn)
                fwd[col, 1, target, im_l] = -np.sin(turn)
        for slot in range(5):
            k1 = slot_freq(col, slot) if slot < 4 else 64
            turn = 2 * np.pi * (k1 * idx % SEQ) / SEQ
            inv[col, 0, slot] = np.cos(turn)
            inv[col, 1, slot] = np.sin(turn)
    return (
        first.astype(ml_dtypes.bfloat16),
        last.astype(ml_dtypes.bfloat16),
        second.astype(ml_dtypes.bfloat16),
        fwd,
        inv,
    )


def swap_bits(planes, pairs):
    lane = lax.broadcasted_iota(jnp.int32, planes[0].shape, 1)
    planes = list(planes)
    for plane_bit, lane_bit in pairs:
        shift = 1 << lane_bit
        upper = (lane & shift) != 0
        for i in range(len(planes)):
            if i & (1 << plane_bit):
                continue
            j = i | (1 << plane_bit)
            low, high = planes[i], planes[j]
            planes[i] = jnp.where(upper, pltpu.roll(high, shift, 1), low)
            planes[j] = jnp.where(upper, high, pltpu.roll(low, 128 - shift, 1))
    return planes


LOW4 = ((0, 0), (1, 1), (2, 2), (3, 3))
HIGH3 = ((0, 4), (1, 5), (2, 6))


def home(src, dst_ref):
    for i in range(6):
        block = src[128 * i : 128 * (i + 1), :].astype(F32).T
        dst_ref[:, :, 128 * i : 128 * (i + 1)] = block.astype(BF16).reshape(8, 16, 128)


def kernel(
    x_hbm, w_hbm, cot_hbm, fr_ref, fi_ref, first_hbm, last_hbm, second_hbm, fwd_ref, inv_ref,
    mixed_hbm, i_recv, fgr_hbm, fgi_hbm, d2_recv,
    mixed_ref, fgr_ref, fgi_ref,
    x_ref, w_ref, cot_ref, first_ref, last_ref, second_ref,
    xt, xrecv, ct, crecv, w9, wt, wb, fo, fm, rev, fh, tf, ti,
    xp, hx_send, hx_recv, cp, ap, bp, sp, yp, fld,
    s_send, s_recv, g_send, g_recv, y_send, y_recv, z_send, z_recv,
    pp, sr, si, qq, gs_send, gm_recv, gp, third, edge, late, hg_send, hg_recv,
    d1_send, d1_recv, d2_send, m_send, m_recv, i_send,
    send_sem, recv_sem, local_sem,
):
    row = lax.axis_index("row")
    col = lax.axis_index("col")
    low_half = col < 8

    def remote(src, dst, which, target):
        return pltpu.make_async_remote_copy(
            src_ref=src,
            dst_ref=dst,
            send_sem=send_sem.at[which],
            recv_sem=recv_sem.at[which],
            device_id=target,
            device_id_type=MESH,
        )

    def exchange(axis, me, which, src_at, dst):
        def body(step, carry):
            peer = lax.rem(me + step, NP)
            remote(src_at(peer), dst, which, {axis: peer}).start()
            return carry

        lax.fori_loop(1, NP, body, 0)

    def wait_bytes(ref, sem):
        pltpu.make_async_copy(ref, ref, sem).wait()

    leaving, arriving = {}, {}
    stores = []

    def store(src, dst):
        stores.append(pltpu.make_async_copy(src, dst, local_sem.at[10 + len(stores)]))
        stores[-1].start()

    def under_way(which, sent, received):
        leaving[which], arriving[which] = sent, received

    def arrived(which):
        wait_bytes(arriving.pop(which), recv_sem.at[which])

    def drain():
        for which in list(arriving):
            arrived(which)
        for which, ref in leaving.items():
            wait_bytes(ref, send_sem.at[which])

    def tile_of(ref, peer):
        return ref.at[pl.ds(pl.multiple_of(peer * DL, DL), DL)]

    def over_groups(body):
        def step(g, carry):
            body(pl.ds(pl.multiple_of(g * GR, GR), GR))
            return carry

        lax.fori_loop(0, DL // GR, step, 0, unroll=True)

    x_load = pltpu.make_async_copy(x_hbm, x_ref, local_sem.at[4])
    cot_load = pltpu.make_async_copy(cot_hbm, cot_ref, local_sem.at[5])
    w_load = pltpu.make_async_copy(w_hbm, w_ref, local_sem.at[6])
    x_load.start()
    cot_load.start()
    w_load.start()
    loads = [
        pltpu.make_async_copy(first_hbm, first_ref, local_sem.at[7]),
        pltpu.make_async_copy(second_hbm, second_ref, local_sem.at[8]),
        pltpu.make_async_copy(last_hbm, last_ref, local_sem.at[9]),
        pltpu.make_async_copy(fr_ref, fo.at[0], local_sem.at[0]),
        pltpu.make_async_copy(fi_ref, fo.at[1], local_sem.at[1]),
        pltpu.make_async_copy(fwd_ref.at[col], tf, local_sem.at[2]),
        pltpu.make_async_copy(inv_ref.at[col], ti, local_sem.at[3]),
    ]
    for load in loads:
        load.start()

    barrier = pltpu.get_barrier_semaphore()

    def greet(step, carry):
        pl.semaphore_signal(
            barrier, inc=1, device_id={"row": lax.rem(row + step, NP)}, device_id_type=MESH
        )
        pl.semaphore_signal(
            barrier, inc=1, device_id={"col": lax.rem(col + step, NP)}, device_id_type=MESH
        )
        return carry

    lax.fori_loop(1, NP, greet, 0)

    def turn_home(src_ref, dst):
        for i in range(6):
            block = src_ref[:, :, 128 * i : 128 * (i + 1)].reshape(128, 128).astype(F32)
            dst[128 * i : 128 * (i + 1), :] = block.T.astype(BF16)

    x_load.wait()
    turn_home(x_ref, xt)
    pl.semaphore_wait(barrier, 2 * (NP - 1))

    partner = 15 - col
    extra_row = jnp.where(low_half, 4, 0)
    extra_to = jnp.where(low_half, partner, lax.rem(16 - col, 8))
    for part, ref in enumerate((fr_ref, fi_ref)):
        remote(ref.at[pl.ds(5, 3)], fm.at[part, pl.ds(1, 3)], FM, {"col": partner}).start()
        remote(ref.at[extra_row], fm.at[part, 0], FM, {"col": extra_to}).start()
    under_way(FM, fm, fm)

    exchange("row", row, XR, lambda p: tile_of(xt, p), tile_of(xrecv, row))
    under_way(XR, xt.at[pl.ds(0, 15 * DL)], xrecv.at[pl.ds(0, 15 * DL)])
    own_rows = pl.ds(pl.multiple_of(row * DL, DL), DL)
    xrecv[own_rows, :] = xt[own_rows, :]
    cot_load.wait()
    turn_home(cot_ref, ct)
    exchange("row", row, CR, lambda p: tile_of(ct, p), tile_of(crecv, row))
    under_way(CR, ct.at[pl.ds(0, 15 * DL)], crecv.at[pl.ds(0, 15 * DL)])
    crecv[own_rows, :] = ct[own_rows, :]

    w_load.wait()
    w9[...] = jnp.zeros_like(w9)
    for tap in range(3):
        for stream in range(3):
            q = 3 * tap + stream
            w9[q : q + 1, :] = w_ref[tap : tap + 1, 768 * stream : 768 * (stream + 1)]
    for i in range(6):
        wt[128 * i : 128 * (i + 1), :] = w9[:, 128 * i : 128 * (i + 1)].T
    columns = wt[own_rows, :]
    for q in range(9):
        wb[q] = jnp.broadcast_to(columns[:, q : q + 1], (DL, 128))
    for load in loads:
        load.wait()

    lane = lax.broadcasted_iota(jnp.int32, (DL, 128), 1)

    def planes_in(recv, dst, base):
        def body(rows):
            planes = [recv[i, rows, :].astype(F32) for i in range(NP)]
            planes = swap_bits(planes, LOW4)
            for i in range(NP):
                dst[base + i, rows, :] = planes[i]

        over_groups(body)

    def tiles_out(src, dst, table):
        def body(rows):
            flat = src[:, rows, :].reshape(NP * GR, 128)
            out = jnp.dot(flat, first_ref[...], preferred_element_type=F32).reshape(NP, GR, 128)
            tiles = swap_bits([out[i] for i in range(NP)], LOW4)
            for i in range(NP):
                turned = tiles[i] * tf[0, i : i + 1, :] + pltpu.roll(tiles[i], 64, 1) * tf[1, i : i + 1, :]
                dst[i, rows, :] = turned.astype(BF16)

        over_groups(body)

    arrived(XR)
    x3 = xrecv.reshape(NP, DL, 128)
    planes_in(x3, xp, 2)
    hx_send[0] = xp[16].astype(BF16)
    hx_send[1] = xp[17].astype(BF16)
    remote(hx_send, hx_recv, HX, {"col": lax.rem(col + 1, NP)}).start()
    under_way(HX, hx_send, hx_recv)

    def streams(first, last):
        def body(rows):
            taps = [wb[q, rows, :] for q in range(9)]
            behind2, behind1 = xp[first, rows, :], xp[first + 1, rows, :]
            for i in range(first, last):
                now = xp[i + 2, rows, :]
                z = [taps[j] * now + taps[3 + j] * behind1 + taps[6 + j] * behind2 for j in range(3)]
                ap[i, rows, :] = z[0]
                bp[i, rows, :] = z[1]
                sp[i, rows, :] = z[2]
                fld[i, rows, :] = (z[0] * z[1]).astype(BF16)
                behind2, behind1 = behind1, now

        return body

    over_groups(streams(2, NP))
    arrived(CR)
    planes_in(crecv.reshape(NP, DL, 128), cp, 0)
    arrived(HX)
    for i in range(2):
        halo = hx_recv[i].astype(F32)
        back = jnp.where(lane >= 16, pltpu.roll(halo, 16, 1), pltpu.roll(halo, 17, 1))
        back = jnp.where(lane == 0, 0.0, back)
        xp[i] = jnp.where(col == 0, back, halo)

    over_groups(streams(0, 2))
    tiles_out(fld, s_send, tf)
    exchange("col", col, SS, lambda p: s_send.at[p], s_recv.at[col])
    under_way(SS, s_send.at[pl.ds(0, 15)], s_recv.at[pl.ds(0, 15)])
    s_recv[col] = s_send[col]

    def gate_grad(rows):
        for i in range(NP):
            fld[i, rows, :] = (cp[i, rows, :] * sp[i, rows, :]).astype(BF16)

    over_groups(gate_grad)
    tiles_out(fld, g_send, tf)
    exchange("col", col, GG, lambda p: g_send.at[p], g_recv.at[col])
    under_way(GG, g_send.at[pl.ds(0, 15)], g_recv.at[pl.ds(0, 15)])
    g_recv[col] = g_send[col]

    arrived(FM)
    at_row = lax.broadcasted_iota(jnp.int32, (N2, N2), 0)
    at_col = lax.broadcasted_iota(jnp.int32, (N2, N2), 1)
    reverse = jnp.where(at_row + at_col == N2 - 1, 1.0, 0.0).astype(BF16)
    rev[...] = jnp.dot(
        fm[...].reshape(8 * DL, N2), reverse, preferred_element_type=F32
    ).reshape(2, 4, DL, N2)

    def mirror_at(slot):
        return jnp.where(low_half, (4 - slot) % 4, 3 - slot)

    own_at = jnp.where(low_half, 0, 1)
    for slot in range(4):
        rev_re = rev[0, mirror_at(slot)]
        rev_im = -rev[1, mirror_at(slot)]
        if slot == 0:
            fh[0, 4] = rev_re
            fh[1, 4] = rev_im
            rev_re = jnp.where(col == 0, 0.0, rev_re)
            rev_im = jnp.where(col == 0, 0.0, rev_im)
        fh[0, slot] = fo[0, own_at + slot].astype(F32) + rev_re
        fh[1, slot] = fo[1, own_at + slot].astype(F32) + rev_im

    parts = [(0, 4), (1, 5), (2, 6), (3, 7), (8, 9)]

    def spectrum(recv):
        def body(rows):
            planes = swap_bits([recv[i, rows, :].astype(F32) for i in range(NP)], HIGH3)
            for i in range(NP):
                half = i // 8
                pp[i % 8, rows, 128 * half : 128 * (half + 1)] = planes[i].astype(BF16)

        over_groups(body)
        middle = pp[4].astype(F32)
        pp[8] = (middle * ti[0, 4:5, :]).astype(BF16)
        pp[9] = (-middle * ti[1, 4:5, :]).astype(BF16)
        pp[4] = jnp.where(col == 0, 0.0, middle).astype(BF16)

    def products(slot):
        re, im = parts[slot]
        both = jnp.concatenate([pp[re], pp[im]], 0)
        out = jnp.dot(both, second_ref[...], preferred_element_type=F32)
        return out[:DL, :N2], out[:DL, N2:], out[DL:, :N2], out[DL:, N2:]

    def value(slot):
        re_cos, re_sin, im_cos, im_sin = products(slot)
        return re_cos + im_sin, im_cos - re_sin

    def turned_back(slot):
        re_cos, re_sin, im_cos, im_sin = products(slot)
        return re_cos - im_sin, im_cos + re_sin

    def restore(dst):
        for slot in range(4):
            z_re, z_im = turned_back(slot)
            cos, sin = ti[0, slot : slot + 1, :], ti[1, slot : slot + 1, :]
            qq[slot] = z_re * cos - z_im * sin
            q_im = z_im * cos + z_re * sin
            if slot == 0:
                z_re4, z_im4 = turned_back(4)
                q_im = jnp.where(col == 0, z_re4 * ti[0, 4:5, :] - z_im4 * ti[1, 4:5, :], q_im)
            qq[4 + slot] = q_im

        def body(rows):
            planes = [
                qq[i % 8, rows, 128 * (i // 8) : 128 * (i // 8 + 1)] for i in range(NP)
            ]
            planes = swap_bits(planes, HIGH3)
            for i in range(NP):
                dst[i, rows, :] = planes[i].astype(BF16)

        over_groups(body)

    arrived(SS)
    spectrum(s_recv)
    for slot in range(5):
        re, im = parts[slot]
        s_re, s_im = value(slot)
        sr[slot] = s_re
        si[slot] = s_im
        f_re, f_im = fh[0, slot], fh[1, slot]
        pp[re] = (s_re * f_re - s_im * f_im).astype(BF16)
        pp[im] = (s_re * f_im + s_im * f_re).astype(BF16)
    restore(y_send)
    exchange("col", col, YY, lambda p: y_send.at[p], y_recv.at[col])
    under_way(YY, y_send.at[pl.ds(0, 15)], y_recv.at[pl.ds(0, 15)])
    y_recv[col] = y_send[col]

    arrived(GG)
    spectrum(g_recv)
    for slot in range(5):
        re, im = parts[slot]
        g_re, g_im = value(slot)
        f_re, f_im = fh[0, slot], fh[1, slot]
        pp[re] = (g_re * f_re + g_im * f_im).astype(BF16)
        pp[im] = (g_im * f_re - g_re * f_im).astype(BF16)
        s_re, s_im = sr[slot], si[slot]
        grad_re = (s_re * g_re + s_im * g_im) * (1.0 / SEQ)
        grad_im = (s_re * g_im - s_im * g_re) * (1.0 / SEQ)
        if slot < 4:
            fgr_ref[own_at + slot] = grad_re
            fgi_ref[own_at + slot] = grad_im
            gs_send[0, mirror_at(slot)] = grad_re.astype(BF16)
            gs_send[1, mirror_at(slot)] = grad_im.astype(BF16)
        else:
            gs_send[0, 0] = jnp.where(col == 0, grad_re, gs_send[0, 0].astype(F32)).astype(BF16)
            gs_send[1, 0] = jnp.where(col == 0, grad_im, gs_send[1, 0].astype(F32)).astype(BF16)
    restore(z_send)
    exchange("col", col, ZZ, lambda p: z_send.at[p], z_recv.at[col])
    under_way(ZZ, z_send.at[pl.ds(0, 15)], z_recv.at[pl.ds(0, 15)])
    z_recv[col] = z_send[col]
    def send_mirrored():
        back_to = jnp.where(low_half, jnp.where(col == 0, 8, 16 - col), partner)
        back_to = lax.rem(back_to, NP)
        for part in range(2):
            remote(gs_send.at[part, pl.ds(1, 3)], gm_recv.at[part, pl.ds(1, 3)], GM, {"col": partner}).start()
            remote(gs_send.at[part, 0], gm_recv.at[part, 0], GM, {"col": back_to}).start()
        under_way(GM, gs_send, gm_recv)

    def field_back(recv, dst):
        def body(rows):
            planes = swap_bits([recv[i, rows, :].astype(F32) for i in range(NP)], LOW4)
            flat = jnp.stack([p.astype(BF16) for p in planes]).reshape(NP * GR, 128)
            out = jnp.dot(flat, last_ref[...], preferred_element_type=F32)
            dst[:, rows, :] = out.astype(BF16).astype(F32).reshape(NP, GR, 128)

        over_groups(body)

    def send_home(make, dst):
        def body(rows):
            tiles = swap_bits([make(i, rows) for i in range(NP)], LOW4)
            for i in range(NP):
                dst[i, rows, :] = tiles[i].astype(BF16)

        over_groups(body)

    arrived(YY)
    field_back(y_recv, yp)
    send_home(lambda i, rows: sp[i, rows, :] * yp[i, rows, :], m_send)
    exchange("row", row, MR, lambda p: m_send.at[p], tile_of(m_recv, row))
    under_way(MR, m_send.at[pl.ds(0, 15)], m_recv.at[pl.ds(0, 15 * DL)])
    m_recv[own_rows, :] = m_send[row]

    def rounded(value):
        return value.astype(BF16).astype(F32)

    def third_grads(rows):
        taps = [wb[3 * t + 2, rows, :] for t in range(3)]
        sums = [jnp.zeros((GR, 128), F32)] * 3
        before1 = before2 = None
        for i in range(NP):
            grad = rounded(cp[i, rows, :] * yp[i, rows, :])
            at_tap = [taps[t] * grad for t in range(3)]
            sums = [sums[t] + xp[i + 2 - t, rows, :] * grad for t in range(3)]
            if i == 0:
                edge[0, rows, :] = at_tap[2]
                first_one = at_tap[1]
            if i == 1:
                edge[1, rows, :] = first_one + at_tap[2]
            if before2 is not None:
                third[i - 2, rows, :] = before2 + at_tap[2]
            before2 = None if before1 is None else before1 + at_tap[1]
            before1 = at_tap[0]
        third[14, rows, :] = before2
        third[15, rows, :] = before1
        for t in range(3):
            late[t, rows, :] = sums[t]

    over_groups(third_grads)

    arrived(ZZ)
    field_back(z_recv, gp)

    def tap_grads(i, rows):
        gs = gp[i, rows, :]
        grads = (rounded(gs * bp[i, rows, :]), rounded(gs * ap[i, rows, :]))
        return grads, [
            wb[3 * t, rows, :] * grads[0] + wb[3 * t + 1, rows, :] * grads[1] for t in range(3)
        ]

    def edge_grads(rows):
        _, first_taps = tap_grads(0, rows)
        _, next_taps = tap_grads(1, rows)
        hg_send[0, rows, :] = (edge[0, rows, :] + first_taps[2]).astype(BF16)
        hg_send[1, rows, :] = (edge[1, rows, :] + first_taps[1] + next_taps[2]).astype(BF16)

    over_groups(edge_grads)
    remote(hg_send, hg_recv, HG, {"col": lax.rem(col + NP - 1, NP)}).start()
    under_way(HG, hg_send, hg_recv)

    def stream_grads(rows):
        sums = [jnp.zeros((GR, 128), F32)] * 6
        before1 = before2 = None
        for i in range(NP):
            grads, at_tap = tap_grads(i, rows)
            past = [xp[i + 2 - t, rows, :] for t in range(3)]
            sums = [sums[q] + past[q // 2] * grads[q % 2] for q in range(6)]
            if before2 is not None:
                gp[i - 2, rows, :] = third[i - 2, rows, :] + before2 + at_tap[2]
            before2 = None if before1 is None else before1 + at_tap[1]
            before1 = at_tap[0]
        gp[14, rows, :] = third[14, rows, :] + before2
        gp[15, rows, :] = third[15, rows, :] + before1
        at = lax.broadcasted_iota(jnp.int32, (GR, 128), 1)
        total = jnp.zeros((GR, 128), F32)
        for q in range(9):
            tap, stream = divmod(q, 3)
            value = late[tap, rows, :] if stream == 2 else sums[2 * tap + stream]
            total = jnp.where(at == q, jnp.sum(value, axis=1, keepdims=True), total)
        wt[rows, :] = total[:, :16]

    over_groups(stream_grads)
    d1_send[...] = jnp.zeros_like(d1_send)
    terms = wt[:DL, :].T * (1.0 / math.sqrt(SEQ))
    d1_send[:, :DL] = terms[:8]
    d1_send[0:1, 64 : 64 + DL] = terms[8:9]
    exchange("col", col, D1, lambda p: d1_send, d1_recv.at[col])
    under_way(D1, d1_recv.at[pl.ds(0, 15)], d1_recv.at[pl.ds(0, 15)])
    d1_recv[col] = d1_send[...]
    send_mirrored()

    arrived(HG)
    for i in range(2):
        halo = hg_recv[i].astype(F32)
        ahead = jnp.where(lane < 112, pltpu.roll(halo, 112, 1), pltpu.roll(halo, 111, 1))
        ahead = jnp.where(lane == 127, 0.0, ahead)
        gp[14 + i] = gp[14 + i] + jnp.where(col == NP - 1, ahead, halo)
    send_home(lambda i, rows: gp[i, rows, :], i_send)
    exchange("row", row, IR, lambda p: i_send.at[p], tile_of(i_recv, row))
    under_way(IR, i_send.at[pl.ds(0, 15)], i_recv.at[pl.ds(0, 15 * DL)])
    store(i_send.at[row], i_recv.at[own_rows])

    arrived(D1)
    total = d1_recv[0]
    for i in range(1, NP):
        total = total + d1_recv[i]
    d2_send[...] = total
    exchange("row", row, D2, lambda p: d2_send, d2_recv.at[row])
    under_way(D2, d1_recv.at[pl.ds(0, 15)], d2_recv.at[pl.ds(0, 15)])
    store(d2_send, d2_recv.at[row])

    arrived(MR)
    home(m_recv, mixed_ref)
    store(mixed_ref, mixed_hbm)

    arrived(GM)
    rev[...] = jnp.dot(
        gm_recv[...].reshape(8 * DL, N2), reverse, preferred_element_type=F32
    ).reshape(2, 4, DL, N2)
    fgr_ref[extra_row] = rev[0, 0]
    fgi_ref[extra_row] = -rev[1, 0]
    for i in range(1, 4):
        fgr_ref[4 + i] = rev[0, i]
        fgi_ref[4 + i] = -rev[1, i]

    store(fgr_ref, fgr_hbm)
    store(fgi_ref, fgi_hbm)

    arrived(D2)
    arrived(IR)
    for copy in stores:
        copy.wait()

    drain()


def finish(*refs):
    sources, results, (mixed, tiles, grad_re, grad_im, d2_recv, ig_ref, dw_ref) = (
        refs[:5], refs[5:10], refs[10:17],
    )
    load_sem, store_sem = refs[17:]
    held = (mixed, tiles, grad_re, grad_im, d2_recv)
    ready = (mixed, ig_ref, grad_re, grad_im, dw_ref)
    loads = [pltpu.make_async_copy(sources[i], held[i], load_sem.at[i]) for i in range(5)]
    stores = [pltpu.make_async_copy(ready[i], results[i], store_sem.at[i]) for i in range(5)]
    for i in (1, 4, 2, 3, 0):
        loads[i].start()
    loads[1].wait()
    home(tiles, ig_ref)
    stores[1].start()
    for i in (2, 3, 0):
        loads[i].wait()
        stores[i].start()
    loads[4].wait()
    spot = lax.broadcasted_iota(jnp.int32, (16, 128), 1)
    blocks = [jnp.zeros((16, 128), F32)] * 6
    for i in range(NP):
        block, off = divmod(DL * i, 128)
        packed = d2_recv[i]
        piece = jnp.concatenate([packed, pltpu.roll(packed, 64, 1)], 0)
        piece = jnp.where(spot < DL, piece, 0.0)
        piece = pltpu.roll(piece, off, 1) if off else piece
        if off + DL > 128:
            blocks[block] = blocks[block] + jnp.where(spot >= off, piece, 0.0)
            blocks[block + 1] = blocks[block + 1] + jnp.where(spot < off, piece, 0.0)
        else:
            blocks[block] = blocks[block] + piece
    for tap in range(3):
        for stream in range(3):
            q = 3 * tap + stream
            for i in range(6):
                at = 768 * stream + 128 * i
                dw_ref[tap : tap + 1, at : at + 128] = blocks[i][q : q + 1, :]
    stores[4].start()
    for copy in stores:
        copy.wait()


def per_device(sequence, conv_weights, cotangent, filter_re, filter_im):
    first, last, second, fwd, inv = (jnp.asarray(t) for t in tables())
    vmem = pl.BlockSpec(memory_space=pltpu.VMEM)
    hbm = pl.BlockSpec(memory_space=pl.ANY)
    tiles = pltpu.VMEM((NP, DL, 128), BF16)
    planes = pltpu.VMEM((NP, DL, 128), F32)
    flat = pltpu.VMEM((NP * DL, 128), BF16)
    spec = pltpu.VMEM((2, 4, DL, N2), BF16)
    pair = pltpu.VMEM((2, DL, 128), BF16)
    small = pltpu.VMEM((NP, 8, 128), F32)
    one = pltpu.VMEM((8, 128), F32)
    shapes = (
        jax.ShapeDtypeStruct(sequence.shape, BF16),
        jax.ShapeDtypeStruct(sequence.shape, BF16),
        jax.ShapeDtypeStruct(filter_re.shape, F32),
        jax.ShapeDtypeStruct(filter_re.shape, F32),
        jax.ShapeDtypeStruct(conv_weights.shape, F32),
    )
    mixed, grads, filter_re_grad, filter_im_grad, weights = shapes
    between = (
        mixed,
        jax.ShapeDtypeStruct((NP * DL, 128), BF16),
        filter_re_grad,
        filter_im_grad,
        jax.ShapeDtypeStruct((NP, 8, 128), F32),
    )
    outs = pl.pallas_call(
        kernel,
        out_shape=between,
        in_specs=[hbm] * 10,
        out_specs=[hbm] * 5,
        scratch_shapes=[
            *(pltpu.VMEM(s.shape, s.dtype) for s in (mixed, filter_re_grad, filter_im_grad)),
            pltpu.VMEM(sequence.shape, BF16),
            pltpu.VMEM(conv_weights.shape, F32),
            pltpu.VMEM(sequence.shape, BF16),
            pltpu.VMEM((128, 128), BF16),
            pltpu.VMEM((128, 128), BF16),
            pltpu.VMEM((N2, 2 * N2), BF16),
            flat, flat, flat, flat,
            pltpu.VMEM((16, 768), F32),
            pltpu.VMEM((768, 16), F32),
            pltpu.VMEM((9, DL, 128), F32),
            pltpu.VMEM((2, 8, DL, N2), BF16),
            spec,
            pltpu.VMEM((2, 4, DL, N2), F32),
            pltpu.VMEM((2, 5, DL, N2), F32),
            pltpu.VMEM((2, 16, 128), F32),
            pltpu.VMEM((2, 8, N2), F32),
            pltpu.VMEM((NP + 2, DL, 128), F32),
            pair, pair,
            planes, planes, planes, planes, planes,
            tiles,
            tiles, tiles, tiles, tiles, tiles, tiles, tiles, tiles,
            pltpu.VMEM((10, DL, N2), BF16),
            pltpu.VMEM((5, DL, N2), F32),
            pltpu.VMEM((5, DL, N2), F32),
            pltpu.VMEM((8, DL, N2), F32),
            spec, spec,
            planes, planes,
            pltpu.VMEM((2, DL, 128), F32),
            pltpu.VMEM((3, DL, 128), F32),
            pair, pair,
            one, small, one,
            tiles, flat, tiles,
            pltpu.SemaphoreType.DMA((14,)),
            pltpu.SemaphoreType.DMA((14,)),
            pltpu.SemaphoreType.DMA((15,)),
        ],
        compiler_params=pltpu.CompilerParams(
            collective_id=0, has_side_effects=True, vmem_limit_bytes=56 * 1024 * 1024
        ),
    )(
        sequence, conv_weights, cotangent, filter_re, filter_im,
        first, last, second, fwd, inv,
    )
    return pl.pallas_call(
        finish,
        out_shape=shapes,
        in_specs=[hbm] * 5,
        out_specs=[hbm] * 5,
        scratch_shapes=[
            *(pltpu.VMEM(s.shape, s.dtype) for s in between + (grads, weights)),
            pltpu.SemaphoreType.DMA((5,)),
            pltpu.SemaphoreType.DMA((5,)),
        ],
    )(*outs)


def solution(mesh):
    return jax.shard_map(
        per_device,
        mesh=mesh,
        in_specs=(
            P("row", "col", None),
            P(),
            P("row", "col", None),
            P("col", "row", None),
            P("col", "row", None),
        ),
        out_specs=(
            P("row", "col", None),
            P("row", "col", None),
            P("col", "row", None),
            P("col", "row", None),
            P(),
        ),
        check_vma=False,
    )
```

```python
import functools
import math

import jax
import jax.numpy as jnp
import ml_dtypes
import numpy as np
from jax import lax
from jax.experimental import pallas as pl
from jax.experimental.pallas import tpu as pltpu
from jax.sharding import PartitionSpec as P

MESH = pl.DeviceIdType.MESH
F32 = jnp.float32
BF16 = jnp.bfloat16

NP = 16
DL = 48
GR = 16
N1 = 128
N2 = 256
SEQ = N1 * N2

XR, CR, FM, HX, SS, GG, YY, ZZ, GM, HG, D1, MR, IR, D2 = range(14)


def slot_freq(col, slot):
    return 8 * col + slot + (1 if col >= 8 else 0)


def tables():
    lane_n1 = np.array([8 * (l % 16) + l // 16 for l in range(128)])
    first = np.zeros((128, 128))
    last = np.zeros((128, 128))
    for col in range(16):
        for slot in range(4):
            k1 = slot_freq(col, slot)
            turn = 2 * np.pi * (lane_n1 * k1 % 128) / 128
            re_row, im_row = slot * 16 + col, (slot + 4) * 16 + col
            if k1 == 0:
                first[:, re_row] = 1.0
                first[:, im_row] = np.cos(np.pi * lane_n1)
                last[re_row] = 1.0
                last[im_row] = np.cos(np.pi * lane_n1)
            else:
                first[:, re_row] = np.cos(turn)
                first[:, im_row] = -np.sin(turn)
                last[re_row] = np.cos(turn)
                last[im_row] = -np.sin(turn)
    last = last / SEQ
    idx = np.arange(N2)
    angle = 2 * np.pi * (idx[:, None] * idx[None, :] % N2) / N2
    second = np.concatenate([np.cos(angle), np.sin(angle)], 1)
    fwd = np.zeros((16, 2, 16, 128), np.float32)
    inv = np.zeros((16, 2, 8, N2), np.float32)
    low = np.arange(16)
    for col in range(16):
        for target in range(16):
            for slot in range(4):
                k1 = slot_freq(target, slot)
                turn = 2 * np.pi * (k1 * (16 * col + low) % SEQ) / SEQ
                re_l, im_l = slot * 16 + low, (slot + 4) * 16 + low
                fwd[col, 0, target, re_l] = np.cos(turn)
                fwd[col, 0, target, im_l] = np.cos(turn)
                fwd[col, 1, target, re_l] = np.sin(turn)
                fwd[col, 1, target, im_l] = -np.sin(turn)
        for slot in range(5):
            k1 = slot_freq(col, slot) if slot < 4 else 64
            turn = 2 * np.pi * (k1 * idx % SEQ) / SEQ
            inv[col, 0, slot] = np.cos(turn)
            inv[col, 1, slot] = np.sin(turn)
    return (
        first.astype(ml_dtypes.bfloat16),
        last.astype(ml_dtypes.bfloat16),
        second.astype(ml_dtypes.bfloat16),
        fwd,
        inv,
    )


def swap_bits(planes, pairs):
    lane = lax.broadcasted_iota(jnp.int32, planes[0].shape, 1)
    planes = list(planes)
    for plane_bit, lane_bit in pairs:
        shift = 1 << lane_bit
        upper = (lane & shift) != 0
        for i in range(len(planes)):
            if i & (1 << plane_bit):
                continue
            j = i | (1 << plane_bit)
            low, high = planes[i], planes[j]
            planes[i] = jnp.where(upper, pltpu.roll(high, shift, 1), low)
            planes[j] = jnp.where(upper, high, pltpu.roll(low, 128 - shift, 1))
    return planes


LOW4 = ((0, 0), (1, 1), (2, 2), (3, 3))
HIGH3 = ((0, 4), (1, 5), (2, 6))


def home(src, dst_ref):
    for i in range(6):
        block = src[128 * i : 128 * (i + 1), :].astype(F32).T
        dst_ref[:, :, 128 * i : 128 * (i + 1)] = block.astype(BF16).reshape(8, 16, 128)


def kernel(
    x_hbm, w_hbm, cot_hbm, fr_ref, fi_ref, first_hbm, last_hbm, second_hbm, fwd_ref, inv_ref,
    mixed_hbm, i_recv, fgr_hbm, fgi_hbm, d2_recv,
    mixed_ref, fgr_ref, fgi_ref,
    x_ref, w_ref, cot_ref, first_ref, last_ref, second_ref,
    xt, xrecv, ct, crecv, w9, wt, wb, fo, fm, rev, fh, tf, ti,
    xp, hx_send, hx_recv, cp, ap, bp, sp, yp, fld,
    s_send, s_recv, g_send, g_recv, y_send, y_recv, z_send, z_recv,
    pp, sr, si, qq, gs_send, gm_recv, gp, third, edge, late, hg_send, hg_recv,
    d1_send, d1_recv, d2_send, m_send, m_recv, i_send,
    send_sem, recv_sem, local_sem,
):
    row = lax.axis_index("row")
    col = lax.axis_index("col")
    low_half = col < 8

    def remote(src, dst, which, target):
        return pltpu.make_async_remote_copy(
            src_ref=src,
            dst_ref=dst,
            send_sem=send_sem.at[which],
            recv_sem=recv_sem.at[which],
            device_id=target,
            device_id_type=MESH,
        )

    def exchange(axis, me, which, src_at, dst):
        def body(turn, carry):
            away = lax.div(turn, 2) * (2 * lax.rem(turn, 2) - 1)
            peer = lax.rem(me + NP // 2 + away, NP)
            remote(src_at(peer), dst, which, {axis: peer}).start()
            return carry

        lax.fori_loop(1, NP, body, 0)

    def wait_bytes(ref, sem):
        pltpu.make_async_copy(ref, ref, sem).wait()

    leaving, arriving = {}, {}
    stores = []

    def store(src, dst):
        stores.append(pltpu.make_async_copy(src, dst, local_sem.at[10 + len(stores)]))
        stores[-1].start()

    def under_way(which, sent, received):
        leaving[which], arriving[which] = sent, received

    def arrived(which):
        wait_bytes(arriving.pop(which), recv_sem.at[which])

    def drain():
        for which in list(arriving):
            arrived(which)
        for which, ref in leaving.items():
            wait_bytes(ref, send_sem.at[which])

    def tile_of(ref, peer):
        return ref.at[pl.ds(pl.multiple_of(peer * DL, DL), DL)]

    def over_groups(body):
        def step(g, carry):
            body(pl.ds(pl.multiple_of(g * GR, GR), GR))
            return carry

        lax.fori_loop(0, DL // GR, step, 0, unroll=True)

    x_load = pltpu.make_async_copy(x_hbm, x_ref, local_sem.at[4])
    cot_load = pltpu.make_async_copy(cot_hbm, cot_ref, local_sem.at[5])
    w_load = pltpu.make_async_copy(w_hbm, w_ref, local_sem.at[6])
    x_load.start()
    cot_load.start()
    w_load.start()
    barrier = pltpu.get_barrier_semaphore()

    def greet(step, carry):
        pl.semaphore_signal(
            barrier, inc=1, device_id={"row": lax.rem(row + step, NP)}, device_id_type=MESH
        )
        pl.semaphore_signal(
            barrier, inc=1, device_id={"col": lax.rem(col + step, NP)}, device_id_type=MESH
        )
        return carry

    lax.fori_loop(1, NP, greet, 0)

    loads = [
        pltpu.make_async_copy(first_hbm, first_ref, local_sem.at[7]),
        pltpu.make_async_copy(second_hbm, second_ref, local_sem.at[8]),
        pltpu.make_async_copy(last_hbm, last_ref, local_sem.at[9]),
        pltpu.make_async_copy(fr_ref, fo.at[0], local_sem.at[0]),
        pltpu.make_async_copy(fi_ref, fo.at[1], local_sem.at[1]),
        pltpu.make_async_copy(fwd_ref.at[col], tf, local_sem.at[2]),
        pltpu.make_async_copy(inv_ref.at[col], ti, local_sem.at[3]),
    ]
    for load in loads:
        load.start()

    def turn_home(src_ref, dst):
        for i in range(6):
            block = src_ref[:, :, 128 * i : 128 * (i + 1)].reshape(128, 128).astype(F32)
            dst[128 * i : 128 * (i + 1), :] = block.T.astype(BF16)

    x_load.wait()
    turn_home(x_ref, xt)
    pl.semaphore_wait(barrier, 2 * (NP - 1))

    partner = 15 - col
    extra_row = jnp.where(low_half, 4, 0)
    extra_to = jnp.where(low_half, partner, lax.rem(16 - col, 8))
    for part, ref in enumerate((fr_ref, fi_ref)):
        remote(ref.at[pl.ds(5, 3)], fm.at[part, pl.ds(1, 3)], FM, {"col": partner}).start()
        remote(ref.at[extra_row], fm.at[part, 0], FM, {"col": extra_to}).start()
    under_way(FM, fm, fm)

    exchange("row", row, XR, lambda p: tile_of(xt, p), tile_of(xrecv, row))
    under_way(XR, xt.at[pl.ds(0, 15 * DL)], xrecv.at[pl.ds(0, 15 * DL)])
    own_rows = pl.ds(pl.multiple_of(row * DL, DL), DL)
    xrecv[own_rows, :] = xt[own_rows, :]
    cot_load.wait()
    turn_home(cot_ref, ct)
    exchange("row", row, CR, lambda p: tile_of(ct, p), tile_of(crecv, row))
    under_way(CR, ct.at[pl.ds(0, 15 * DL)], crecv.at[pl.ds(0, 15 * DL)])
    crecv[own_rows, :] = ct[own_rows, :]

    w_load.wait()
    w9[...] = jnp.zeros_like(w9)
    for tap in range(3):
        for stream in range(3):
            q = 3 * tap + stream
            w9[q : q + 1, :] = w_ref[tap : tap + 1, 768 * stream : 768 * (stream + 1)]
    for i in range(6):
        wt[128 * i : 128 * (i + 1), :] = w9[:, 128 * i : 128 * (i + 1)].T
    columns = wt[own_rows, :]
    for q in range(9):
        wb[q] = jnp.broadcast_to(columns[:, q : q + 1], (DL, 128))
    for load in loads:
        load.wait()

    lane = lax.broadcasted_iota(jnp.int32, (DL, 128), 1)

    def planes_in(recv, dst, base):
        def body(rows):
            planes = [recv[i, rows, :].astype(F32) for i in range(NP)]
            planes = swap_bits(planes, LOW4)
            for i in range(NP):
                dst[base + i, rows, :] = planes[i]

        over_groups(body)

    def tiles_out(src, dst, table):
        def body(rows):
            flat = src[:, rows, :].reshape(NP * GR, 128)
            out = jnp.dot(flat, first_ref[...], preferred_element_type=F32).reshape(NP, GR, 128)
            tiles = swap_bits([out[i] for i in range(NP)], LOW4)
            for i in range(NP):
                turned = tiles[i] * tf[0, i : i + 1, :] + pltpu.roll(tiles[i], 64, 1) * tf[1, i : i + 1, :]
                dst[i, rows, :] = turned.astype(BF16)

        over_groups(body)

    arrived(XR)
    x3 = xrecv.reshape(NP, DL, 128)
    planes_in(x3, xp, 2)
    hx_send[0] = xp[16].astype(BF16)
    hx_send[1] = xp[17].astype(BF16)
    remote(hx_send, hx_recv, HX, {"col": lax.rem(col + 1, NP)}).start()
    under_way(HX, hx_send, hx_recv)

    def streams(first, last):
        def body(rows):
            taps = [wb[q, rows, :] for q in range(9)]
            behind2, behind1 = xp[first, rows, :], xp[first + 1, rows, :]
            for i in range(first, last):
                now = xp[i + 2, rows, :]
                z = [taps[j] * now + taps[3 + j] * behind1 + taps[6 + j] * behind2 for j in range(3)]
                ap[i, rows, :] = z[0]
                bp[i, rows, :] = z[1]
                sp[i, rows, :] = z[2]
                fld[i, rows, :] = (z[0] * z[1]).astype(BF16)
                behind2, behind1 = behind1, now

        return body

    over_groups(streams(2, NP))
    arrived(HX)
    for i in range(2):
        halo = hx_recv[i].astype(F32)
        back = jnp.where(lane >= 16, pltpu.roll(halo, 16, 1), pltpu.roll(halo, 17, 1))
        back = jnp.where(lane == 0, 0.0, back)
        xp[i] = jnp.where(col == 0, back, halo)

    over_groups(streams(0, 2))
    tiles_out(fld, s_send, tf)
    exchange("col", col, SS, lambda p: s_send.at[p], s_recv.at[col])
    under_way(SS, s_send.at[pl.ds(0, 15)], s_recv.at[pl.ds(0, 15)])
    s_recv[col] = s_send[col]

    arrived(CR)
    planes_in(crecv.reshape(NP, DL, 128), cp, 0)

    def gate_grad(rows):
        for i in range(NP):
            fld[i, rows, :] = (cp[i, rows, :] * sp[i, rows, :]).astype(BF16)

    over_groups(gate_grad)
    tiles_out(fld, g_send, tf)
    exchange("col", col, GG, lambda p: g_send.at[p], g_recv.at[col])
    under_way(GG, g_send.at[pl.ds(0, 15)], g_recv.at[pl.ds(0, 15)])
    g_recv[col] = g_send[col]

    arrived(FM)
    at_row = lax.broadcasted_iota(jnp.int32, (N2, N2), 0)
    at_col = lax.broadcasted_iota(jnp.int32, (N2, N2), 1)
    reverse = jnp.where(at_row + at_col == N2 - 1, 1.0, 0.0).astype(BF16)
    rev[...] = jnp.dot(
        fm[...].reshape(8 * DL, N2), reverse, preferred_element_type=F32
    ).reshape(2, 4, DL, N2)

    def mirror_at(slot):
        return jnp.where(low_half, (4 - slot) % 4, 3 - slot)

    own_at = jnp.where(low_half, 0, 1)
    for slot in range(4):
        rev_re = rev[0, mirror_at(slot)]
        rev_im = -rev[1, mirror_at(slot)]
        if slot == 0:
            fh[0, 4] = rev_re
            fh[1, 4] = rev_im
            rev_re = jnp.where(col == 0, 0.0, rev_re)
            rev_im = jnp.where(col == 0, 0.0, rev_im)
        fh[0, slot] = fo[0, own_at + slot].astype(F32) + rev_re
        fh[1, slot] = fo[1, own_at + slot].astype(F32) + rev_im

    parts = [(0, 4), (1, 5), (2, 6), (3, 7), (8, 9)]

    def spectrum(recv):
        def body(rows):
            planes = swap_bits([recv[i, rows, :].astype(F32) for i in range(NP)], HIGH3)
            for i in range(NP):
                half = i // 8
                pp[i % 8, rows, 128 * half : 128 * (half + 1)] = planes[i].astype(BF16)

        over_groups(body)
        middle = pp[4].astype(F32)
        pp[8] = (middle * ti[0, 4:5, :]).astype(BF16)
        pp[9] = (-middle * ti[1, 4:5, :]).astype(BF16)
        pp[4] = jnp.where(col == 0, 0.0, middle).astype(BF16)

    def products(slot):
        re, im = parts[slot]
        both = jnp.concatenate([pp[re], pp[im]], 0)
        out = jnp.dot(both, second_ref[...], preferred_element_type=F32)
        return out[:DL, :N2], out[:DL, N2:], out[DL:, :N2], out[DL:, N2:]

    def value(slot):
        re_cos, re_sin, im_cos, im_sin = products(slot)
        return re_cos + im_sin, im_cos - re_sin

    def turned_back(slot):
        re_cos, re_sin, im_cos, im_sin = products(slot)
        return re_cos - im_sin, im_cos + re_sin

    def restore(dst):
        for slot in range(4):
            z_re, z_im = turned_back(slot)
            cos, sin = ti[0, slot : slot + 1, :], ti[1, slot : slot + 1, :]
            qq[slot] = z_re * cos - z_im * sin
            q_im = z_im * cos + z_re * sin
            if slot == 0:
                z_re4, z_im4 = turned_back(4)
                q_im = jnp.where(col == 0, z_re4 * ti[0, 4:5, :] - z_im4 * ti[1, 4:5, :], q_im)
            qq[4 + slot] = q_im

        def body(rows):
            planes = [
                qq[i % 8, rows, 128 * (i // 8) : 128 * (i // 8 + 1)] for i in range(NP)
            ]
            planes = swap_bits(planes, HIGH3)
            for i in range(NP):
                dst[i, rows, :] = planes[i].astype(BF16)

        over_groups(body)

    arrived(SS)
    spectrum(s_recv)
    for slot in range(5):
        re, im = parts[slot]
        s_re, s_im = value(slot)
        sr[slot] = s_re
        si[slot] = s_im
        f_re, f_im = fh[0, slot], fh[1, slot]
        pp[re] = (s_re * f_re - s_im * f_im).astype(BF16)
        pp[im] = (s_re * f_im + s_im * f_re).astype(BF16)
    restore(y_send)
    exchange("col", col, YY, lambda p: y_send.at[p], y_recv.at[col])
    under_way(YY, y_send.at[pl.ds(0, 15)], y_recv.at[pl.ds(0, 15)])
    y_recv[col] = y_send[col]

    arrived(GG)
    spectrum(g_recv)
    for slot in range(5):
        re, im = parts[slot]
        g_re, g_im = value(slot)
        f_re, f_im = fh[0, slot], fh[1, slot]
        pp[re] = (g_re * f_re + g_im * f_im).astype(BF16)
        pp[im] = (g_im * f_re - g_re * f_im).astype(BF16)
        s_re, s_im = sr[slot], si[slot]
        grad_re = (s_re * g_re + s_im * g_im) * (1.0 / SEQ)
        grad_im = (s_re * g_im - s_im * g_re) * (1.0 / SEQ)
        if slot < 4:
            fgr_ref[own_at + slot] = grad_re
            fgi_ref[own_at + slot] = grad_im
            gs_send[0, mirror_at(slot)] = grad_re.astype(BF16)
            gs_send[1, mirror_at(slot)] = grad_im.astype(BF16)
        else:
            gs_send[0, 0] = jnp.where(col == 0, grad_re, gs_send[0, 0].astype(F32)).astype(BF16)
            gs_send[1, 0] = jnp.where(col == 0, grad_im, gs_send[1, 0].astype(F32)).astype(BF16)
    restore(z_send)
    exchange("col", col, ZZ, lambda p: z_send.at[p], z_recv.at[col])
    under_way(ZZ, z_send.at[pl.ds(0, 15)], z_recv.at[pl.ds(0, 15)])
    z_recv[col] = z_send[col]
    def send_mirrored():
        back_to = jnp.where(low_half, jnp.where(col == 0, 8, 16 - col), partner)
        back_to = lax.rem(back_to, NP)
        for part in range(2):
            remote(gs_send.at[part, pl.ds(1, 3)], gm_recv.at[part, pl.ds(1, 3)], GM, {"col": partner}).start()
            remote(gs_send.at[part, 0], gm_recv.at[part, 0], GM, {"col": back_to}).start()
        under_way(GM, gs_send, gm_recv)

    def field_back(recv, dst):
        def body(rows):
            planes = swap_bits([recv[i, rows, :].astype(F32) for i in range(NP)], LOW4)
            flat = jnp.stack([p.astype(BF16) for p in planes]).reshape(NP * GR, 128)
            out = jnp.dot(flat, last_ref[...], preferred_element_type=F32)
            dst[:, rows, :] = out.astype(BF16).astype(F32).reshape(NP, GR, 128)

        over_groups(body)

    def send_home(make, dst):
        def body(rows):
            tiles = swap_bits([make(i, rows) for i in range(NP)], LOW4)
            for i in range(NP):
                dst[i, rows, :] = tiles[i].astype(BF16)

        over_groups(body)

    arrived(YY)
    field_back(y_recv, yp)
    send_home(lambda i, rows: sp[i, rows, :] * yp[i, rows, :], m_send)
    exchange("row", row, MR, lambda p: m_send.at[p], tile_of(m_recv, row))
    under_way(MR, m_send.at[pl.ds(0, 15)], m_recv.at[pl.ds(0, 15 * DL)])
    m_recv[own_rows, :] = m_send[row]

    def rounded(value):
        return value.astype(BF16).astype(F32)

    def third_grads(rows):
        taps = [wb[3 * t + 2, rows, :] for t in range(3)]
        sums = [jnp.zeros((GR, 128), F32)] * 3
        before1 = before2 = None
        for i in range(NP):
            grad = rounded(cp[i, rows, :] * yp[i, rows, :])
            at_tap = [taps[t] * grad for t in range(3)]
            sums = [sums[t] + xp[i + 2 - t, rows, :] * grad for t in range(3)]
            if i == 0:
                edge[0, rows, :] = at_tap[2]
                first_one = at_tap[1]
            if i == 1:
                edge[1, rows, :] = first_one + at_tap[2]
            if before2 is not None:
                third[i - 2, rows, :] = before2 + at_tap[2]
            before2 = None if before1 is None else before1 + at_tap[1]
            before1 = at_tap[0]
        third[14, rows, :] = before2
        third[15, rows, :] = before1
        for t in range(3):
            late[t, rows, :] = sums[t]

    over_groups(third_grads)

    arrived(ZZ)
    field_back(z_recv, gp)

    def tap_grads(i, rows):
        gs = gp[i, rows, :]
        grads = (rounded(gs * bp[i, rows, :]), rounded(gs * ap[i, rows, :]))
        return grads, [
            wb[3 * t, rows, :] * grads[0] + wb[3 * t + 1, rows, :] * grads[1] for t in range(3)
        ]

    def edge_grads(rows):
        _, first_taps = tap_grads(0, rows)
        _, next_taps = tap_grads(1, rows)
        hg_send[0, rows, :] = (edge[0, rows, :] + first_taps[2]).astype(BF16)
        hg_send[1, rows, :] = (edge[1, rows, :] + first_taps[1] + next_taps[2]).astype(BF16)

    over_groups(edge_grads)
    remote(hg_send, hg_recv, HG, {"col": lax.rem(col + NP - 1, NP)}).start()
    under_way(HG, hg_send, hg_recv)

    def stream_grads(rows):
        sums = [jnp.zeros((GR, 128), F32)] * 6
        before1 = before2 = None
        for i in range(NP):
            grads, at_tap = tap_grads(i, rows)
            past = [xp[i + 2 - t, rows, :] for t in range(3)]
            sums = [sums[q] + past[q // 2] * grads[q % 2] for q in range(6)]
            if before2 is not None:
                gp[i - 2, rows, :] = third[i - 2, rows, :] + before2 + at_tap[2]
            before2 = None if before1 is None else before1 + at_tap[1]
            before1 = at_tap[0]
        gp[14, rows, :] = third[14, rows, :] + before2
        gp[15, rows, :] = third[15, rows, :] + before1
        at = lax.broadcasted_iota(jnp.int32, (GR, 128), 1)
        total = jnp.zeros((GR, 128), F32)
        for q in range(9):
            tap, stream = divmod(q, 3)
            value = late[tap, rows, :] if stream == 2 else sums[2 * tap + stream]
            total = jnp.where(at == q, jnp.sum(value, axis=1, keepdims=True), total)
        wt[rows, :] = total[:, :16]

    over_groups(stream_grads)
    d1_send[...] = jnp.zeros_like(d1_send)
    terms = wt[:DL, :].T * (1.0 / math.sqrt(SEQ))
    d1_send[:, :DL] = terms[:8]
    d1_send[0:1, 64 : 64 + DL] = terms[8:9]
    exchange("col", col, D1, lambda p: d1_send, d1_recv.at[col])
    under_way(D1, d1_recv.at[pl.ds(0, 15)], d1_recv.at[pl.ds(0, 15)])
    d1_recv[col] = d1_send[...]
    send_mirrored()

    arrived(HG)
    for i in range(2):
        halo = hg_recv[i].astype(F32)
        ahead = jnp.where(lane < 112, pltpu.roll(halo, 112, 1), pltpu.roll(halo, 111, 1))
        ahead = jnp.where(lane == 127, 0.0, ahead)
        gp[14 + i] = gp[14 + i] + jnp.where(col == NP - 1, ahead, halo)
    send_home(lambda i, rows: gp[i, rows, :], i_send)
    exchange("row", row, IR, lambda p: i_send.at[p], tile_of(i_recv, row))
    under_way(IR, i_send.at[pl.ds(0, 15)], i_recv.at[pl.ds(0, 15 * DL)])
    store(i_send.at[row], i_recv.at[own_rows])

    arrived(D1)
    total = d1_recv[0]
    for i in range(1, NP):
        total = total + d1_recv[i]
    d2_send[...] = total
    exchange("row", row, D2, lambda p: d2_send, d2_recv.at[row])
    under_way(D2, d1_recv.at[pl.ds(0, 15)], d2_recv.at[pl.ds(0, 15)])
    store(d2_send, d2_recv.at[row])

    arrived(MR)
    home(m_recv, mixed_ref)
    store(mixed_ref, mixed_hbm)

    arrived(GM)
    rev[...] = jnp.dot(
        gm_recv[...].reshape(8 * DL, N2), reverse, preferred_element_type=F32
    ).reshape(2, 4, DL, N2)
    fgr_ref[extra_row] = rev[0, 0]
    fgi_ref[extra_row] = -rev[1, 0]
    for i in range(1, 4):
        fgr_ref[4 + i] = rev[0, i]
        fgi_ref[4 + i] = -rev[1, i]

    store(fgr_ref, fgr_hbm)
    store(fgi_ref, fgi_hbm)

    arrived(D2)
    arrived(IR)
    for copy in stores:
        copy.wait()

    drain()


def finish(*refs):
    sources, results, (mixed, tiles, grad_re, grad_im, d2_recv, ig_ref, dw_ref) = (
        refs[:5], refs[5:10], refs[10:17],
    )
    load_sem, store_sem = refs[17:]
    held = (mixed, tiles, grad_re, grad_im, d2_recv)
    ready = (mixed, ig_ref, grad_re, grad_im, dw_ref)
    loads = [pltpu.make_async_copy(sources[i], held[i], load_sem.at[i]) for i in range(5)]
    stores = [pltpu.make_async_copy(ready[i], results[i], store_sem.at[i]) for i in range(5)]
    for i in (1, 4, 2, 3, 0):
        loads[i].start()
    loads[1].wait()
    home(tiles, ig_ref)
    stores[1].start()
    for i in (2, 3, 0):
        loads[i].wait()
        stores[i].start()
    loads[4].wait()
    spot = lax.broadcasted_iota(jnp.int32, (16, 128), 1)
    blocks = [jnp.zeros((16, 128), F32)] * 6
    for i in range(NP):
        block, off = divmod(DL * i, 128)
        packed = d2_recv[i]
        piece = jnp.concatenate([packed, pltpu.roll(packed, 64, 1)], 0)
        piece = jnp.where(spot < DL, piece, 0.0)
        piece = pltpu.roll(piece, off, 1) if off else piece
        if off + DL > 128:
            blocks[block] = blocks[block] + jnp.where(spot >= off, piece, 0.0)
            blocks[block + 1] = blocks[block + 1] + jnp.where(spot < off, piece, 0.0)
        else:
            blocks[block] = blocks[block] + piece
    for tap in range(3):
        for stream in range(3):
            q = 3 * tap + stream
            for i in range(6):
                at = 768 * stream + 128 * i
                dw_ref[tap : tap + 1, at : at + 128] = blocks[i][q : q + 1, :]
    stores[4].start()
    for copy in stores:
        copy.wait()


def per_device(sequence, conv_weights, cotangent, filter_re, filter_im):
    first, last, second, fwd, inv = (jnp.asarray(t) for t in tables())
    vmem = pl.BlockSpec(memory_space=pltpu.VMEM)
    hbm = pl.BlockSpec(memory_space=pl.ANY)
    tiles = pltpu.VMEM((NP, DL, 128), BF16)
    planes = pltpu.VMEM((NP, DL, 128), F32)
    flat = pltpu.VMEM((NP * DL, 128), BF16)
    spec = pltpu.VMEM((2, 4, DL, N2), BF16)
    pair = pltpu.VMEM((2, DL, 128), BF16)
    small = pltpu.VMEM((NP, 8, 128), F32)
    one = pltpu.VMEM((8, 128), F32)
    shapes = (
        jax.ShapeDtypeStruct(sequence.shape, BF16),
        jax.ShapeDtypeStruct(sequence.shape, BF16),
        jax.ShapeDtypeStruct(filter_re.shape, F32),
        jax.ShapeDtypeStruct(filter_re.shape, F32),
        jax.ShapeDtypeStruct(conv_weights.shape, F32),
    )
    mixed, grads, filter_re_grad, filter_im_grad, weights = shapes
    between = (
        mixed,
        jax.ShapeDtypeStruct((NP * DL, 128), BF16),
        filter_re_grad,
        filter_im_grad,
        jax.ShapeDtypeStruct((NP, 8, 128), F32),
    )
    outs = pl.pallas_call(
        kernel,
        out_shape=between,
        in_specs=[hbm] * 10,
        out_specs=[hbm] * 5,
        scratch_shapes=[
            *(pltpu.VMEM(s.shape, s.dtype) for s in (mixed, filter_re_grad, filter_im_grad)),
            pltpu.VMEM(sequence.shape, BF16),
            pltpu.VMEM(conv_weights.shape, F32),
            pltpu.VMEM(sequence.shape, BF16),
            pltpu.VMEM((128, 128), BF16),
            pltpu.VMEM((128, 128), BF16),
            pltpu.VMEM((N2, 2 * N2), BF16),
            flat, flat, flat, flat,
            pltpu.VMEM((16, 768), F32),
            pltpu.VMEM((768, 16), F32),
            pltpu.VMEM((9, DL, 128), F32),
            pltpu.VMEM((2, 8, DL, N2), BF16),
            spec,
            pltpu.VMEM((2, 4, DL, N2), F32),
            pltpu.VMEM((2, 5, DL, N2), F32),
            pltpu.VMEM((2, 16, 128), F32),
            pltpu.VMEM((2, 8, N2), F32),
            pltpu.VMEM((NP + 2, DL, 128), F32),
            pair, pair,
            planes, planes, planes, planes, planes,
            tiles,
            tiles, tiles, tiles, tiles, tiles, tiles, tiles, tiles,
            pltpu.VMEM((10, DL, N2), BF16),
            pltpu.VMEM((5, DL, N2), F32),
            pltpu.VMEM((5, DL, N2), F32),
            pltpu.VMEM((8, DL, N2), F32),
            spec, spec,
            planes, planes,
            pltpu.VMEM((2, DL, 128), F32),
            pltpu.VMEM((3, DL, 128), F32),
            pair, pair,
            one, small, one,
            tiles, flat, tiles,
            pltpu.SemaphoreType.DMA((14,)),
            pltpu.SemaphoreType.DMA((14,)),
            pltpu.SemaphoreType.DMA((15,)),
        ],
        compiler_params=pltpu.CompilerParams(
            collective_id=0, has_side_effects=True, vmem_limit_bytes=56 * 1024 * 1024
        ),
    )(
        sequence, conv_weights, cotangent, filter_re, filter_im,
        first, last, second, fwd, inv,
    )
    return pl.pallas_call(
        finish,
        out_shape=shapes,
        in_specs=[hbm] * 5,
        out_specs=[hbm] * 5,
        scratch_shapes=[
            *(pltpu.VMEM(s.shape, s.dtype) for s in between + (grads, weights)),
            pltpu.SemaphoreType.DMA((5,)),
            pltpu.SemaphoreType.DMA((5,)),
        ],
    )(*outs)


def solution(mesh):
    return jax.shard_map(
        per_device,
        mesh=mesh,
        in_specs=(
            P("row", "col", None),
            P(),
            P("row", "col", None),
            P("col", "row", None),
            P("col", "row", None),
        ),
        out_specs=(
            P("row", "col", None),
            P("row", "col", None),
            P("col", "row", None),
            P("col", "row", None),
            P(),
        ),
        check_vma=False,
    )
```

```python
import functools
import math

import jax
import jax.numpy as jnp
import ml_dtypes
import numpy as np
from jax import lax
from jax.experimental import pallas as pl
from jax.experimental.pallas import tpu as pltpu
from jax.sharding import PartitionSpec as P

MESH = pl.DeviceIdType.MESH
F32 = jnp.float32
BF16 = jnp.bfloat16

NP = 16
DL = 48
GR = 16
N1 = 128
N2 = 256
SEQ = N1 * N2

XR, CR, FM, HX, SS, GG, YY, ZZ, GM, HG, D1, MR, IR, D2 = range(14)


def slot_freq(col, slot):
    return 8 * col + slot + (1 if col >= 8 else 0)


def tables():
    lane_n1 = np.array([8 * (l % 16) + l // 16 for l in range(128)])
    first = np.zeros((128, 128))
    last = np.zeros((128, 128))
    for col in range(16):
        for slot in range(4):
            k1 = slot_freq(col, slot)
            turn = 2 * np.pi * (lane_n1 * k1 % 128) / 128
            re_row, im_row = slot * 16 + col, (slot + 4) * 16 + col
            if k1 == 0:
                first[:, re_row] = 1.0
                first[:, im_row] = np.cos(np.pi * lane_n1)
                last[re_row] = 1.0
                last[im_row] = np.cos(np.pi * lane_n1)
            else:
                first[:, re_row] = np.cos(turn)
                first[:, im_row] = -np.sin(turn)
                last[re_row] = np.cos(turn)
                last[im_row] = -np.sin(turn)
    last = last / SEQ
    idx = np.arange(N2)
    angle = 2 * np.pi * (idx[:, None] * idx[None, :] % N2) / N2
    second = np.concatenate([np.cos(angle), np.sin(angle)], 1)
    fwd = np.zeros((16, 2, 16, 128), np.float32)
    inv = np.zeros((16, 2, 8, N2), np.float32)
    low = np.arange(16)
    for col in range(16):
        for target in range(16):
            for slot in range(4):
                k1 = slot_freq(target, slot)
                turn = 2 * np.pi * (k1 * (16 * col + low) % SEQ) / SEQ
                re_l, im_l = slot * 16 + low, (slot + 4) * 16 + low
                fwd[col, 0, target, re_l] = np.cos(turn)
                fwd[col, 0, target, im_l] = np.cos(turn)
                fwd[col, 1, target, re_l] = np.sin(turn)
                fwd[col, 1, target, im_l] = -np.sin(turn)
        for slot in range(5):
            k1 = slot_freq(col, slot) if slot < 4 else 64
            turn = 2 * np.pi * (k1 * idx % SEQ) / SEQ
            inv[col, 0, slot] = np.cos(turn)
            inv[col, 1, slot] = np.sin(turn)
    return (
        first.astype(ml_dtypes.bfloat16),
        last.astype(ml_dtypes.bfloat16),
        second.astype(ml_dtypes.bfloat16),
        fwd,
        inv,
    )


def swap_bits(planes, pairs):
    lane = lax.broadcasted_iota(jnp.int32, planes[0].shape, 1)
    planes = list(planes)
    for plane_bit, lane_bit in pairs:
        shift = 1 << lane_bit
        upper = (lane & shift) != 0
        for i in range(len(planes)):
            if i & (1 << plane_bit):
                continue
            j = i | (1 << plane_bit)
            low, high = planes[i], planes[j]
            planes[i] = jnp.where(upper, pltpu.roll(high, shift, 1), low)
            planes[j] = jnp.where(upper, high, pltpu.roll(low, 128 - shift, 1))
    return planes


LOW4 = ((0, 0), (1, 1), (2, 2), (3, 3))
HIGH3 = ((0, 4), (1, 5), (2, 6))


def home(src, dst_ref):
    for i in range(6):
        block = src[128 * i : 128 * (i + 1), :].astype(F32).T
        dst_ref[:, :, 128 * i : 128 * (i + 1)] = block.astype(BF16).reshape(8, 16, 128)


def kernel(
    x_hbm, w_hbm, cot_hbm, fr_ref, fi_ref, first_hbm, last_hbm, second_hbm, fwd_ref, inv_ref,
    mixed_hbm, i_recv, fgr_hbm, fgi_hbm, d2_recv,
    mixed_ref, fgr_ref, fgi_ref,
    x_ref, w_ref, cot_ref, first_ref, last_ref, second_ref,
    xt, xrecv, ct, crecv, w9, wt, wb, fo, fm, rev, fh, tf, ti,
    xp, hx_send, hx_recv, cp, ap, bp, sp, yp, fld,
    s_send, s_recv, g_send, g_recv, y_send, y_recv, z_send, z_recv,
    pp, sr, si, qq, gs_send, gm_recv, gp, third, edge, late, hg_send, hg_recv,
    d1_send, d1_recv, d2_send, m_send, m_recv, i_send,
    send_sem, recv_sem, local_sem,
):
    row = lax.axis_index("row")
    col = lax.axis_index("col")
    low_half = col < 8

    def remote(src, dst, which, target):
        return pltpu.make_async_remote_copy(
            src_ref=src,
            dst_ref=dst,
            send_sem=send_sem.at[which],
            recv_sem=recv_sem.at[which],
            device_id=target,
            device_id_type=MESH,
        )

    def exchange(axis, me, which, src_at, dst):
        def body(turn, carry):
            away = lax.div(turn, 2) * (2 * lax.rem(turn, 2) - 1)
            peer = lax.rem(me + NP // 2 + away, NP)
            remote(src_at(peer), dst, which, {axis: peer}).start()
            return carry

        lax.fori_loop(1, NP, body, 0)

    def wait_bytes(ref, sem):
        pltpu.make_async_copy(ref, ref, sem).wait()

    leaving, arriving = {}, {}
    stores = []

    def store(src, dst):
        stores.append(pltpu.make_async_copy(src, dst, local_sem.at[10 + len(stores)]))
        stores[-1].start()

    def under_way(which, sent, received):
        leaving[which], arriving[which] = sent, received

    def arrived(which):
        wait_bytes(arriving.pop(which), recv_sem.at[which])

    def drain():
        for which in list(arriving):
            arrived(which)
        for which, ref in leaving.items():
            wait_bytes(ref, send_sem.at[which])

    def tile_of(ref, peer):
        return ref.at[pl.ds(pl.multiple_of(peer * DL, DL), DL)]

    def over_groups(body):
        def step(g, carry):
            body(pl.ds(pl.multiple_of(g * GR, GR), GR))
            return carry

        lax.fori_loop(0, DL // GR, step, 0, unroll=True)

    x_load = pltpu.make_async_copy(x_hbm, x_ref, local_sem.at[4])
    cot_load = pltpu.make_async_copy(cot_hbm, cot_ref, local_sem.at[5])
    w_load = pltpu.make_async_copy(w_hbm, w_ref, local_sem.at[6])
    x_load.start()
    cot_load.start()
    w_load.start()
    barrier = pltpu.get_barrier_semaphore()

    def greet(turn, carry):
        step = NP // 2 + lax.div(turn, 2) * (2 * lax.rem(turn, 2) - 1)
        pl.semaphore_signal(
            barrier, inc=1, device_id={"row": lax.rem(row + step, NP)}, device_id_type=MESH
        )
        pl.semaphore_signal(
            barrier, inc=1, device_id={"col": lax.rem(col + step, NP)}, device_id_type=MESH
        )
        return carry

    lax.fori_loop(1, NP, greet, 0)

    loads = [
        pltpu.make_async_copy(first_hbm, first_ref, local_sem.at[7]),
        pltpu.make_async_copy(second_hbm, second_ref, local_sem.at[8]),
        pltpu.make_async_copy(last_hbm, last_ref, local_sem.at[9]),
        pltpu.make_async_copy(fr_ref, fo.at[0], local_sem.at[0]),
        pltpu.make_async_copy(fi_ref, fo.at[1], local_sem.at[1]),
        pltpu.make_async_copy(fwd_ref.at[col], tf, local_sem.at[2]),
        pltpu.make_async_copy(inv_ref.at[col], ti, local_sem.at[3]),
    ]
    for load in loads:
        load.start()

    def turn_home(src_ref, dst):
        for i in range(6):
            block = src_ref[:, :, 128 * i : 128 * (i + 1)].reshape(128, 128).astype(F32)
            dst[128 * i : 128 * (i + 1), :] = block.T.astype(BF16)

    x_load.wait()
    turn_home(x_ref, xt)
    pl.semaphore_wait(barrier, 2 * (NP - 1))

    partner = 15 - col
    extra_row = jnp.where(low_half, 4, 0)
    extra_to = jnp.where(low_half, partner, lax.rem(16 - col, 8))
    for part, ref in enumerate((fr_ref, fi_ref)):
        remote(ref.at[pl.ds(5, 3)], fm.at[part, pl.ds(1, 3)], FM, {"col": partner}).start()
        remote(ref.at[extra_row], fm.at[part, 0], FM, {"col": extra_to}).start()
    under_way(FM, fm, fm)

    exchange("row", row, XR, lambda p: tile_of(xt, p), tile_of(xrecv, row))
    under_way(XR, xt.at[pl.ds(0, 15 * DL)], xrecv.at[pl.ds(0, 15 * DL)])
    own_rows = pl.ds(pl.multiple_of(row * DL, DL), DL)
    xrecv[own_rows, :] = xt[own_rows, :]
    cot_load.wait()
    turn_home(cot_ref, ct)
    exchange("row", row, CR, lambda p: tile_of(ct, p), tile_of(crecv, row))
    under_way(CR, ct.at[pl.ds(0, 15 * DL)], crecv.at[pl.ds(0, 15 * DL)])
    crecv[own_rows, :] = ct[own_rows, :]

    w_load.wait()
    w9[...] = jnp.zeros_like(w9)
    for tap in range(3):
        for stream in range(3):
            q = 3 * tap + stream
            w9[q : q + 1, :] = w_ref[tap : tap + 1, 768 * stream : 768 * (stream + 1)]
    for i in range(6):
        wt[128 * i : 128 * (i + 1), :] = w9[:, 128 * i : 128 * (i + 1)].T
    columns = wt[own_rows, :]
    for q in range(9):
        wb[q] = jnp.broadcast_to(columns[:, q : q + 1], (DL, 128))
    for load in loads:
        load.wait()

    lane = lax.broadcasted_iota(jnp.int32, (DL, 128), 1)

    def planes_in(recv, dst, base):
        def body(rows):
            planes = [recv[i, rows, :].astype(F32) for i in range(NP)]
            planes = swap_bits(planes, LOW4)
            for i in range(NP):
                dst[base + i, rows, :] = planes[i]

        over_groups(body)

    def tiles_out(src, dst, table):
        def body(rows):
            flat = src[:, rows, :].reshape(NP * GR, 128)
            out = jnp.dot(flat, first_ref[...], preferred_element_type=F32).reshape(NP, GR, 128)
            tiles = swap_bits([out[i] for i in range(NP)], LOW4)
            for i in range(NP):
                turned = tiles[i] * tf[0, i : i + 1, :] + pltpu.roll(tiles[i], 64, 1) * tf[1, i : i + 1, :]
                dst[i, rows, :] = turned.astype(BF16)

        over_groups(body)

    arrived(XR)
    x3 = xrecv.reshape(NP, DL, 128)
    planes_in(x3, xp, 2)
    hx_send[0] = xp[16].astype(BF16)
    hx_send[1] = xp[17].astype(BF16)
    remote(hx_send, hx_recv, HX, {"col": lax.rem(col + 1, NP)}).start()
    under_way(HX, hx_send, hx_recv)

    def streams(first, last):
        def body(rows):
            taps = [wb[q, rows, :] for q in range(9)]
            behind2, behind1 = xp[first, rows, :], xp[first + 1, rows, :]
            for i in range(first, last):
                now = xp[i + 2, rows, :]
                z = [taps[j] * now + taps[3 + j] * behind1 + taps[6 + j] * behind2 for j in range(3)]
                ap[i, rows, :] = z[0]
                bp[i, rows, :] = z[1]
                sp[i, rows, :] = z[2]
                fld[i, rows, :] = (z[0] * z[1]).astype(BF16)
                behind2, behind1 = behind1, now

        return body

    over_groups(streams(2, NP))
    arrived(HX)
    for i in range(2):
        halo = hx_recv[i].astype(F32)
        back = jnp.where(lane >= 16, pltpu.roll(halo, 16, 1), pltpu.roll(halo, 17, 1))
        back = jnp.where(lane == 0, 0.0, back)
        xp[i] = jnp.where(col == 0, back, halo)

    over_groups(streams(0, 2))
    tiles_out(fld, s_send, tf)
    exchange("col", col, SS, lambda p: s_send.at[p], s_recv.at[col])
    under_way(SS, s_send.at[pl.ds(0, 15)], s_recv.at[pl.ds(0, 15)])
    s_recv[col] = s_send[col]

    arrived(CR)
    planes_in(crecv.reshape(NP, DL, 128), cp, 0)

    def gate_grad(rows):
        for i in range(NP):
            fld[i, rows, :] = (cp[i, rows, :] * sp[i, rows, :]).astype(BF16)

    over_groups(gate_grad)
    tiles_out(fld, g_send, tf)
    exchange("col", col, GG, lambda p: g_send.at[p], g_recv.at[col])
    under_way(GG, g_send.at[pl.ds(0, 15)], g_recv.at[pl.ds(0, 15)])
    g_recv[col] = g_send[col]

    arrived(FM)
    at_row = lax.broadcasted_iota(jnp.int32, (N2, N2), 0)
    at_col = lax.broadcasted_iota(jnp.int32, (N2, N2), 1)
    reverse = jnp.where(at_row + at_col == N2 - 1, 1.0, 0.0).astype(BF16)
    rev[...] = jnp.dot(
        fm[...].reshape(8 * DL, N2), reverse, preferred_element_type=F32
    ).reshape(2, 4, DL, N2)

    def mirror_at(slot):
        return jnp.where(low_half, (4 - slot) % 4, 3 - slot)

    own_at = jnp.where(low_half, 0, 1)
    for slot in range(4):
        rev_re = rev[0, mirror_at(slot)]
        rev_im = -rev[1, mirror_at(slot)]
        if slot == 0:
            fh[0, 4] = rev_re
            fh[1, 4] = rev_im
            rev_re = jnp.where(col == 0, 0.0, rev_re)
            rev_im = jnp.where(col == 0, 0.0, rev_im)
        fh[0, slot] = fo[0, own_at + slot].astype(F32) + rev_re
        fh[1, slot] = fo[1, own_at + slot].astype(F32) + rev_im

    parts = [(0, 4), (1, 5), (2, 6), (3, 7), (8, 9)]

    def spectrum(recv):
        def body(rows):
            planes = swap_bits([recv[i, rows, :].astype(F32) for i in range(NP)], HIGH3)
            for i in range(NP):
                half = i // 8
                pp[i % 8, rows, 128 * half : 128 * (half + 1)] = planes[i].astype(BF16)

        over_groups(body)
        middle = pp[4].astype(F32)
        pp[8] = (middle * ti[0, 4:5, :]).astype(BF16)
        pp[9] = (-middle * ti[1, 4:5, :]).astype(BF16)
        pp[4] = jnp.where(col == 0, 0.0, middle).astype(BF16)

    def products(slot):
        re, im = parts[slot]
        both = jnp.concatenate([pp[re], pp[im]], 0)
        out = jnp.dot(both, second_ref[...], preferred_element_type=F32)
        return out[:DL, :N2], out[:DL, N2:], out[DL:, :N2], out[DL:, N2:]

    def value(slot):
        re_cos, re_sin, im_cos, im_sin = products(slot)
        return re_cos + im_sin, im_cos - re_sin

    def turned_back(slot):
        re_cos, re_sin, im_cos, im_sin = products(slot)
        return re_cos - im_sin, im_cos + re_sin

    def restore(dst):
        for slot in range(4):
            z_re, z_im = turned_back(slot)
            cos, sin = ti[0, slot : slot + 1, :], ti[1, slot : slot + 1, :]
            qq[slot] = z_re * cos - z_im * sin
            q_im = z_im * cos + z_re * sin
            if slot == 0:
                z_re4, z_im4 = turned_back(4)
                q_im = jnp.where(col == 0, z_re4 * ti[0, 4:5, :] - z_im4 * ti[1, 4:5, :], q_im)
            qq[4 + slot] = q_im

        def body(rows):
            planes = [
                qq[i % 8, rows, 128 * (i // 8) : 128 * (i // 8 + 1)] for i in range(NP)
            ]
            planes = swap_bits(planes, HIGH3)
            for i in range(NP):
                dst[i, rows, :] = planes[i].astype(BF16)

        over_groups(body)

    arrived(SS)
    spectrum(s_recv)
    for slot in range(5):
        re, im = parts[slot]
        s_re, s_im = value(slot)
        sr[slot] = s_re
        si[slot] = s_im
        f_re, f_im = fh[0, slot], fh[1, slot]
        pp[re] = (s_re * f_re - s_im * f_im).astype(BF16)
        pp[im] = (s_re * f_im + s_im * f_re).astype(BF16)
    restore(y_send)
    exchange("col", col, YY, lambda p: y_send.at[p], y_recv.at[col])
    under_way(YY, y_send.at[pl.ds(0, 15)], y_recv.at[pl.ds(0, 15)])
    y_recv[col] = y_send[col]

    arrived(GG)
    spectrum(g_recv)
    for slot in range(5):
        re, im = parts[slot]
        g_re, g_im = value(slot)
        f_re, f_im = fh[0, slot], fh[1, slot]
        pp[re] = (g_re * f_re + g_im * f_im).astype(BF16)
        pp[im] = (g_im * f_re - g_re * f_im).astype(BF16)
        s_re, s_im = sr[slot], si[slot]
        grad_re = (s_re * g_re + s_im * g_im) * (1.0 / SEQ)
        grad_im = (s_re * g_im - s_im * g_re) * (1.0 / SEQ)
        if slot < 4:
            fgr_ref[own_at + slot] = grad_re
            fgi_ref[own_at + slot] = grad_im
            gs_send[0, mirror_at(slot)] = grad_re.astype(BF16)
            gs_send[1, mirror_at(slot)] = grad_im.astype(BF16)
        else:
            gs_send[0, 0] = jnp.where(col == 0, grad_re, gs_send[0, 0].astype(F32)).astype(BF16)
            gs_send[1, 0] = jnp.where(col == 0, grad_im, gs_send[1, 0].astype(F32)).astype(BF16)
    restore(z_send)
    exchange("col", col, ZZ, lambda p: z_send.at[p], z_recv.at[col])
    under_way(ZZ, z_send.at[pl.ds(0, 15)], z_recv.at[pl.ds(0, 15)])
    z_recv[col] = z_send[col]
    def send_mirrored():
        back_to = jnp.where(low_half, jnp.where(col == 0, 8, 16 - col), partner)
        back_to = lax.rem(back_to, NP)
        for part in range(2):
            remote(gs_send.at[part, pl.ds(1, 3)], gm_recv.at[part, pl.ds(1, 3)], GM, {"col": partner}).start()
            remote(gs_send.at[part, 0], gm_recv.at[part, 0], GM, {"col": back_to}).start()
        under_way(GM, gs_send, gm_recv)

    def field_back(recv, dst):
        def body(rows):
            planes = swap_bits([recv[i, rows, :].astype(F32) for i in range(NP)], LOW4)
            flat = jnp.stack([p.astype(BF16) for p in planes]).reshape(NP * GR, 128)
            out = jnp.dot(flat, last_ref[...], preferred_element_type=F32)
            dst[:, rows, :] = out.astype(BF16).astype(F32).reshape(NP, GR, 128)

        over_groups(body)

    def send_home(make, dst):
        def body(rows):
            tiles = swap_bits([make(i, rows) for i in range(NP)], LOW4)
            for i in range(NP):
                dst[i, rows, :] = tiles[i].astype(BF16)

        over_groups(body)

    arrived(YY)
    field_back(y_recv, yp)
    send_home(lambda i, rows: sp[i, rows, :] * yp[i, rows, :], m_send)
    exchange("row", row, MR, lambda p: m_send.at[p], tile_of(m_recv, row))
    under_way(MR, m_send.at[pl.ds(0, 15)], m_recv.at[pl.ds(0, 15 * DL)])
    m_recv[own_rows, :] = m_send[row]

    def rounded(value):
        return value.astype(BF16).astype(F32)

    def third_grads(rows):
        taps = [wb[3 * t + 2, rows, :] for t in range(3)]
        sums = [jnp.zeros((GR, 128), F32)] * 3
        before1 = before2 = None
        for i in range(NP):
            grad = rounded(cp[i, rows, :] * yp[i, rows, :])
            at_tap = [taps[t] * grad for t in range(3)]
            sums = [sums[t] + xp[i + 2 - t, rows, :] * grad for t in range(3)]
            if i == 0:
                edge[0, rows, :] = at_tap[2]
                first_one = at_tap[1]
            if i == 1:
                edge[1, rows, :] = first_one + at_tap[2]
            if before2 is not None:
                third[i - 2, rows, :] = before2 + at_tap[2]
            before2 = None if before1 is None else before1 + at_tap[1]
            before1 = at_tap[0]
        third[14, rows, :] = before2
        third[15, rows, :] = before1
        for t in range(3):
            late[t, rows, :] = sums[t]

    over_groups(third_grads)

    arrived(ZZ)
    field_back(z_recv, gp)

    def tap_grads(i, rows):
        gs = gp[i, rows, :]
        grads = (rounded(gs * bp[i, rows, :]), rounded(gs * ap[i, rows, :]))
        return grads, [
            wb[3 * t, rows, :] * grads[0] + wb[3 * t + 1, rows, :] * grads[1] for t in range(3)
        ]

    def edge_grads(rows):
        _, first_taps = tap_grads(0, rows)
        _, next_taps = tap_grads(1, rows)
        hg_send[0, rows, :] = (edge[0, rows, :] + first_taps[2]).astype(BF16)
        hg_send[1, rows, :] = (edge[1, rows, :] + first_taps[1] + next_taps[2]).astype(BF16)

    over_groups(edge_grads)
    remote(hg_send, hg_recv, HG, {"col": lax.rem(col + NP - 1, NP)}).start()
    under_way(HG, hg_send, hg_recv)

    def stream_grads(rows):
        sums = [jnp.zeros((GR, 128), F32)] * 6
        before1 = before2 = None
        for i in range(NP):
            grads, at_tap = tap_grads(i, rows)
            past = [xp[i + 2 - t, rows, :] for t in range(3)]
            sums = [sums[q] + past[q // 2] * grads[q % 2] for q in range(6)]
            if before2 is not None:
                gp[i - 2, rows, :] = third[i - 2, rows, :] + before2 + at_tap[2]
            before2 = None if before1 is None else before1 + at_tap[1]
            before1 = at_tap[0]
        gp[14, rows, :] = third[14, rows, :] + before2
        gp[15, rows, :] = third[15, rows, :] + before1
        at = lax.broadcasted_iota(jnp.int32, (GR, 128), 1)
        total = jnp.zeros((GR, 128), F32)
        for q in range(9):
            tap, stream = divmod(q, 3)
            value = late[tap, rows, :] if stream == 2 else sums[2 * tap + stream]
            total = jnp.where(at == q, jnp.sum(value, axis=1, keepdims=True), total)
        wt[rows, :] = total[:, :16]

    over_groups(stream_grads)
    d1_send[...] = jnp.zeros_like(d1_send)
    terms = wt[:DL, :].T * (1.0 / math.sqrt(SEQ))
    d1_send[:, :DL] = terms[:8]
    d1_send[0:1, 64 : 64 + DL] = terms[8:9]
    exchange("col", col, D1, lambda p: d1_send, d1_recv.at[col])
    under_way(D1, d1_recv.at[pl.ds(0, 15)], d1_recv.at[pl.ds(0, 15)])
    d1_recv[col] = d1_send[...]
    send_mirrored()

    arrived(HG)
    for i in range(2):
        halo = hg_recv[i].astype(F32)
        ahead = jnp.where(lane < 112, pltpu.roll(halo, 112, 1), pltpu.roll(halo, 111, 1))
        ahead = jnp.where(lane == 127, 0.0, ahead)
        gp[14 + i] = gp[14 + i] + jnp.where(col == NP - 1, ahead, halo)
    send_home(lambda i, rows: gp[i, rows, :], i_send)
    exchange("row", row, IR, lambda p: i_send.at[p], tile_of(i_recv, row))
    under_way(IR, i_send.at[pl.ds(0, 15)], i_recv.at[pl.ds(0, 15 * DL)])
    store(i_send.at[row], i_recv.at[own_rows])

    arrived(D1)
    total = d1_recv[0]
    for i in range(1, NP):
        total = total + d1_recv[i]
    d2_send[...] = total
    exchange("row", row, D2, lambda p: d2_send, d2_recv.at[row])
    under_way(D2, d1_recv.at[pl.ds(0, 15)], d2_recv.at[pl.ds(0, 15)])
    store(d2_send, d2_recv.at[row])

    arrived(MR)
    home(m_recv, mixed_ref)
    store(mixed_ref, mixed_hbm)

    arrived(GM)
    rev[...] = jnp.dot(
        gm_recv[...].reshape(8 * DL, N2), reverse, preferred_element_type=F32
    ).reshape(2, 4, DL, N2)
    fgr_ref[extra_row] = rev[0, 0]
    fgi_ref[extra_row] = -rev[1, 0]
    for i in range(1, 4):
        fgr_ref[4 + i] = rev[0, i]
        fgi_ref[4 + i] = -rev[1, i]

    store(fgr_ref, fgr_hbm)
    store(fgi_ref, fgi_hbm)

    arrived(D2)
    arrived(IR)
    for copy in stores:
        copy.wait()

    drain()


def finish(*refs):
    sources, results, (mixed, tiles, grad_re, grad_im, d2_recv, ig_ref, dw_ref) = (
        refs[:5], refs[5:10], refs[10:17],
    )
    load_sem, store_sem = refs[17:]
    held = (mixed, tiles, grad_re, grad_im, d2_recv)
    ready = (mixed, ig_ref, grad_re, grad_im, dw_ref)
    loads = [pltpu.make_async_copy(sources[i], held[i], load_sem.at[i]) for i in range(5)]
    stores = [pltpu.make_async_copy(ready[i], results[i], store_sem.at[i]) for i in range(5)]
    for i in (1, 4, 2, 3, 0):
        loads[i].start()
    loads[1].wait()
    home(tiles, ig_ref)
    stores[1].start()
    for i in (2, 3, 0):
        loads[i].wait()
        stores[i].start()
    loads[4].wait()
    spot = lax.broadcasted_iota(jnp.int32, (16, 128), 1)
    blocks = [jnp.zeros((16, 128), F32)] * 6
    for i in range(NP):
        block, off = divmod(DL * i, 128)
        packed = d2_recv[i]
        piece = jnp.concatenate([packed, pltpu.roll(packed, 64, 1)], 0)
        piece = jnp.where(spot < DL, piece, 0.0)
        piece = pltpu.roll(piece, off, 1) if off else piece
        if off + DL > 128:
            blocks[block] = blocks[block] + jnp.where(spot >= off, piece, 0.0)
            blocks[block + 1] = blocks[block + 1] + jnp.where(spot < off, piece, 0.0)
        else:
            blocks[block] = blocks[block] + piece
    for tap in range(3):
        for stream in range(3):
            q = 3 * tap + stream
            for i in range(6):
                at = 768 * stream + 128 * i
                dw_ref[tap : tap + 1, at : at + 128] = blocks[i][q : q + 1, :]
    stores[4].start()
    for copy in stores:
        copy.wait()


def per_device(sequence, conv_weights, cotangent, filter_re, filter_im):
    first, last, second, fwd, inv = (jnp.asarray(t) for t in tables())
    vmem = pl.BlockSpec(memory_space=pltpu.VMEM)
    hbm = pl.BlockSpec(memory_space=pl.ANY)
    tiles = pltpu.VMEM((NP, DL, 128), BF16)
    planes = pltpu.VMEM((NP, DL, 128), F32)
    flat = pltpu.VMEM((NP * DL, 128), BF16)
    spec = pltpu.VMEM((2, 4, DL, N2), BF16)
    pair = pltpu.VMEM((2, DL, 128), BF16)
    small = pltpu.VMEM((NP, 8, 128), F32)
    one = pltpu.VMEM((8, 128), F32)
    shapes = (
        jax.ShapeDtypeStruct(sequence.shape, BF16),
        jax.ShapeDtypeStruct(sequence.shape, BF16),
        jax.ShapeDtypeStruct(filter_re.shape, F32),
        jax.ShapeDtypeStruct(filter_re.shape, F32),
        jax.ShapeDtypeStruct(conv_weights.shape, F32),
    )
    mixed, grads, filter_re_grad, filter_im_grad, weights = shapes
    between = (
        mixed,
        jax.ShapeDtypeStruct((NP * DL, 128), BF16),
        filter_re_grad,
        filter_im_grad,
        jax.ShapeDtypeStruct((NP, 8, 128), F32),
    )
    outs = pl.pallas_call(
        kernel,
        out_shape=between,
        in_specs=[hbm] * 10,
        out_specs=[hbm] * 5,
        scratch_shapes=[
            *(pltpu.VMEM(s.shape, s.dtype) for s in (mixed, filter_re_grad, filter_im_grad)),
            pltpu.VMEM(sequence.shape, BF16),
            pltpu.VMEM(conv_weights.shape, F32),
            pltpu.VMEM(sequence.shape, BF16),
            pltpu.VMEM((128, 128), BF16),
            pltpu.VMEM((128, 128), BF16),
            pltpu.VMEM((N2, 2 * N2), BF16),
            flat, flat, flat, flat,
            pltpu.VMEM((16, 768), F32),
            pltpu.VMEM((768, 16), F32),
            pltpu.VMEM((9, DL, 128), F32),
            pltpu.VMEM((2, 8, DL, N2), BF16),
            spec,
            pltpu.VMEM((2, 4, DL, N2), F32),
            pltpu.VMEM((2, 5, DL, N2), F32),
            pltpu.VMEM((2, 16, 128), F32),
            pltpu.VMEM((2, 8, N2), F32),
            pltpu.VMEM((NP + 2, DL, 128), F32),
            pair, pair,
            planes, planes, planes, planes, planes,
            tiles,
            tiles, tiles, tiles, tiles, tiles, tiles, tiles, tiles,
            pltpu.VMEM((10, DL, N2), BF16),
            pltpu.VMEM((5, DL, N2), F32),
            pltpu.VMEM((5, DL, N2), F32),
            pltpu.VMEM((8, DL, N2), F32),
            spec, spec,
            planes, planes,
            pltpu.VMEM((2, DL, 128), F32),
            pltpu.VMEM((3, DL, 128), F32),
            pair, pair,
            one, small, one,
            tiles, flat, tiles,
            pltpu.SemaphoreType.DMA((14,)),
            pltpu.SemaphoreType.DMA((14,)),
            pltpu.SemaphoreType.DMA((15,)),
        ],
        compiler_params=pltpu.CompilerParams(
            collective_id=0, has_side_effects=True, vmem_limit_bytes=56 * 1024 * 1024
        ),
    )(
        sequence, conv_weights, cotangent, filter_re, filter_im,
        first, last, second, fwd, inv,
    )
    return pl.pallas_call(
        finish,
        out_shape=shapes,
        in_specs=[hbm] * 5,
        out_specs=[hbm] * 5,
        scratch_shapes=[
            *(pltpu.VMEM(s.shape, s.dtype) for s in between + (grads, weights)),
            pltpu.SemaphoreType.DMA((5,)),
            pltpu.SemaphoreType.DMA((5,)),
        ],
    )(*outs)


def solution(mesh):
    return jax.shard_map(
        per_device,
        mesh=mesh,
        in_specs=(
            P("row", "col", None),
            P(),
            P("row", "col", None),
            P("col", "row", None),
            P("col", "row", None),
        ),
        out_specs=(
            P("row", "col", None),
            P("row", "col", None),
            P("col", "row", None),
            P("col", "row", None),
            P(),
        ),
        check_vma=False,
    )
```
